32 devices in a mesh: row: 8 (over z, y), col: 4 (over x, core).
Axes of the slice: x: 2, y: 2, z: 4, core: 2. Of those that a mesh axis runs over, the one named last changes fastest.
Arguments:
- block_tiles: bfloat16 [8, 4, 128, 128, 128], P('row', 'col'), may hold values from -0.5 to 0.5
- tile_row: int32 [8, 4, 128], P('row', 'col'), may hold values from 0 to 495
- tile_col: int32 [8, 4, 128], P('row', 'col'), may hold values from 0 to 3903
- primal: float32 [1998848], P(('col', 'row')), may hold values from -6 to 6
- duals: float32 [507904], P('row'), may hold values from -6 to 6
- cost_vec: float32 [1998848], P(('col', 'row')), may hold values from -6 to 6
- lower_bound: float32 [1998848], P(('col', 'row')), may hold values from -1.5 to -0.25
- upper_bound: float32 [1998848], P(('col', 'row')), may hold values from 0.25 to 1.5
- bound_kind: int32 [1998848], P(('col', 'row')), may hold values from 0 to 3
- right_side: float32 [507904], P('row'), may hold values from -6 to 6
- row_kind: int32 [507904], P('row'), may hold values from 0 to 1
- step_sizes: float32 [2], replicated, may hold values from 0.3 to 1
Outputs:
- primal_next: float32 [1998848], P(('col', 'row'))
- dual_next: float32 [507904], P('row')
The draws below stay inside these ranges and needn't reach their ends.
Inputs may be any that keep to these rules, and one draw needn't show every extreme that they name: `tile_row`: index of a tile row inside the device's own row range. `tile_col`: index of a tile column inside the device's own column range.
All inputs are finite; a program needn't handle non-finite values.
Results may differ from the reference program's by a relative error of at most 0.0031.
Values may be sent and summed in bfloat16 or wider, within the bound.
No kernel may reach another device: no remote copies, remote signals or barrier semaphores. Data moves between devices by JAX's collectives and lax.ppermute only.
A program may use at most 64 MiB of HBM per device.

```python
import math
import jax
import jax.numpy as jnp
from jax import lax

TILE = 128
RBLK = 496
CBLK = 3904
K_TILES = 128
M = 507904
N = 1998848
N_ROW = 8
N_COL = 4


def with_ends(values, stream_key, least, largest):
    index_at = [jax.random.randint(jax.random.fold_in(stream_key, axis), (), 0, length) for axis, length in enumerate(values.shape)]
    widest = values.shape.index(max(values.shape))
    next_to = index_at[:widest] + [(index_at[widest] + 1) % values.shape[widest]] + index_at[widest + 1:]
    return values.at[tuple(index_at)].set(least).at[tuple(next_to)].set(largest)


def level_of(own_key, extent, split, smallest, largest):
    level = 1.0
    for position, shards_of in split:
        steps = jax.random.uniform(jax.random.fold_in(jax.random.fold_in(own_key, 6), position), (shards_of,), jnp.float32, smallest / len(split), largest / len(split))
        level = level * jnp.repeat(jnp.exp(steps), extent[position] // shards_of).reshape((-1,) + (1,) * (len(extent) - 1 - position))
    return level


def bell_draw(key, shape, width, most, split=(), held_as=jnp.bfloat16):
    level = level_of(key, shape, split, -0.22, 0.18) if split else 1.0
    result = jax.random.normal(key, shape, jnp.float32) * width * level
    return jnp.minimum(jnp.maximum(result, -most), most).astype(held_as)


def setup_inputs(seed: int = 0) -> dict:
    streams_of = jax.random.split(jax.random.key(seed), 13)
    block_tiles = bell_draw(streams_of[0], (N_ROW, N_COL, K_TILES, TILE, TILE), (128 * K_TILES * N_COL // RBLK) ** -0.5, 0.5, ((0, 8), (1, 4)))
    tile_row = with_ends(jax.random.randint(streams_of[1], (N_ROW, N_COL, K_TILES), 0, RBLK), jax.random.fold_in(streams_of[1], 1), 0, RBLK - 1).astype(jnp.int32)
    tile_col = with_ends(jax.random.randint(streams_of[2], (N_ROW, N_COL, K_TILES), 0, CBLK), jax.random.fold_in(streams_of[2], 1), 0, CBLK - 1).astype(jnp.int32)
    primal = bell_draw(streams_of[3], (N,), 1.0, 6.0, ((0, 32),), jnp.float32)
    duals = bell_draw(streams_of[4], (M,), 1.0, 6.0, ((0, 8),), jnp.float32)
    cost_vec = bell_draw(streams_of[5], (N,), 1.0, 6.0, ((0, 32),), jnp.float32)
    lower_bound = jnp.clip(-1.5 + 1.25 * jax.random.uniform(streams_of[6], (N,), jnp.float32) ** level_of(streams_of[6], (N,), ((0, 32),), -0.2, 0.2), -1.5, -0.25)
    upper_bound = jnp.clip(0.25 + 1.25 * jax.random.uniform(streams_of[7], (N,), jnp.float32) ** level_of(streams_of[7], (N,), ((0, 32),), -0.2, 0.2), 0.25, 1.5)
    bound_kind = with_ends(jax.random.randint(streams_of[8], (N,), 0, 4), jax.random.fold_in(streams_of[8], 1), 0, 3).astype(jnp.int32)
    right_side = bell_draw(streams_of[9], (M,), 1.0, 6.0, ((0, 8),), jnp.float32)
    row_kind = with_ends(jax.random.randint(streams_of[10], (M,), 0, 2), jax.random.fold_in(streams_of[10], 1), 0, 1).astype(jnp.int32)
    step_sizes = jnp.clip(jnp.exp(jax.random.uniform(streams_of[11], (2,), jnp.float32, math.log(0.3), math.log(1.0))), 0.3, 1.0)
    return dict(block_tiles=block_tiles, tile_row=tile_row, tile_col=tile_col, primal=primal, duals=duals, cost_vec=cost_vec, lower_bound=lower_bound, upper_bound=upper_bound, bound_kind=bound_kind, right_side=right_side, row_kind=row_kind, step_sizes=step_sizes)


def project(values, lower_bound, upper_bound, bound_kind):
    with_lower = (bound_kind % 2) == 1
    with_upper = bound_kind >= 2
    values = jnp.where(with_lower, jnp.maximum(values, lower_bound), values)
    return jnp.where(with_upper, jnp.minimum(values, upper_bound), values)


def reference(block_tiles, tile_row, tile_col, primal, duals, cost_vec, lower_bound, upper_bound, bound_kind, right_side, row_kind, step_sizes):
    n_cells = N_ROW * N_COL
    flat_tiles = block_tiles.reshape(n_cells, K_TILES, TILE, TILE)
    flat_rows = tile_row.reshape(n_cells, K_TILES).astype(jnp.int32)
    flat_cols = tile_col.reshape(n_cells, K_TILES).astype(jnp.int32)
    device_ids = jnp.arange(n_cells, dtype=jnp.int32)
    dual_blocks = lax.optimization_barrier(duals.astype(jnp.bfloat16)).astype(jnp.float32).reshape(N_ROW, RBLK, TILE)

    def add_transpose(running, pieces):
        tiles_here, rows_here, cols_here, device_id = pieces
        grid_row = device_id // N_COL
        grid_col = device_id % N_COL
        blocks = dual_blocks[grid_row][rows_here]
        products = jnp.einsum('kij,ki->kj', tiles_here.astype(jnp.float32), blocks)
        segment_term = jax.ops.segment_sum(products, cols_here, num_segments=CBLK)
        return running.at[grid_col].add(segment_term), None

    zeros_cols = jnp.zeros((N_COL, CBLK, TILE), jnp.float32)
    col_sums, _ = lax.scan(add_transpose, zeros_cols, (flat_tiles, flat_rows, flat_cols, device_ids))
    stepped = primal - step_sizes[0] * (cost_vec - col_sums.reshape(-1))
    primal_next = project(stepped, lower_bound, upper_bound, bound_kind)
    extrap = lax.optimization_barrier((2.0 * primal_next - primal).astype(jnp.bfloat16)).astype(jnp.float32).reshape(N_COL, CBLK, TILE)

    def add_forward(running, pieces):
        tiles_here, rows_here, cols_here, device_id = pieces
        grid_row = device_id // N_COL
        grid_col = device_id % N_COL
        blocks = extrap[grid_col][cols_here]
        products = jnp.einsum('kij,kj->ki', tiles_here.astype(jnp.float32), blocks)
        segment_term = jax.ops.segment_sum(products, rows_here, num_segments=RBLK)
        return running.at[grid_row].add(segment_term), None

    zeros_rows = jnp.zeros((N_ROW, RBLK, TILE), jnp.float32)
    row_sums, _ = lax.scan(add_forward, zeros_rows, (flat_tiles, flat_rows, flat_cols, device_ids))
    updated = duals + step_sizes[1] * (right_side - row_sums.reshape(-1))
    dual_next = jnp.where(row_kind == 1, jnp.maximum(updated, 0.0), updated)
    return primal_next, dual_next
```

```python
import jax
import jax.numpy as jnp
from jax import lax
from jax.experimental import pallas as pl
from jax.experimental.pallas import tpu as pltpu
from jax.sharding import PartitionSpec as P

TILE = 128
GROUP = 16
SPARE = 8

f32 = jnp.float32
bf16 = jnp.bfloat16
VMEM = pl.BlockSpec(memory_space=pltpu.VMEM)
SMEM = pl.BlockSpec(memory_space=pltpu.SMEM)
HBM = pl.BlockSpec(memory_space=pl.ANY)


def tile_copies(tiles_hbm, tiles_vmem, sems):
    n_groups = tiles_vmem.shape[0] // GROUP
    return [
        pltpu.make_async_copy(
            tiles_hbm.at[pl.ds(g * GROUP, GROUP)],
            tiles_vmem.at[pl.ds(g * GROUP, GROUP)],
            sems.at[g],
        )
        for g in range(n_groups)
    ]


def one_row_of(block, position):
    rows = lax.broadcasted_iota(jnp.int32, block.shape, 0)
    return jnp.where(rows == position, block, 0.0).astype(bf16)


def halves(values):
    high = values.astype(bf16)
    low = (values - high.astype(f32)).astype(bf16)
    return jnp.concatenate([high, low], axis=-1)


def transpose_product_kernel(rows_ref, cols_ref, duals_ref, tiles_hbm, out_ref, tiles_vmem, picked, sems):
    copies = tile_copies(tiles_hbm, tiles_vmem, sems)
    for copy in copies:
        copy.start()
    k_tiles = tiles_vmem.shape[0]
    for k in range(k_tiles):
        picked[pl.ds(k, 1), :] = duals_ref[pl.ds(rows_ref[k], 1), :]
    out_ref[pl.ds(k_tiles, SPARE), :] = jnp.broadcast_to(cols_ref[...].astype(f32), (SPARE, TILE))
    for g, copy in enumerate(copies):
        here = pl.ds(g * GROUP, GROUP)
        block = picked[here, :].astype(bf16).astype(f32)
        left = jnp.concatenate([one_row_of(block, m) for m in range(GROUP)], axis=1)
        copy.wait()
        out_ref[here, :] = jnp.dot(
            left, tiles_vmem[here].reshape(GROUP * TILE, TILE), preferred_element_type=f32
        )


def primal_kernel(
    terms_ref, primal_ref, cost_ref, lower_ref, upper_ref, kind_ref, steps_ref, next_ref, wanted_ref, extrap
):
    sources, rows_each, _ = terms_ref.shape
    k_tiles = rows_each - SPARE
    blocks = primal_ref.shape[0]
    padded = extrap.shape[0]
    first = lax.axis_index("row") * blocks
    block_down = lax.broadcasted_iota(jnp.int32, (blocks, k_tiles), 0)
    masks, terms = [], []
    for s in range(sources):
        places = terms_ref[s, pl.ds(k_tiles, 1), :].astype(jnp.int32) - first
        masks.append(jnp.where(block_down == places, 1.0, 0.0).astype(bf16))
        terms.append(halves(terms_ref[s, pl.ds(0, k_tiles), :]))
    both = jnp.dot(
        jnp.concatenate(masks, axis=1), jnp.concatenate(terms, axis=0), preferred_element_type=f32
    )
    col_sums = both[:, :TILE] + both[:, TILE:]
    primal = primal_ref[...]
    kind = kind_ref[...]
    moved = primal - steps_ref[0] * (cost_ref[...] - col_sums)
    moved = jnp.where(kind % 2 == 1, jnp.maximum(moved, lower_ref[...]), moved)
    moved = jnp.where(kind >= 2, jnp.minimum(moved, upper_ref[...]), moved)
    next_ref[...] = moved
    if padded > blocks:
        extrap[pl.ds(padded - 32, 32), :] = jnp.zeros((32, TILE), f32)
    extrap[pl.ds(0, blocks), :] = 2.0 * moved - primal
    right = extrap[...].astype(bf16)
    block_across = lax.broadcasted_iota(jnp.int32, (k_tiles, padded), 1)
    for s in range(sources):
        places = jnp.transpose(terms_ref[s, pl.ds(k_tiles, SPARE), :])[:, 0:1].astype(jnp.int32) - first
        places = jnp.where(places < blocks, places, -1)
        mask = jnp.where(block_across == places, 1.0, 0.0).astype(bf16)
        wanted_ref[s] = jnp.dot(mask, right, preferred_element_type=f32).astype(bf16)


def product_kernel(rows_ref, wanted_ref, tiles_hbm, out_ref, tiles_vmem, sems):
    copies = tile_copies(tiles_hbm, tiles_vmem, sems)
    for copy in copies:
        copy.start()
    k_tiles = tiles_vmem.shape[0]
    out_ref[pl.ds(k_tiles, SPARE), :] = jnp.broadcast_to(rows_ref[...].astype(f32), (SPARE, TILE))
    for g, copy in enumerate(copies):
        here = pl.ds(g * GROUP, GROUP)
        block = jnp.zeros((GROUP, TILE), f32)
        for s in range(wanted_ref.shape[0]):
            block += wanted_ref[s, here, :].astype(f32)
        copy.wait()
        total = jnp.zeros((GROUP, TILE), f32)
        for m in range(GROUP):
            total += lax.dot_general(
                one_row_of(block, m),
                tiles_vmem[g * GROUP + m],
                (((1,), (1,)), ((), ())),
                preferred_element_type=f32,
            )
        out_ref[here, :] = total


def dual_kernel(terms_ref, duals_ref, right_ref, kind_ref, steps_ref, next_ref):
    sources, rows_each, _ = terms_ref.shape
    k_tiles = rows_each - SPARE
    blocks = duals_ref.shape[0]
    block_down = lax.broadcasted_iota(jnp.int32, (blocks, k_tiles), 0)
    masks, terms = [], []
    for s in range(sources):
        places = terms_ref[s, pl.ds(k_tiles, 1), :].astype(jnp.int32)
        masks.append(jnp.where(block_down == places, 1.0, 0.0).astype(bf16))
        terms.append(halves(terms_ref[s, pl.ds(0, k_tiles), :]))
    both = jnp.dot(
        jnp.concatenate(masks, axis=1), jnp.concatenate(terms, axis=0), preferred_element_type=f32
    )
    row_sums = both[:, :TILE] + both[:, TILE:]
    updated = duals_ref[...] + steps_ref[1] * (right_ref[...] - row_sums)
    next_ref[...] = jnp.where(kind_ref[...] == 1, jnp.maximum(updated, 0.0), updated)


def local(
    block_tiles,
    tile_row,
    tile_col,
    primal,
    duals,
    cost_vec,
    lower_bound,
    upper_bound,
    bound_kind,
    right_side,
    row_kind,
    step_sizes,
):
    k_tiles = block_tiles.shape[2]
    tiles = block_tiles.reshape(k_tiles, TILE, TILE)
    n_row = lax.axis_size("row")
    col_blocks = primal.shape[0] // TILE
    row_blocks = duals.shape[0] // TILE
    padded = -(-col_blocks // TILE) * TILE
    n_groups = k_tiles // GROUP
    by_block = lambda array: array.reshape(-1, TILE)
    tiles_scratch = pltpu.VMEM((k_tiles, TILE, TILE), bf16)
    payload = jax.ShapeDtypeStruct((k_tiles + SPARE, TILE), f32)
    params = pltpu.CompilerParams(vmem_limit_bytes=32 * 1024 * 1024)

    col_terms = pl.pallas_call(
        transpose_product_kernel,
        out_shape=payload,
        in_specs=[SMEM, VMEM, VMEM, HBM],
        out_specs=VMEM,
        scratch_shapes=[tiles_scratch, pltpu.VMEM((k_tiles, TILE), f32), pltpu.SemaphoreType.DMA((n_groups,))],
        compiler_params=params,
        name="transpose_product",
    )(tile_row.reshape(-1), tile_col.reshape(1, k_tiles), by_block(duals), tiles)
    all_col_terms = lax.all_gather(col_terms, "row")
    primal_next, wanted = pl.pallas_call(
        primal_kernel,
        out_shape=(
            jax.ShapeDtypeStruct((col_blocks, TILE), f32),
            jax.ShapeDtypeStruct((n_row, k_tiles, TILE), bf16),
        ),
        in_specs=[VMEM] * 6 + [SMEM],
        out_specs=(VMEM, VMEM),
        scratch_shapes=[pltpu.VMEM((padded, TILE), f32)],
        compiler_params=params,
        name="primal_step",
    )(
        all_col_terms,
        by_block(primal),
        by_block(cost_vec),
        by_block(lower_bound),
        by_block(upper_bound),
        by_block(bound_kind),
        step_sizes,
    )
    arrived = lax.all_to_all(wanted, "row", 0, 0)
    row_terms = pl.pallas_call(
        product_kernel,
        out_shape=payload,
        in_specs=[VMEM, VMEM, HBM],
        out_specs=VMEM,
        scratch_shapes=[tiles_scratch, pltpu.SemaphoreType.DMA((n_groups,))],
        compiler_params=params,
        name="product",
    )(tile_row.reshape(1, k_tiles), arrived, tiles)
    all_row_terms = lax.all_gather(row_terms, "col")
    dual_next = pl.pallas_call(
        dual_kernel,
        out_shape=jax.ShapeDtypeStruct((row_blocks, TILE), f32),
        in_specs=[VMEM] * 4 + [SMEM],
        out_specs=VMEM,
        compiler_params=params,
        name="dual_step",
    )(all_row_terms, by_block(duals), by_block(right_side), by_block(row_kind), step_sizes)
    return (primal_next.reshape(-1), dual_next.reshape(-1))


def solution(mesh):
    return jax.shard_map(
        local,
        mesh=mesh,
        in_specs=(
            P("row", "col", None, None, None),
            P("row", "col", None),
            P("row", "col", None),
            P(("col", "row")),
            P("row"),
            P(("col", "row")),
            P(("col", "row")),
            P(("col", "row")),
            P(("col", "row")),
            P("row"),
            P("row"),
            P(),
        ),
        out_specs=(P(("col", "row")), P("row")),
        check_vma=False,
    )
```

```python
import jax
import jax.numpy as jnp
from jax import lax
from jax.experimental import pallas as pl
from jax.experimental.pallas import tpu as pltpu
from jax.sharding import PartitionSpec as P

TILE = 128
GROUP = 16
HEAD = 16
BITS = 14

f32 = jnp.float32
bf16 = jnp.bfloat16
i32 = jnp.int32
i16 = jnp.int16
VMEM = pl.BlockSpec(memory_space=pltpu.VMEM)
SMEM = pl.BlockSpec(memory_space=pltpu.SMEM)
HBM = pl.BlockSpec(memory_space=pltpu.HBM)


def iota(shape, axis):
    return lax.broadcasted_iota(i32, shape, axis)


def one_row_of(block, position):
    return jnp.where(iota(block.shape, 0) == position, block, 0.0).astype(bf16)


def coded(values):
    largest = jnp.maximum(jnp.max(jnp.abs(values), axis=1, keepdims=True), 1e-30)
    exponent = jnp.ceil(jnp.log2(largest))
    whole = jnp.floor(values * jnp.exp2(BITS - exponent) + 0.5)
    return whole.astype(i32).astype(i16), jnp.broadcast_to(exponent, values.shape)


def head_of(places, exponents):
    across = jnp.transpose(exponents)[0:HEAD, :].astype(i32)
    return jnp.where(iota((HEAD, TILE), 0) == 0, places, across).astype(i16)


def block_sums(payloads, first, blocks):
    down = iota((blocks, TILE), 0)
    masks, terms = [], []
    for payload in payloads:
        k_tiles = payload.shape[0] - HEAD
        head = payload[pl.ds(k_tiles, HEAD), :].astype(i32)
        scale = jnp.exp2(head[1:2, :].astype(f32) - BITS)
        masks.append(jnp.where(down == head[0:1, :] - first, scale, 0.0).astype(bf16))
        whole = payload[pl.ds(0, k_tiles), :].astype(i32)
        low = jnp.bitwise_and(whole, 255)
        parts = [(whole - low).astype(f32).astype(bf16), low.astype(f32).astype(bf16)]
        terms.append(jnp.concatenate(parts, axis=1))
    both = jnp.dot(
        jnp.concatenate(masks, axis=1), jnp.concatenate(terms, axis=0), preferred_element_type=f32
    )
    return both[:, :TILE] + both[:, TILE:]


def started(sources, targets, sems):
    copies = [
        pltpu.make_async_copy(source, target, sems.at[n])
        for n, (source, target) in enumerate(zip(sources, targets))
    ]
    for copy in copies:
        copy.start()
    return copies


def transpose_product_kernel(
    rows_hbm, cols_hbm, duals_hbm, tiles_hbm, out_ref, rows, cols, duals, tiles, picked, exponents, sems
):
    k_tiles = tiles.shape[0]
    n_groups = k_tiles // GROUP
    small = [
        pltpu.make_async_copy(source, target, sems.at[n_groups + n])
        for n, (source, target) in enumerate([(rows_hbm, rows), (duals_hbm, duals), (cols_hbm, cols)])
    ]
    large = [
        pltpu.make_async_copy(
            tiles_hbm.at[pl.ds(g * GROUP, GROUP)], tiles.at[pl.ds(g * GROUP, GROUP)], sems.at[g]
        )
        for g in range(n_groups)
    ]
    for copy in small + large:
        copy.start()
    for copy in small:
        copy.wait()
    for k in range(k_tiles):
        picked[pl.ds(k, 1), :] = duals[pl.ds(rows[k], 1), :]
    for g, copy in enumerate(large):
        here = pl.ds(g * GROUP, GROUP)
        block = picked[here, :].astype(bf16).astype(f32)
        left = jnp.concatenate([one_row_of(block, m) for m in range(GROUP)], axis=1)
        copy.wait()
        terms = jnp.dot(left, tiles[here].reshape(GROUP * TILE, TILE), preferred_element_type=f32)
        out_ref[here, :], exponents[here, :] = coded(terms)
    out_ref[pl.ds(k_tiles, HEAD), :] = head_of(cols[...], exponents[...])


def primal_kernel(n_row, *refs):
    payloads, refs = refs[:n_row], refs[n_row:]
    sources, (steps_ref, next_ref), refs = refs[:5], refs[5:7], refs[7:]
    wanted, (extrap, *local_refs, sems) = refs[:n_row], refs[n_row:]
    primal_ref, cost_ref, lower_ref, upper_ref, kind_ref = local_refs
    copies = started(sources, local_refs, sems)
    blocks = primal_ref.shape[0]
    padded = extrap.shape[0]
    first = lax.axis_index("row") * blocks
    col_sums = block_sums(payloads, first, blocks)
    for copy in copies:
        copy.wait()
    primal = primal_ref[...]
    kind = kind_ref[...]
    moved = primal - steps_ref[0] * (cost_ref[...] - col_sums)
    moved = jnp.where(kind % 2 == 1, jnp.maximum(moved, lower_ref[...]), moved)
    moved = jnp.where(kind >= 2, jnp.minimum(moved, upper_ref[...]), moved)
    next_ref[...] = moved
    whole = blocks // 8 * 8
    if padded > whole:
        extrap[pl.ds(whole, padded - whole), :] = jnp.zeros((padded - whole, TILE), f32)
    extrap[pl.ds(0, blocks), :] = 2.0 * moved - primal
    right = extrap[...].astype(bf16)
    for payload, target in zip(payloads, wanted):
        k_tiles = target.shape[0]
        head = payload[pl.ds(k_tiles, HEAD), :].astype(i32)
        places = jnp.transpose(head.astype(f32))[:, 0:1].astype(i32) - first
        mask = jnp.where(iota((k_tiles, padded), 1) == places, 1.0, 0.0)
        target[...] = jnp.dot(mask.astype(bf16), right, preferred_element_type=f32).astype(bf16)


def product_kernel(rows_ref, tiles_ref, *refs):
    arrived, out_ref = refs[:-1], refs[-1]
    k_tiles = tiles_ref.shape[0]
    block = arrived[0][...].astype(f32)
    for ref in arrived[1:]:
        block += ref[...].astype(f32)
    down = jnp.transpose(block)
    lane = iota((TILE, k_tiles), 1)
    right = jnp.concatenate(
        [jnp.where(lane % 2 == 0, down, 0.0), jnp.where(lane % 2 == 1, down, 0.0)], axis=0
    ).astype(bf16)
    terms = jnp.zeros((TILE, k_tiles), f32)
    for g in range(k_tiles // 8):
        even = jnp.concatenate([tiles_ref[8 * g + m] for m in (0, 2, 4, 6)], axis=0)
        odd = jnp.concatenate([tiles_ref[8 * g + m] for m in (1, 3, 5, 7)], axis=0)
        products = jnp.dot(jnp.concatenate([even, odd], axis=1), right, preferred_element_type=f32)
        for p in range(4):
            terms = jnp.where(lane // 2 == 4 * g + p, products[p * TILE : (p + 1) * TILE], terms)
    out_ref[pl.ds(0, k_tiles), :], exponents = coded(jnp.transpose(terms))
    out_ref[pl.ds(k_tiles, HEAD), :] = head_of(rows_ref[...], exponents)


def dual_kernel(n_col, *refs):
    payloads, sources, (steps_ref, next_ref) = refs[:n_col], refs[n_col : n_col + 3], refs[n_col + 3 : n_col + 5]
    *local_refs, sems = refs[n_col + 5 :]
    duals_ref, right_ref, kind_ref = local_refs
    copies = started(sources, local_refs, sems)
    row_sums = block_sums(payloads, 0, duals_ref.shape[0])
    for copy in copies:
        copy.wait()
    updated = duals_ref[...] + steps_ref[1] * (right_ref[...] - row_sums)
    next_ref[...] = jnp.where(kind_ref[...] == 1, jnp.maximum(updated, 0.0), updated)


def exchange(arrays, axis, back=False):
    size = lax.axis_size(axis)
    arrived = []
    for n, array in enumerate(arrays):
        if n == 0:
            arrived.append(array)
            continue
        if size & (size - 1) == 0:
            pairs = [(i, i ^ n) for i in range(size)]
        else:
            pairs = [(i, (i + (-n if back else n)) % size) for i in range(size)]
        arrived.append(lax.ppermute(array, axis, pairs))
    return arrived


def local(
    block_tiles,
    tile_row,
    tile_col,
    primal,
    duals,
    cost_vec,
    lower_bound,
    upper_bound,
    bound_kind,
    right_side,
    row_kind,
    step_sizes,
):
    k_tiles = block_tiles.shape[2]
    tiles = block_tiles.reshape(k_tiles, TILE, TILE)
    n_row = lax.axis_size("row")
    n_col = lax.axis_size("col")
    col_blocks = primal.shape[0] // TILE
    row_blocks = duals.shape[0] // TILE
    padded = -(-col_blocks // TILE) * TILE
    in_hbm = lambda array: pltpu.with_memory_space_constraint(array, pltpu.HBM)
    by_block = lambda array: in_hbm(array.reshape(-1, TILE))
    blocks_of = lambda blocks, kind: pltpu.VMEM((blocks, TILE), kind)
    payload = jax.ShapeDtypeStruct((k_tiles + HEAD, TILE), i16)
    block = jax.ShapeDtypeStruct((k_tiles, TILE), bf16)
    params = pltpu.CompilerParams(vmem_limit_bytes=32 * 1024 * 1024)

    col_terms = pl.pallas_call(
        transpose_product_kernel,
        out_shape=payload,
        in_specs=[HBM] * 4,
        out_specs=VMEM,
        scratch_shapes=[
            pltpu.SMEM((k_tiles,), i32),
            pltpu.VMEM((1, k_tiles), i32),
            pltpu.VMEM((row_blocks, TILE), f32),
            pltpu.VMEM((k_tiles, TILE, TILE), bf16),
            pltpu.VMEM((k_tiles, TILE), f32),
            pltpu.VMEM((k_tiles, TILE), f32),
            pltpu.SemaphoreType.DMA((k_tiles // GROUP + 3,)),
        ],
        compiler_params=params,
        name="transpose_product",
    )(in_hbm(tile_row.reshape(-1)), in_hbm(tile_col.reshape(1, k_tiles)), by_block(duals), in_hbm(tiles))
    primal_next, *wanted = pl.pallas_call(
        lambda *refs: primal_kernel(n_row, *refs),
        out_shape=(jax.ShapeDtypeStruct((col_blocks, TILE), f32), *[block] * n_row),
        in_specs=[VMEM] * n_row + [HBM] * 5 + [SMEM],
        out_specs=(VMEM,) * (n_row + 1),
        scratch_shapes=[
            blocks_of(padded, f32),
            *[blocks_of(col_blocks, f32)] * 4,
            blocks_of(col_blocks, i32),
            pltpu.SemaphoreType.DMA((5,)),
        ],
        compiler_params=params,
        name="primal_step",
    )(
        *exchange([col_terms] * n_row, "row"),
        by_block(primal),
        by_block(cost_vec),
        by_block(lower_bound),
        by_block(upper_bound),
        by_block(bound_kind),
        step_sizes,
    )
    row_terms = pl.pallas_call(
        product_kernel,
        out_shape=payload,
        in_specs=[VMEM] * (n_row + 2),
        out_specs=VMEM,
        compiler_params=params,
        name="product",
    )(tile_row.reshape(1, k_tiles), tiles, *exchange(wanted, "row", back=True))
    dual_next = pl.pallas_call(
        lambda *refs: dual_kernel(n_col, *refs),
        out_shape=jax.ShapeDtypeStruct((row_blocks, TILE), f32),
        in_specs=[VMEM] * n_col + [HBM] * 3 + [SMEM],
        out_specs=VMEM,
        scratch_shapes=[
            *[blocks_of(row_blocks, f32)] * 2,
            blocks_of(row_blocks, i32),
            pltpu.SemaphoreType.DMA((3,)),
        ],
        compiler_params=params,
        name="dual_step",
    )(*exchange([row_terms] * n_col, "col"), by_block(duals), by_block(right_side), by_block(row_kind), step_sizes)
    return (primal_next.reshape(-1), dual_next.reshape(-1))


def solution(mesh):
    return jax.shard_map(
        local,
        mesh=mesh,
        in_specs=(
            P("row", "col", None, None, None),
            P("row", "col", None),
            P("row", "col", None),
            P(("col", "row")),
            P("row"),
            P(("col", "row")),
            P(("col", "row")),
            P(("col", "row")),
            P(("col", "row")),
            P("row"),
            P("row"),
            P(),
        ),
        out_specs=(P(("col", "row")), P("row")),
        check_vma=False,
    )
```

```python
import jax
import jax.numpy as jnp
from jax import lax
from jax.experimental import pallas as pl
from jax.experimental.pallas import tpu as pltpu
from jax.sharding import PartitionSpec as P

TILE = 128
GROUP = 16
HEAD = 16
BITS = 14

f32 = jnp.float32
bf16 = jnp.bfloat16
i32 = jnp.int32
i16 = jnp.int16
VMEM = pl.BlockSpec(memory_space=pltpu.VMEM)
SMEM = pl.BlockSpec(memory_space=pltpu.SMEM)
HBM = pl.BlockSpec(memory_space=pltpu.HBM)


def iota(shape, axis):
    return lax.broadcasted_iota(i32, shape, axis)


def one_row_of(block, position):
    return jnp.where(iota(block.shape, 0) == position, block, 0.0).astype(bf16)


def coded(values):
    largest = jnp.maximum(jnp.max(jnp.abs(values), axis=1, keepdims=True), 1e-30)
    exponent = jnp.ceil(jnp.log2(largest))
    whole = jnp.floor(values * jnp.exp2(BITS - exponent) + 0.5)
    return whole.astype(i32).astype(i16), jnp.broadcast_to(exponent, values.shape)


def head_of(places, exponents):
    across = jnp.transpose(exponents)[0:HEAD, :].astype(i32)
    return jnp.where(iota((HEAD, TILE), 0) == 0, places, across).astype(i16)


def block_sums(payloads, first, blocks):
    down = iota((blocks, TILE), 0)
    masks, terms = [], []
    for payload in payloads:
        k_tiles = payload.shape[0] - HEAD
        head = payload[pl.ds(k_tiles, HEAD), :].astype(i32)
        scale = jnp.exp2(head[1:2, :].astype(f32) - BITS)
        masks.append(jnp.where(down == head[0:1, :] - first, scale, 0.0).astype(bf16))
        whole = payload[pl.ds(0, k_tiles), :].astype(i32)
        low = jnp.bitwise_and(whole, 255)
        parts = [(whole - low).astype(f32).astype(bf16), low.astype(f32).astype(bf16)]
        terms.append(jnp.concatenate(parts, axis=1))
    both = jnp.dot(
        jnp.concatenate(masks, axis=1), jnp.concatenate(terms, axis=0), preferred_element_type=f32
    )
    return both[:, :TILE] + both[:, TILE:]


def started(sources, targets, sems):
    copies = [
        pltpu.make_async_copy(source, target, sems.at[n])
        for n, (source, target) in enumerate(zip(sources, targets))
    ]
    for copy in copies:
        copy.start()
    return copies


def transpose_product_kernel(*refs):
    (rows_hbm, cols_hbm, duals_hbm, tiles_hbm), others_hbm, refs = refs[:4], refs[4:11], refs[11:]
    (out_ref, duals, tiles), others, refs = refs[:3], refs[3:10], refs[10:]
    rows, cols, picked, exponents, small_sems, tile_sems, other_sems = refs
    k_tiles = tiles.shape[0]
    n_groups = k_tiles // GROUP
    groups = [pl.ds(g * GROUP, GROUP) for g in range(n_groups)]
    small = started([rows_hbm, duals_hbm, cols_hbm], [rows, duals, cols], small_sems)
    large = started([tiles_hbm.at[g] for g in groups], [tiles.at[g] for g in groups], tile_sems)
    later = started(others_hbm, others, other_sems)
    for copy in small:
        copy.wait()
    for k in range(k_tiles):
        picked[pl.ds(k, 1), :] = duals[pl.ds(rows[k], 1), :]
    for here, copy in zip(groups, large):
        block = picked[here, :].astype(bf16).astype(f32)
        left = jnp.concatenate([one_row_of(block, m) for m in range(GROUP)], axis=1)
        copy.wait()
        terms = jnp.dot(left, tiles[here].reshape(GROUP * TILE, TILE), preferred_element_type=f32)
        whole, exponents[here, :] = coded(terms)
        for target in range(out_ref.shape[0]):
            out_ref[target, here, :] = whole
    head = head_of(cols[...], exponents[...])
    for target in range(out_ref.shape[0]):
        out_ref[target, pl.ds(k_tiles, HEAD), :] = head
    for copy in later:
        copy.wait()


def primal_kernel(
    payloads, primal_ref, cost_ref, lower_ref, upper_ref, kind_ref, steps_ref, next_ref, wanted, extrap
):
    n_row, k_tiles, _ = wanted.shape
    blocks = primal_ref.shape[0]
    padded = extrap.shape[0]
    first = lax.axis_index("row") * blocks
    col_sums = block_sums([payloads.at[s] for s in range(n_row)], first, blocks)
    primal = primal_ref[...]
    kind = kind_ref[...]
    moved = primal - steps_ref[0] * (cost_ref[...] - col_sums)
    moved = jnp.where(kind % 2 == 1, jnp.maximum(moved, lower_ref[...]), moved)
    moved = jnp.where(kind >= 2, jnp.minimum(moved, upper_ref[...]), moved)
    next_ref[...] = moved
    whole = blocks // 8 * 8
    if padded > whole:
        extrap[pl.ds(whole, padded - whole), :] = jnp.zeros((padded - whole, TILE), f32)
    extrap[pl.ds(0, blocks), :] = 2.0 * moved - primal
    right = extrap[...].astype(bf16)
    for s in range(n_row):
        head = payloads[s, pl.ds(k_tiles, HEAD), :].astype(f32)
        places = jnp.transpose(head)[:, 0:1].astype(i32) - first
        mask = jnp.where(iota((k_tiles, padded), 1) == places, 1.0, 0.0)
        wanted[s] = jnp.dot(mask.astype(bf16), right, preferred_element_type=f32).astype(bf16)


def product_kernel(rows_ref, tiles_ref, arrived, out_ref):
    k_tiles = tiles_ref.shape[0]
    block = arrived[0].astype(f32)
    for s in range(1, arrived.shape[0]):
        block += arrived[s].astype(f32)
    down = jnp.transpose(block)
    lane = iota((TILE, k_tiles), 1)
    right = jnp.concatenate(
        [jnp.where(lane % 2 == 0, down, 0.0), jnp.where(lane % 2 == 1, down, 0.0)], axis=0
    ).astype(bf16)
    terms = jnp.zeros((TILE, k_tiles), f32)
    for g in range(k_tiles // 8):
        even = jnp.concatenate([tiles_ref[8 * g + m] for m in (0, 2, 4, 6)], axis=0)
        odd = jnp.concatenate([tiles_ref[8 * g + m] for m in (1, 3, 5, 7)], axis=0)
        products = jnp.dot(jnp.concatenate([even, odd], axis=1), right, preferred_element_type=f32)
        for p in range(4):
            terms = jnp.where(lane // 2 == 4 * g + p, products[p * TILE : (p + 1) * TILE], terms)
    out_ref[pl.ds(0, k_tiles), :], exponents = coded(jnp.transpose(terms))
    out_ref[pl.ds(k_tiles, HEAD), :] = head_of(rows_ref[...], exponents)


def dual_kernel(n_col, *refs):
    payloads, (duals_ref, right_ref, kind_ref, steps_ref, next_ref) = refs[:n_col], refs[n_col:]
    row_sums = block_sums(payloads, 0, duals_ref.shape[0])
    updated = duals_ref[...] + steps_ref[1] * (right_ref[...] - row_sums)
    next_ref[...] = jnp.where(kind_ref[...] == 1, jnp.maximum(updated, 0.0), updated)


def exchange(arrays, axis, back=False):
    size = lax.axis_size(axis)
    arrived = []
    for n, array in enumerate(arrays):
        if n == 0:
            arrived.append(array)
            continue
        if size & (size - 1) == 0:
            pairs = [(i, i ^ n) for i in range(size)]
        else:
            pairs = [(i, (i + (-n if back else n)) % size) for i in range(size)]
        arrived.append(lax.ppermute(array, axis, pairs))
    return arrived


def local(
    block_tiles,
    tile_row,
    tile_col,
    primal,
    duals,
    cost_vec,
    lower_bound,
    upper_bound,
    bound_kind,
    right_side,
    row_kind,
    step_sizes,
):
    k_tiles = block_tiles.shape[2]
    tiles = block_tiles.reshape(k_tiles, TILE, TILE)
    n_row = lax.axis_size("row")
    n_col = lax.axis_size("col")
    col_blocks = primal.shape[0] // TILE
    row_blocks = duals.shape[0] // TILE
    padded = -(-col_blocks // TILE) * TILE
    in_hbm = lambda array: pltpu.with_memory_space_constraint(array, pltpu.HBM)
    by_block = lambda array: in_hbm(array.reshape(-1, TILE))
    shape_of = lambda array: jax.ShapeDtypeStruct(array.shape, array.dtype)
    params = pltpu.CompilerParams(vmem_limit_bytes=32 * 1024 * 1024)
    primal_side = [by_block(a) for a in (primal, cost_vec, lower_bound, upper_bound, bound_kind)]
    dual_side = [by_block(a) for a in (right_side, row_kind)]
    own = [by_block(duals), in_hbm(tiles)]

    col_terms, *kept = pl.pallas_call(
        transpose_product_kernel,
        out_shape=(
            jax.ShapeDtypeStruct((n_row, k_tiles + HEAD, TILE), i16),
            *[shape_of(a) for a in own + primal_side + dual_side],
        ),
        in_specs=[HBM] * 11,
        out_specs=(VMEM,) * 10,
        scratch_shapes=[
            pltpu.SMEM((k_tiles,), i32),
            pltpu.VMEM((1, k_tiles), i32),
            pltpu.VMEM((k_tiles, TILE), f32),
            pltpu.VMEM((k_tiles, TILE), f32),
            pltpu.SemaphoreType.DMA((3,)),
            pltpu.SemaphoreType.DMA((k_tiles // GROUP,)),
            pltpu.SemaphoreType.DMA((7,)),
        ],
        compiler_params=params,
        name="transpose_product",
    )(in_hbm(tile_row.reshape(-1)), in_hbm(tile_col.reshape(1, k_tiles)), *own, *primal_side, *dual_side)
    duals_kept, tiles_kept = kept[:2]
    primal_next, wanted = pl.pallas_call(
        primal_kernel,
        out_shape=(
            jax.ShapeDtypeStruct((col_blocks, TILE), f32),
            jax.ShapeDtypeStruct((n_row, k_tiles, TILE), bf16),
        ),
        in_specs=[VMEM] * 6 + [SMEM],
        out_specs=(VMEM,) * 2,
        scratch_shapes=[pltpu.VMEM((padded, TILE), f32)],
        compiler_params=params,
        name="primal_step",
    )(lax.all_to_all(col_terms, "row", 0, 0), *kept[2:7], step_sizes)
    row_terms = pl.pallas_call(
        product_kernel,
        out_shape=jax.ShapeDtypeStruct((k_tiles + HEAD, TILE), i16),
        in_specs=[VMEM] * 3,
        out_specs=VMEM,
        compiler_params=params,
        name="product",
    )(tile_row.reshape(1, k_tiles), tiles_kept, lax.all_to_all(wanted, "row", 0, 0))
    dual_next = pl.pallas_call(
        lambda *refs: dual_kernel(n_col, *refs),
        out_shape=jax.ShapeDtypeStruct((row_blocks, TILE), f32),
        in_specs=[VMEM] * (n_col + 3) + [SMEM],
        out_specs=VMEM,
        compiler_params=params,
        name="dual_step",
    )(*exchange([row_terms] * n_col, "col"), duals_kept, *kept[7:], step_sizes)
    return (primal_next.reshape(-1), dual_next.reshape(-1))


def solution(mesh):
    return jax.shard_map(
        local,
        mesh=mesh,
        in_specs=(
            P("row", "col", None, None, None),
            P("row", "col", None),
            P("row", "col", None),
            P(("col", "row")),
            P("row"),
            P(("col", "row")),
            P(("col", "row")),
            P(("col", "row")),
            P(("col", "row")),
            P("row"),
            P("row"),
            P(),
        ),
        out_specs=(P(("col", "row")), P("row")),
        check_vma=False,
    )
```

```python
import functools
import jax
import jax.numpy as jnp
from jax import lax
from jax.experimental import pallas as pl
from jax.experimental.pallas import tpu as pltpu
from jax.sharding import PartitionSpec as P

TILE = 128
GROUP = 16
SLOTS = 48
HEAD = 16
BITS = 14

f32 = jnp.float32
bf16 = jnp.bfloat16
i32 = jnp.int32
i16 = jnp.int16
VMEM = pl.BlockSpec(memory_space=pltpu.VMEM)
SMEM = pl.BlockSpec(memory_space=pltpu.SMEM)
HBM = pl.BlockSpec(memory_space=pltpu.HBM)


def iota(shape, axis):
    return lax.broadcasted_iota(i32, shape, axis)


def where_one(condition):
    return jnp.where(condition, 1.0, 0.0)


def one_row_of(block, position):
    return jnp.where(iota(block.shape, 0) == position, block, 0.0).astype(bf16)


def rounds_of(n_row):
    chunks = n_row * SLOTS // TILE
    return chunks, -(-(2 * chunks + 1) // 8) * 8


def coded(values):
    largest = jnp.maximum(jnp.max(jnp.abs(values), axis=1, keepdims=True), 1e-30)
    exponent = jnp.ceil(jnp.log2(largest))
    whole = jnp.floor(values * jnp.exp2(BITS - exponent) + 0.5).astype(i32)
    return whole, jnp.broadcast_to(exponent, values.shape)


def two_parts(whole):
    low = jnp.bitwise_and(whole, 255)
    parts = [(whole - low).astype(f32), low.astype(f32)]
    return jnp.concatenate(parts, axis=1).astype(bf16)


def picked_sums(masks, wholes):
    left = masks[0] if len(masks) == 1 else jnp.concatenate(masks, axis=1)
    both = jnp.dot(
        left.astype(bf16),
        jnp.concatenate([two_parts(w) for w in wholes], axis=0),
        preferred_element_type=f32,
    )
    return both[:, :TILE] + both[:, TILE:]


def scaled_mask(down, places, exponents):
    return jnp.where(down == places, jnp.exp2(exponents.astype(f32) - BITS), 0.0)


def started(sources, targets, sems):
    copies = [
        pltpu.make_async_copy(source, target, sems.at[n])
        for n, (source, target) in enumerate(zip(sources, targets))
    ]
    for copy in copies:
        copy.start()
    return copies


def transpose_product_kernel(owned, *refs):
    (rows_hbm, cols_hbm, duals_hbm, tiles_hbm), others_hbm, refs = refs[:4], refs[4:9], refs[9:]
    (out_ref, slot_ref, duals, tiles), others, refs = refs[:4], refs[4:9], refs[9:]
    rows, cols, picked, exponents, parts, small_sems, tile_sems, other_sems = refs
    n_row = out_ref.shape[0]
    chunks, head_rows = rounds_of(n_row)
    most = SLOTS - head_rows
    k_tiles = tiles.shape[0]
    n_groups = k_tiles // GROUP
    groups = [pl.ds(g * GROUP, GROUP) for g in range(n_groups)]
    small = started([cols_hbm, rows_hbm, duals_hbm], [cols, rows, duals], small_sems)
    large = started([tiles_hbm.at[g] for g in groups], [tiles.at[g] for g in groups], tile_sems)
    later = started(others_hbm, others, other_sems)

    small[0].wait()
    square = (k_tiles, k_tiles)
    col_across = cols[...]
    col_down = jnp.transpose(jnp.broadcast_to(col_across.astype(f32), square)).astype(i32)
    owner_across = sum((col_across >= o * owned).astype(i32) for o in range(1, n_row))
    owner_down = sum((col_down >= o * owned).astype(i32) for o in range(1, n_row))
    same = owner_down == owner_across
    earlier_down = iota(square, 0) < iota(square, 1)
    earlier_across = iota(square, 1) < iota(square, 0)
    rank_across = jnp.sum(where_one(same & earlier_down), axis=0, keepdims=True).astype(i32)
    rank_down = jnp.sum(where_one(same & earlier_across), axis=1, keepdims=True).astype(i32)
    slot_across = jnp.where(rank_across < most, owner_across * SLOTS + head_rows + rank_across, -1)
    slot_down = jnp.where(rank_down < most, owner_down * SLOTS + head_rows + rank_down, -1)
    slot_ref[...] = slot_down
    too_many = where_one(jnp.max(rank_across, axis=1, keepdims=True) >= most)
    to_slots = where_one(iota((n_row * SLOTS, k_tiles), 0) == slot_across)
    here = jnp.where(rank_down < most, lax.axis_index("row") * SLOTS + head_rows + rank_down, -1)
    to_lanes = where_one(iota((k_tiles, n_row * SLOTS), 1) == here)
    of_owner = where_one(iota((n_row, k_tiles), 0) == owner_across)
    place = col_across - owner_across * owned + 1
    place_low = jnp.bitwise_and(place, 255)
    head_left = jnp.concatenate(
        [of_owner * (place - place_low).astype(f32), of_owner * place_low.astype(f32), of_owner], axis=0
    ).astype(bf16)

    for copy in small[1:]:
        copy.wait()
    for k in range(k_tiles):
        picked[pl.ds(k, 1), :] = duals[pl.ds(rows[k], 1), :]
    for group, copy in zip(groups, large):
        block = picked[group, :].astype(bf16).astype(f32)
        left = jnp.concatenate([one_row_of(block, m) for m in range(GROUP)], axis=1)
        copy.wait()
        terms = jnp.dot(left, tiles[group].reshape(GROUP * TILE, TILE), preferred_element_type=f32)
        whole, exponents[group, :] = coded(terms)
        parts[group, :] = two_parts(whole)

    scaled = [to_lanes, to_lanes * jnp.concatenate([exponents[...]] * chunks, axis=1)]
    heads = jnp.dot(head_left, jnp.concatenate(scaled, axis=1).astype(bf16), preferred_element_type=f32)
    width = n_row * SLOTS
    places = heads[:n_row, :width] + heads[n_row : 2 * n_row, :width]
    scales = heads[2 * n_row :, width:]
    both = jnp.dot(to_slots.astype(bf16), parts[...], preferred_element_type=f32)
    body = both[:, :TILE] + both[:, TILE:]
    line = iota((head_rows, TILE), 0)
    for o in range(n_row):
        head = jnp.where(line == 2 * chunks, too_many, 0.0)
        for c in range(chunks):
            lanes = slice(c * TILE, (c + 1) * TILE)
            head = jnp.where(line == c, places[o : o + 1, lanes], head)
            head = jnp.where(line == chunks + c, scales[o : o + 1, lanes], head)
        rows_of = body[o * SLOTS + head_rows : (o + 1) * SLOTS]
        out_ref[o] = jnp.concatenate([head, rows_of], axis=0).astype(i32).astype(i16)
    for copy in later:
        copy.wait()


def primal_kernel(
    payloads, primal_ref, cost_ref, lower_ref, upper_ref, kind_ref, steps_ref, next_ref, wanted, flag_ref, extrap
):
    n_row = payloads.shape[0]
    chunks, head_rows = rounds_of(n_row)
    blocks = primal_ref.shape[0]
    padded = extrap.shape[0]
    head = jnp.zeros((head_rows, TILE), f32)
    for s in range(n_row):
        head += payloads[s].astype(i32)[:head_rows].astype(f32)
    flag_ref[...] = jnp.broadcast_to(head[2 * chunks : 2 * chunks + 1], flag_ref.shape)
    whole = payloads[...].reshape(n_row * SLOTS, TILE).astype(i32)
    down = iota((blocks, TILE), 0) + 1
    head_whole = head.astype(i32)
    masks, wholes = [], []
    for c in range(chunks):
        masks.append(scaled_mask(down, head_whole[c : c + 1], head_whole[chunks + c : chunks + c + 1]))
        wholes.append(whole[c * TILE : (c + 1) * TILE])
    col_sums = picked_sums(masks, wholes)
    primal = primal_ref[...]
    kind = kind_ref[...]
    moved = primal - steps_ref[0] * (cost_ref[...] - col_sums)
    moved = jnp.where(kind % 2 == 1, jnp.maximum(moved, lower_ref[...]), moved)
    moved = jnp.where(kind >= 2, jnp.minimum(moved, upper_ref[...]), moved)
    next_ref[...] = moved
    aligned = blocks // 8 * 8
    if padded > aligned:
        extrap[pl.ds(aligned, padded - aligned), :] = jnp.zeros((padded - aligned, TILE), f32)
    extrap[pl.ds(0, blocks), :] = 2.0 * moved - primal
    right = extrap[...].astype(bf16)
    across = iota((TILE, padded), 1) + 1
    places = jnp.transpose(head).astype(i32)
    sent = [
        jnp.dot(where_one(across == places[:, c : c + 1]).astype(bf16), right, preferred_element_type=f32)
        for c in range(chunks)
    ]
    wanted[...] = jnp.concatenate(sent, axis=0).astype(bf16).reshape(wanted.shape)


def product_kernel(*refs):
    (rows_ref, slot_ref, tiles_ref, arrived, flag_ref), others_hbm, refs = refs[:5], refs[5:7], refs[7:]
    out_ref, others, sems = refs[0], refs[1:3], refs[3]
    later = started(others_hbm, others, sems)
    k_tiles = tiles_ref.shape[0]
    received = arrived[...].reshape(-1, TILE)
    across = iota((k_tiles, received.shape[0]), 1)
    slots = jnp.concatenate([slot_ref[...]] * (received.shape[0] // TILE), axis=1)
    block = jnp.dot(where_one(across == slots).astype(bf16), received, preferred_element_type=f32)
    down = jnp.transpose(block)
    lane = iota((TILE, k_tiles), 1)
    right = jnp.concatenate(
        [jnp.where(lane % 2 == 0, down, 0.0), jnp.where(lane % 2 == 1, down, 0.0)], axis=0
    ).astype(bf16)
    terms = jnp.zeros((TILE, k_tiles), f32)
    for g in range(k_tiles // 8):
        even = jnp.concatenate([tiles_ref[8 * g + m] for m in (0, 2, 4, 6)], axis=0)
        odd = jnp.concatenate([tiles_ref[8 * g + m] for m in (1, 3, 5, 7)], axis=0)
        products = jnp.dot(jnp.concatenate([even, odd], axis=1), right, preferred_element_type=f32)
        for p in range(4):
            terms = jnp.where(lane // 2 == 4 * g + p, products[p * TILE : (p + 1) * TILE], terms)
    whole, exponents = coded(jnp.transpose(terms))
    out_ref[pl.ds(0, k_tiles), :] = whole.astype(i16)
    line = iota((HEAD, TILE), 0)
    head = jnp.where(line == 0, rows_ref[...], jnp.transpose(exponents)[0:HEAD, :].astype(i32))
    head = jnp.where(line == 2, flag_ref[0:1, :].astype(i32), head)
    out_ref[pl.ds(k_tiles, HEAD), :] = head.astype(i16)
    for copy in later:
        copy.wait()


def dual_kernel(n_col, *refs):
    payloads, (duals_ref, right_ref, kind_ref, steps_ref, next_ref, flag_ref) = refs[:n_col], refs[n_col:]
    k_tiles = payloads[0].shape[0] - HEAD
    down = iota((duals_ref.shape[0], k_tiles), 0)
    masks, wholes = [], []
    flags = jnp.zeros((1, TILE), i32)
    for payload in payloads:
        head = payload[pl.ds(k_tiles, HEAD), :].astype(i32)
        masks.append(scaled_mask(down, head[0:1], head[1:2]))
        wholes.append(payload[pl.ds(0, k_tiles), :].astype(i32))
        flags += head[2:3]
    row_sums = picked_sums(masks, wholes)
    updated = duals_ref[...] + steps_ref[1] * (right_ref[...] - row_sums)
    next_ref[...] = jnp.where(kind_ref[...] == 1, jnp.maximum(updated, 0.0), updated)
    flag_ref[0] = jnp.max(flags)


def partners(axis):
    size = lax.axis_size(axis)
    if size & (size - 1) == 0:
        there = [[(i, i ^ n) for i in range(size)] for n in range(1, size)]
    else:
        there = [[(i, (i + n) % size) for i in range(size)] for n in range(1, size)]
    return [(pairs, [(j, i) for i, j in pairs]) for pairs in there]


def gathered_along(array, axis):
    return [array] + [lax.ppermute(array, axis, there) for there, _ in partners(axis)]


def sums_at(places, terms, blocks):
    mask = (jnp.arange(blocks)[:, None] == jnp.concatenate(places)[None, :]).astype(f32)
    return jnp.dot(mask, jnp.concatenate(terms), precision=lax.Precision.HIGHEST).reshape(-1)


def full_step(
    tiles, rows, cols, primal, duals, cost_vec, lower_bound, upper_bound, bound_kind, right_side, row_kind, steps
):
    col_blocks = primal.shape[0] // TILE
    row_blocks = duals.shape[0] // TILE
    wide = tiles.astype(f32)
    dual_blocks = duals.astype(bf16).astype(f32).reshape(row_blocks, TILE)[rows]
    col_terms = jnp.einsum("kij,ki->kj", wide, dual_blocks)
    first = lax.axis_index("row") * col_blocks
    places = [there - first for there in gathered_along(cols, "row")]
    places = [jnp.where((p >= 0) & (p < col_blocks), p, col_blocks) for p in places]
    col_sums = sums_at(places, gathered_along(col_terms, "row"), col_blocks)
    moved = primal - steps[0] * (cost_vec - col_sums)
    moved = jnp.where(bound_kind % 2 == 1, jnp.maximum(moved, lower_bound), moved)
    moved = jnp.where(bound_kind >= 2, jnp.minimum(moved, upper_bound), moved)
    extrap = (2.0 * moved - primal).astype(bf16).reshape(col_blocks, TILE)
    wanted = [
        jnp.where((p < col_blocks)[:, None], extrap[jnp.minimum(p, col_blocks - 1)], jnp.zeros((), bf16))
        for p in places
    ]
    blocks = wanted[0].astype(f32)
    for block, (_, back) in zip(wanted[1:], partners("row")):
        blocks += lax.ppermute(block, "row", back).astype(f32)
    row_terms = jnp.einsum("kij,kj->ki", wide, blocks)
    row_sums = sums_at(gathered_along(rows, "col"), gathered_along(row_terms, "col"), row_blocks)
    updated = duals + steps[1] * (right_side - row_sums)
    return moved, jnp.where(row_kind == 1, jnp.maximum(updated, 0.0), updated)


def local(
    block_tiles,
    tile_row,
    tile_col,
    primal,
    duals,
    cost_vec,
    lower_bound,
    upper_bound,
    bound_kind,
    right_side,
    row_kind,
    step_sizes,
):
    k_tiles = block_tiles.shape[2]
    tiles = block_tiles.reshape(k_tiles, TILE, TILE)
    rows = tile_row.reshape(-1)
    cols = tile_col.reshape(-1)
    n_row = lax.axis_size("row")
    n_col = lax.axis_size("col")
    col_blocks = primal.shape[0] // TILE
    row_blocks = duals.shape[0] // TILE
    padded = -(-col_blocks // TILE) * TILE
    in_hbm = lambda array: pltpu.with_memory_space_constraint(array, pltpu.HBM)
    by_block = lambda array: in_hbm(array.reshape(-1, TILE))
    shape_of = lambda array: jax.ShapeDtypeStruct(array.shape, array.dtype)
    params = pltpu.CompilerParams(vmem_limit_bytes=32 * 1024 * 1024)
    primal_side = [by_block(a) for a in (primal, cost_vec, lower_bound, upper_bound, bound_kind)]
    dual_side = [by_block(a) for a in (right_side, row_kind)]
    own = [by_block(duals), in_hbm(tiles)]

    col_terms, slots, duals_kept, tiles_kept, *primal_kept = pl.pallas_call(
        functools.partial(transpose_product_kernel, col_blocks),
        out_shape=(
            jax.ShapeDtypeStruct((n_row, SLOTS, TILE), i16),
            jax.ShapeDtypeStruct((k_tiles, TILE), i32),
            *[shape_of(a) for a in own + primal_side],
        ),
        in_specs=[HBM] * 9,
        out_specs=(VMEM,) * 9,
        scratch_shapes=[
            pltpu.SMEM((k_tiles,), i32),
            pltpu.VMEM((1, k_tiles), i32),
            pltpu.VMEM((k_tiles, TILE), f32),
            pltpu.VMEM((k_tiles, TILE), f32),
            pltpu.VMEM((k_tiles, 2 * TILE), bf16),
            pltpu.SemaphoreType.DMA((3,)),
            pltpu.SemaphoreType.DMA((k_tiles // GROUP,)),
            pltpu.SemaphoreType.DMA((5,)),
        ],
        compiler_params=params,
        name="transpose_product",
    )(in_hbm(rows), in_hbm(cols.reshape(1, k_tiles)), *own, *primal_side)
    primal_next, wanted, flag = pl.pallas_call(
        primal_kernel,
        out_shape=(
            jax.ShapeDtypeStruct((col_blocks, TILE), f32),
            jax.ShapeDtypeStruct((n_row, SLOTS, TILE), bf16),
            jax.ShapeDtypeStruct((8, TILE), f32),
        ),
        in_specs=[VMEM] * 6 + [SMEM],
        out_specs=(VMEM,) * 3,
        scratch_shapes=[pltpu.VMEM((padded, TILE), f32)],
        compiler_params=params,
        name="primal_step",
    )(lax.all_to_all(col_terms, "row", 0, 0), *primal_kept, step_sizes)
    row_terms, *dual_kept = pl.pallas_call(
        product_kernel,
        out_shape=(
            jax.ShapeDtypeStruct((k_tiles + HEAD, TILE), i16),
            *[shape_of(a) for a in dual_side],
        ),
        in_specs=[VMEM] * 5 + [HBM] * 2,
        out_specs=(VMEM,) * 3,
        scratch_shapes=[pltpu.SemaphoreType.DMA((2,))],
        compiler_params=params,
        name="product",
    )(rows.reshape(1, k_tiles), slots, tiles_kept, lax.all_to_all(wanted, "row", 0, 0), flag, *dual_side)
    dual_next, too_many = pl.pallas_call(
        functools.partial(dual_kernel, n_col),
        out_shape=(jax.ShapeDtypeStruct((row_blocks, TILE), f32), jax.ShapeDtypeStruct((1,), i32)),
        in_specs=[VMEM] * (n_col + 3) + [SMEM],
        out_specs=(VMEM, SMEM),
        compiler_params=params,
        name="dual_step",
    )(*gathered_along(row_terms, "col"), duals_kept, *dual_kept, step_sizes)
    vectors = (primal, duals, cost_vec, lower_bound, upper_bound, bound_kind, right_side, row_kind, step_sizes)
    return lax.cond(
        too_many[0] > 0,
        lambda done: full_step(tiles, rows, cols, *vectors),
        lambda done: done,
        (primal_next.reshape(-1), dual_next.reshape(-1)),
    )


def solution(mesh):
    return jax.shard_map(
        local,
        mesh=mesh,
        in_specs=(
            P("row", "col", None, None, None),
            P("row", "col", None),
            P("row", "col", None),
            P(("col", "row")),
            P("row"),
            P(("col", "row")),
            P(("col", "row")),
            P(("col", "row")),
            P(("col", "row")),
            P("row"),
            P("row"),
            P(),
        ),
        out_specs=(P(("col", "row")), P("row")),
        check_vma=False,
    )
```

```python
import functools
import jax
import jax.numpy as jnp
from jax import lax
from jax.experimental import pallas as pl
from jax.experimental.pallas import tpu as pltpu
from jax.sharding import PartitionSpec as P

TILE = 128
GROUP = 16
SLOTS = 48
HEAD = 16
BITS = 14

f32 = jnp.float32
bf16 = jnp.bfloat16
i32 = jnp.int32
i16 = jnp.int16
VMEM = pl.BlockSpec(memory_space=pltpu.VMEM)
SMEM = pl.BlockSpec(memory_space=pltpu.SMEM)
HBM = pl.BlockSpec(memory_space=pltpu.HBM)


def iota(shape, axis):
    return lax.broadcasted_iota(i32, shape, axis)


def where_one(condition):
    return jnp.where(condition, 1.0, 0.0)


def one_row_of(block, position):
    return jnp.where(iota(block.shape, 0) == position, block, 0.0).astype(bf16)


def rounds_of(n_row):
    chunks = n_row * SLOTS // TILE
    return chunks, -(-(2 * chunks + 1) // 8) * 8


def coded(values):
    largest = jnp.maximum(jnp.max(jnp.abs(values), axis=1, keepdims=True), 1e-30)
    exponent = jnp.ceil(jnp.log2(largest))
    whole = jnp.floor(values * jnp.exp2(BITS - exponent) + 0.5).astype(i32)
    return whole, jnp.broadcast_to(exponent, values.shape)


def two_parts(whole):
    low = jnp.bitwise_and(whole, 255)
    parts = [(whole - low).astype(f32), low.astype(f32)]
    return jnp.concatenate(parts, axis=1).astype(bf16)


def picked_sums(masks, wholes):
    left = masks[0] if len(masks) == 1 else jnp.concatenate(masks, axis=1)
    both = jnp.dot(
        left.astype(bf16),
        jnp.concatenate([two_parts(w) for w in wholes], axis=0),
        preferred_element_type=f32,
    )
    return both[:, :TILE] + both[:, TILE:]


def scaled_mask(down, places, exponents):
    return jnp.where(down == places, jnp.exp2(exponents.astype(f32) - BITS), 0.0)


def started(sources, targets, sems):
    copies = [
        pltpu.make_async_copy(source, target, sems.at[n])
        for n, (source, target) in enumerate(zip(sources, targets))
    ]
    for copy in copies:
        copy.start()
    return copies


def transpose_product_kernel(owned, *refs):
    (rows_hbm, cols_hbm, duals_hbm, tiles_hbm), (out_ref, slot_ref, duals, tiles), refs = refs[:4], refs[4:8], refs[8:]
    rows, cols, picked, exponents, parts, small_sems, tile_sems = refs
    n_row = 2 * out_ref.shape[0]
    chunks, head_rows = rounds_of(n_row)
    most = SLOTS - head_rows
    me = lax.axis_index("row")
    k_tiles = tiles.shape[0]
    n_groups = k_tiles // GROUP
    groups = [pl.ds(g * GROUP, GROUP) for g in range(n_groups)]
    small = started([cols_hbm, rows_hbm, duals_hbm], [cols, rows, duals], small_sems)
    large = started([tiles_hbm.at[g] for g in groups], [tiles.at[g] for g in groups], tile_sems)

    small[0].wait()
    square = (k_tiles, k_tiles)
    col_across = cols[...]
    col_down = jnp.transpose(jnp.broadcast_to(col_across.astype(f32), square)).astype(i32)
    owner_across = sum((col_across >= o * owned).astype(i32) for o in range(1, n_row))
    owner_down = sum((col_down >= o * owned).astype(i32) for o in range(1, n_row))
    same = owner_down == owner_across
    earlier_down = iota(square, 0) < iota(square, 1)
    earlier_across = iota(square, 1) < iota(square, 0)
    rank_across = jnp.sum(where_one(same & earlier_down), axis=0, keepdims=True).astype(i32)
    rank_down = jnp.sum(where_one(same & earlier_across), axis=1, keepdims=True).astype(i32)
    slot_across = jnp.where(rank_across < most, owner_across * SLOTS + head_rows + rank_across, -1)
    slot_down = jnp.where(rank_down < most, owner_down * SLOTS + head_rows + rank_down, -1)
    slot_ref[...] = slot_down
    too_many = where_one(jnp.max(rank_across, axis=1, keepdims=True) >= most)
    to_slots = where_one(iota((n_row * SLOTS, k_tiles), 0) == slot_across)
    here = jnp.where(rank_down < most, me * SLOTS + head_rows + rank_down, -1)
    to_lanes = where_one(iota((k_tiles, n_row * SLOTS), 1) == here)
    of_owner = where_one(iota((n_row, k_tiles), 0) == owner_across)
    place = col_across - owner_across * owned + 1
    place_low = jnp.bitwise_and(place, 255)
    head_left = jnp.concatenate(
        [of_owner * (place - place_low).astype(f32), of_owner * place_low.astype(f32), of_owner], axis=0
    ).astype(bf16)

    for copy in small[1:]:
        copy.wait()
    for k in range(k_tiles):
        picked[pl.ds(k, 1), :] = duals[pl.ds(rows[k], 1), :]
    for group, copy in zip(groups, large):
        block = picked[group, :].astype(bf16).astype(f32)
        left = jnp.concatenate([one_row_of(block, m) for m in range(GROUP)], axis=1)
        copy.wait()
        terms = jnp.dot(left, tiles[group].reshape(GROUP * TILE, TILE), preferred_element_type=f32)
        whole, exponents[group, :] = coded(terms)
        parts[group, :] = two_parts(whole)

    scaled = [to_lanes, to_lanes * jnp.concatenate([exponents[...]] * chunks, axis=1)]
    heads = jnp.dot(head_left, jnp.concatenate(scaled, axis=1).astype(bf16), preferred_element_type=f32)
    width = n_row * SLOTS
    places = heads[:n_row, :width] + heads[n_row : 2 * n_row, :width]
    scales = heads[2 * n_row :, width:]
    both = jnp.dot(to_slots.astype(bf16), parts[...], preferred_element_type=f32)
    body = both[:, :TILE] + both[:, TILE:]
    line = iota((head_rows, TILE), 0)
    payloads = []
    for o in range(n_row):
        head = jnp.where(line == 2 * chunks, too_many, 0.0)
        for c in range(chunks):
            lanes = slice(c * TILE, (c + 1) * TILE)
            head = jnp.where(line == c, places[o : o + 1, lanes], head)
            head = jnp.where(line == chunks + c, scales[o : o + 1, lanes], head)
        rows_of = body[o * SLOTS + head_rows : (o + 1) * SLOTS]
        payloads.append(jnp.concatenate([head, rows_of], axis=0))
    for z, (same_side, other_side) in enumerate(by_side(me, payloads)):
        out_ref[z, 0] = same_side.astype(i32).astype(i16)
        out_ref[z, 1] = other_side.astype(i32).astype(i16)


def by_side(me, blocks):
    even = me % 2 == 0
    return [
        (jnp.where(even, first, second), jnp.where(even, second, first))
        for first, second in zip(blocks[0::2], blocks[1::2])
    ]


def by_place(me, near, far):
    even = me % 2 == 0
    blocks = []
    for z in range(far.shape[0]):
        same_side, other_side = near[z, 0].astype(f32), far[z].astype(f32)
        blocks += [jnp.where(even, same_side, other_side), jnp.where(even, other_side, same_side)]
    return jnp.concatenate(blocks, axis=0)


def primal_kernel(
    near, far, primal_ref, cost_ref, lower_ref, upper_ref, kind_ref, steps_ref, next_ref, wanted, flag_ref, extrap
):
    n_row = 2 * far.shape[0]
    me = lax.axis_index("row")
    chunks, head_rows = rounds_of(n_row)
    blocks = primal_ref.shape[0]
    padded = extrap.shape[0]
    arrived = by_place(me, near, far)
    head = jnp.zeros((head_rows, TILE), f32)
    for s in range(n_row):
        head += arrived[s * SLOTS : s * SLOTS + head_rows]
    flag_ref[...] = jnp.broadcast_to(head[2 * chunks : 2 * chunks + 1], flag_ref.shape)
    whole = arrived.astype(i32)
    down = iota((blocks, TILE), 0) + 1
    head_whole = head.astype(i32)
    masks, wholes = [], []
    for c in range(chunks):
        masks.append(scaled_mask(down, head_whole[c : c + 1], head_whole[chunks + c : chunks + c + 1]))
        wholes.append(whole[c * TILE : (c + 1) * TILE])
    col_sums = picked_sums(masks, wholes)
    primal = primal_ref[...]
    kind = kind_ref[...]
    moved = primal - steps_ref[0] * (cost_ref[...] - col_sums)
    moved = jnp.where(kind % 2 == 1, jnp.maximum(moved, lower_ref[...]), moved)
    moved = jnp.where(kind >= 2, jnp.minimum(moved, upper_ref[...]), moved)
    next_ref[...] = moved
    aligned = blocks // 8 * 8
    if padded > aligned:
        extrap[pl.ds(aligned, padded - aligned), :] = jnp.zeros((padded - aligned, TILE), f32)
    extrap[pl.ds(0, blocks), :] = 2.0 * moved - primal
    right = extrap[...].astype(bf16)
    across = iota((TILE, padded), 1) + 1
    places = jnp.transpose(head).astype(i32)
    sent = [
        jnp.dot(where_one(across == places[:, c : c + 1]).astype(bf16), right, preferred_element_type=f32)
        for c in range(chunks)
    ]
    sent = jnp.concatenate(sent, axis=0)
    blocks_sent = [sent[s * SLOTS : (s + 1) * SLOTS] for s in range(n_row)]
    for z, (same_side, other_side) in enumerate(by_side(me, blocks_sent)):
        wanted[z, 0] = same_side.astype(bf16)
        wanted[z, 1] = other_side.astype(bf16)


def product_kernel(*refs):
    (rows_ref, slot_ref, tiles_ref, near, far, flag_ref), others_hbm, refs = refs[:6], refs[6:8], refs[8:]
    out_ref, others, sems = refs[0], refs[1:3], refs[3]
    later = started(others_hbm, others, sems)
    k_tiles = tiles_ref.shape[0]
    received = by_place(lax.axis_index("row"), near, far).astype(bf16)
    across = iota((k_tiles, received.shape[0]), 1)
    slots = jnp.concatenate([slot_ref[...]] * (received.shape[0] // TILE), axis=1)
    block = jnp.dot(where_one(across == slots).astype(bf16), received, preferred_element_type=f32)
    down = jnp.transpose(block)
    lane = iota((TILE, k_tiles), 1)
    right = jnp.concatenate(
        [jnp.where(lane % 2 == 0, down, 0.0), jnp.where(lane % 2 == 1, down, 0.0)], axis=0
    ).astype(bf16)
    terms = jnp.zeros((TILE, k_tiles), f32)
    for g in range(k_tiles // 8):
        even = jnp.concatenate([tiles_ref[8 * g + m] for m in (0, 2, 4, 6)], axis=0)
        odd = jnp.concatenate([tiles_ref[8 * g + m] for m in (1, 3, 5, 7)], axis=0)
        products = jnp.dot(jnp.concatenate([even, odd], axis=1), right, preferred_element_type=f32)
        for p in range(4):
            terms = jnp.where(lane // 2 == 4 * g + p, products[p * TILE : (p + 1) * TILE], terms)
    whole, exponents = coded(jnp.transpose(terms))
    out_ref[pl.ds(0, k_tiles), :] = whole.astype(i16)
    line = iota((HEAD, TILE), 0)
    head = jnp.where(line == 0, rows_ref[...], jnp.transpose(exponents)[0:HEAD, :].astype(i32))
    head = jnp.where(line == 2, flag_ref[0:1, :].astype(i32), head)
    out_ref[pl.ds(k_tiles, HEAD), :] = head.astype(i16)
    for copy in later:
        copy.wait()


def dual_kernel(n_col, *refs):
    payloads, (duals_ref, right_ref, kind_ref, steps_ref, next_ref, flag_ref) = refs[:n_col], refs[n_col:]
    k_tiles = payloads[0].shape[0] - HEAD
    down = iota((duals_ref.shape[0], k_tiles), 0)
    masks, wholes = [], []
    flags = jnp.zeros((1, TILE), i32)
    for payload in payloads:
        head = payload[pl.ds(k_tiles, HEAD), :].astype(i32)
        masks.append(scaled_mask(down, head[0:1], head[1:2]))
        wholes.append(payload[pl.ds(0, k_tiles), :].astype(i32))
        flags += head[2:3]
    row_sums = picked_sums(masks, wholes)
    updated = duals_ref[...] + steps_ref[1] * (right_ref[...] - row_sums)
    next_ref[...] = jnp.where(kind_ref[...] == 1, jnp.maximum(updated, 0.0), updated)
    flag_ref[0] = jnp.max(flags)


def partners(axis):
    size = lax.axis_size(axis)
    if size & (size - 1) == 0:
        there = [[(i, i ^ n) for i in range(size)] for n in range(1, size)]
    else:
        there = [[(i, (i + n) % size) for i in range(size)] for n in range(1, size)]
    return [(pairs, [(j, i) for i, j in pairs]) for pairs in there]


def gathered_along(array, axis):
    return [array] + [lax.ppermute(array, axis, there) for there, _ in partners(axis)]


def exchanged_along_row(array):
    size = lax.axis_size("row")
    groups = [list(range(0, size, 2)), list(range(1, size, 2))]
    near = lax.all_to_all(array, "row", 0, 0, axis_index_groups=groups)
    return near, lax.ppermute(near[:, 1], "row", [(i, i ^ 1) for i in range(size)])


def sums_at(places, terms, blocks):
    mask = (jnp.arange(blocks)[:, None] == jnp.concatenate(places)[None, :]).astype(f32)
    return jnp.dot(mask, jnp.concatenate(terms), precision=lax.Precision.HIGHEST).reshape(-1)


def full_step(
    tiles, rows, cols, primal, duals, cost_vec, lower_bound, upper_bound, bound_kind, right_side, row_kind, steps
):
    col_blocks = primal.shape[0] // TILE
    row_blocks = duals.shape[0] // TILE
    wide = tiles.astype(f32)
    dual_blocks = duals.astype(bf16).astype(f32).reshape(row_blocks, TILE)[rows]
    col_terms = jnp.einsum("kij,ki->kj", wide, dual_blocks)
    first = lax.axis_index("row") * col_blocks
    places = [there - first for there in gathered_along(cols, "row")]
    places = [jnp.where((p >= 0) & (p < col_blocks), p, col_blocks) for p in places]
    col_sums = sums_at(places, gathered_along(col_terms, "row"), col_blocks)
    moved = primal - steps[0] * (cost_vec - col_sums)
    moved = jnp.where(bound_kind % 2 == 1, jnp.maximum(moved, lower_bound), moved)
    moved = jnp.where(bound_kind >= 2, jnp.minimum(moved, upper_bound), moved)
    extrap = (2.0 * moved - primal).astype(bf16).reshape(col_blocks, TILE)
    wanted = [
        jnp.where((p < col_blocks)[:, None], extrap[jnp.minimum(p, col_blocks - 1)], jnp.zeros((), bf16))
        for p in places
    ]
    blocks = wanted[0].astype(f32)
    for block, (_, back) in zip(wanted[1:], partners("row")):
        blocks += lax.ppermute(block, "row", back).astype(f32)
    row_terms = jnp.einsum("kij,kj->ki", wide, blocks)
    row_sums = sums_at(gathered_along(rows, "col"), gathered_along(row_terms, "col"), row_blocks)
    updated = duals + steps[1] * (right_side - row_sums)
    return moved, jnp.where(row_kind == 1, jnp.maximum(updated, 0.0), updated)


def local(
    block_tiles,
    tile_row,
    tile_col,
    primal,
    duals,
    cost_vec,
    lower_bound,
    upper_bound,
    bound_kind,
    right_side,
    row_kind,
    step_sizes,
):
    k_tiles = block_tiles.shape[2]
    tiles = block_tiles.reshape(k_tiles, TILE, TILE)
    rows = tile_row.reshape(-1)
    cols = tile_col.reshape(-1)
    n_row = lax.axis_size("row")
    n_col = lax.axis_size("col")
    col_blocks = primal.shape[0] // TILE
    row_blocks = duals.shape[0] // TILE
    padded = -(-col_blocks // TILE) * TILE
    in_hbm = lambda array: pltpu.with_memory_space_constraint(array, pltpu.HBM)
    by_block = lambda array: in_hbm(array.reshape(-1, TILE))
    shape_of = lambda array: jax.ShapeDtypeStruct(array.shape, array.dtype)
    params = pltpu.CompilerParams(vmem_limit_bytes=32 * 1024 * 1024)
    primal_side = [a.reshape(-1, TILE) for a in (primal, cost_vec, lower_bound, upper_bound, bound_kind)]
    dual_side = [by_block(a) for a in (right_side, row_kind)]
    own = [by_block(duals), in_hbm(tiles)]

    col_terms, slots, duals_kept, tiles_kept = pl.pallas_call(
        functools.partial(transpose_product_kernel, col_blocks),
        out_shape=(
            jax.ShapeDtypeStruct((n_row // 2, 2, SLOTS, TILE), i16),
            jax.ShapeDtypeStruct((k_tiles, TILE), i32),
            *[shape_of(a) for a in own],
        ),
        in_specs=[HBM] * 4,
        out_specs=(VMEM,) * 4,
        scratch_shapes=[
            pltpu.SMEM((k_tiles,), i32),
            pltpu.VMEM((1, k_tiles), i32),
            pltpu.VMEM((k_tiles, TILE), f32),
            pltpu.VMEM((k_tiles, TILE), f32),
            pltpu.VMEM((k_tiles, 2 * TILE), bf16),
            pltpu.SemaphoreType.DMA((3,)),
            pltpu.SemaphoreType.DMA((k_tiles // GROUP,)),
        ],
        compiler_params=params,
        name="transpose_product",
    )(in_hbm(rows), in_hbm(cols.reshape(1, k_tiles)), *own)
    primal_next, wanted, flag = pl.pallas_call(
        primal_kernel,
        out_shape=(
            jax.ShapeDtypeStruct((col_blocks, TILE), f32),
            jax.ShapeDtypeStruct((n_row // 2, 2, SLOTS, TILE), bf16),
            jax.ShapeDtypeStruct((8, TILE), f32),
        ),
        in_specs=[VMEM] * 7 + [SMEM],
        out_specs=(VMEM,) * 3,
        scratch_shapes=[pltpu.VMEM((padded, TILE), f32)],
        compiler_params=params,
        name="primal_step",
    )(*exchanged_along_row(col_terms), *primal_side, step_sizes)
    row_terms, *dual_kept = pl.pallas_call(
        product_kernel,
        out_shape=(
            jax.ShapeDtypeStruct((k_tiles + HEAD, TILE), i16),
            *[shape_of(a) for a in dual_side],
        ),
        in_specs=[VMEM] * 6 + [HBM] * 2,
        out_specs=(VMEM,) * 3,
        scratch_shapes=[pltpu.SemaphoreType.DMA((2,))],
        compiler_params=params,
        name="product",
    )(rows.reshape(1, k_tiles), slots, tiles_kept, *exchanged_along_row(wanted), flag, *dual_side)
    dual_next, too_many = pl.pallas_call(
        functools.partial(dual_kernel, n_col),
        out_shape=(jax.ShapeDtypeStruct((row_blocks, TILE), f32), jax.ShapeDtypeStruct((1,), i32)),
        in_specs=[VMEM] * (n_col + 3) + [SMEM],
        out_specs=(VMEM, SMEM),
        compiler_params=params,
        name="dual_step",
    )(*gathered_along(row_terms, "col"), duals_kept, *dual_kept, step_sizes)
    vectors = (primal, duals, cost_vec, lower_bound, upper_bound, bound_kind, right_side, row_kind, step_sizes)
    return lax.cond(
        too_many[0] > 0,
        lambda done: full_step(tiles, rows, cols, *vectors),
        lambda done: done,
        (primal_next.reshape(-1), dual_next.reshape(-1)),
    )


def solution(mesh):
    return jax.shard_map(
        local,
        mesh=mesh,
        in_specs=(
            P("row", "col", None, None, None),
            P("row", "col", None),
            P("row", "col", None),
            P(("col", "row")),
            P("row"),
            P(("col", "row")),
            P(("col", "row")),
            P(("col", "row")),
            P(("col", "row")),
            P("row"),
            P("row"),
            P(),
        ),
        out_specs=(P(("col", "row")), P("row")),
        check_vma=False,
    )
```

```python
import functools
import jax
import jax.numpy as jnp
from jax import lax
from jax.experimental import pallas as pl
from jax.experimental.pallas import tpu as pltpu
from jax.sharding import PartitionSpec as P

TILE = 128
GROUP = 16
CHUNK = 32
SLOTS = 48
HEAD = 16
BITS = 14

f32 = jnp.float32
bf16 = jnp.bfloat16
i32 = jnp.int32
i16 = jnp.int16
VMEM = pl.BlockSpec(memory_space=pltpu.VMEM)
SMEM = pl.BlockSpec(memory_space=pltpu.SMEM)
HBM = pl.BlockSpec(memory_space=pltpu.HBM)


def iota(shape, axis):
    return lax.broadcasted_iota(i32, shape, axis)


def where_one(condition):
    return jnp.where(condition, 1.0, 0.0)


def one_row_of(block, position):
    return jnp.where(iota(block.shape, 0) == position, block, 0.0).astype(bf16)


def rounds_of(n_row):
    chunks = n_row * SLOTS // TILE
    return chunks, -(-(2 * chunks + 1) // 8) * 8


def coded(values):
    largest = jnp.maximum(jnp.max(jnp.abs(values), axis=1, keepdims=True), 1e-30)
    exponent = jnp.ceil(jnp.log2(largest))
    whole = jnp.floor(values * jnp.exp2(BITS - exponent) + 0.5).astype(i32)
    return whole, jnp.broadcast_to(exponent, values.shape)


def two_parts(whole):
    low = jnp.bitwise_and(whole, 255)
    parts = [(whole - low).astype(f32), low.astype(f32)]
    return jnp.concatenate(parts, axis=1).astype(bf16)


def picked_sums(masks, wholes):
    left = masks[0] if len(masks) == 1 else jnp.concatenate(masks, axis=1)
    both = jnp.dot(
        left.astype(bf16),
        jnp.concatenate([two_parts(w) for w in wholes], axis=0),
        preferred_element_type=f32,
    )
    return both[:, :TILE] + both[:, TILE:]


def scaled_mask(down, places, exponents):
    return jnp.where(down == places, jnp.exp2(exponents.astype(f32) - BITS), 0.0)


def started(sources, targets, sems):
    copies = [
        pltpu.make_async_copy(source, target, sems.at[n])
        for n, (source, target) in enumerate(zip(sources, targets))
    ]
    for copy in copies:
        copy.start()
    return copies


def transpose_product_kernel(owned, *refs):
    (rows_hbm, cols_hbm, duals_hbm, tiles_hbm), (out_ref, slot_ref, duals, tiles), refs = refs[:4], refs[4:8], refs[8:]
    rows, cols, picked, terms, small_sems, tile_sems = refs
    n_row = out_ref.shape[0]
    chunks, head_rows = rounds_of(n_row)
    most = SLOTS - head_rows
    k_tiles = tiles.shape[0]
    groups = [pl.ds(g * CHUNK, CHUNK) for g in range(k_tiles // CHUNK)]
    small = started([cols_hbm, rows_hbm, duals_hbm], [cols, rows, duals], small_sems)
    large = started([tiles_hbm.at[g] for g in groups], [tiles.at[g] for g in groups], tile_sems)

    small[0].wait()
    square = (k_tiles, k_tiles)
    col_across = cols[...]
    col_down = jnp.transpose(jnp.broadcast_to(col_across.astype(f32), square)).astype(i32)
    owner_across = sum((col_across >= o * owned).astype(i32) for o in range(1, n_row))
    owner_down = sum((col_down >= o * owned).astype(i32) for o in range(1, n_row))
    same = owner_down == owner_across
    earlier_down = iota(square, 0) < iota(square, 1)
    earlier_across = iota(square, 1) < iota(square, 0)
    rank_across = jnp.sum(where_one(same & earlier_down), axis=0, keepdims=True).astype(i32)
    rank_down = jnp.sum(where_one(same & earlier_across), axis=1, keepdims=True).astype(i32)
    slot_across = jnp.where(rank_across < most, owner_across * SLOTS + head_rows + rank_across, -1)
    slot_down = jnp.where(rank_down < most, owner_down * SLOTS + head_rows + rank_down, -1)
    slot_ref[...] = slot_down
    too_many = where_one(jnp.max(rank_across, axis=1, keepdims=True) >= most)
    to_slots = where_one(iota((n_row * SLOTS, k_tiles), 0) == slot_across)
    here = jnp.where(rank_down < most, lax.axis_index("row") * SLOTS + head_rows + rank_down, -1)
    to_lanes = where_one(iota((k_tiles, n_row * SLOTS), 1) == here)
    of_owner = where_one(iota((n_row, k_tiles), 0) == owner_across)
    place = col_across - owner_across * owned + 1
    place_low = jnp.bitwise_and(place, 255)
    head_left = jnp.concatenate(
        [of_owner * (place - place_low).astype(f32), of_owner * place_low.astype(f32), of_owner], axis=0
    ).astype(bf16)

    for copy in small[1:]:
        copy.wait()
    for k in range(k_tiles):
        picked[pl.ds(k, 1), :] = duals[pl.ds(rows[k], 1), :]
    for g, copy in enumerate(large):
        copy.wait()
        for first in range(g * CHUNK, (g + 1) * CHUNK, GROUP):
            group = pl.ds(first, GROUP)
            block = picked[group, :].astype(bf16).astype(f32)
            left = jnp.concatenate([one_row_of(block, m) for m in range(GROUP)], axis=1)
            terms[group, :] = jnp.dot(
                left, tiles[group].reshape(GROUP * TILE, TILE), preferred_element_type=f32
            )
    whole, exponents = coded(terms[...])

    scaled = [to_lanes, to_lanes * jnp.concatenate([exponents] * chunks, axis=1)]
    heads = jnp.dot(head_left, jnp.concatenate(scaled, axis=1).astype(bf16), preferred_element_type=f32)
    width = n_row * SLOTS
    places = heads[:n_row, :width] + heads[n_row : 2 * n_row, :width]
    scales = heads[2 * n_row :, width:]
    both = jnp.dot(to_slots.astype(bf16), two_parts(whole), preferred_element_type=f32)
    body = both[:, :TILE] + both[:, TILE:]
    line = iota((head_rows, TILE), 0)
    for o in range(n_row):
        head = jnp.where(line == 2 * chunks, too_many, 0.0)
        for c in range(chunks):
            lanes = slice(c * TILE, (c + 1) * TILE)
            head = jnp.where(line == c, places[o : o + 1, lanes], head)
            head = jnp.where(line == chunks + c, scales[o : o + 1, lanes], head)
        rows_of = body[o * SLOTS + head_rows : (o + 1) * SLOTS]
        out_ref[o] = jnp.concatenate([head, rows_of], axis=0).astype(i32).astype(i16)


def primal_kernel(
    payloads, primal_ref, cost_ref, lower_ref, upper_ref, kind_ref, steps_ref, next_hbm, flag_ref, *refs
):
    wanted, (next_ref, extrap, in_order, sem) = refs[:-4], refs[-4:]
    me = lax.axis_index("row")
    n_row = payloads.shape[0]
    chunks, head_rows = rounds_of(n_row)
    blocks = primal_ref.shape[0]
    padded = extrap.shape[0]
    head = jnp.zeros((head_rows, TILE), f32)
    for s in range(n_row):
        head += payloads[s].astype(i32)[:head_rows].astype(f32)
    flag_ref[...] = jnp.broadcast_to(head[2 * chunks : 2 * chunks + 1], flag_ref.shape)
    whole = payloads[...].reshape(n_row * SLOTS, TILE).astype(i32)
    down = iota((blocks, TILE), 0) + 1
    head_whole = head.astype(i32)
    masks, wholes = [], []
    for c in range(chunks):
        masks.append(scaled_mask(down, head_whole[c : c + 1], head_whole[chunks + c : chunks + c + 1]))
        wholes.append(whole[c * TILE : (c + 1) * TILE])
    col_sums = picked_sums(masks, wholes)
    primal = primal_ref[...]
    kind = kind_ref[...]
    moved = primal - steps_ref[0] * (cost_ref[...] - col_sums)
    moved = jnp.where(kind % 2 == 1, jnp.maximum(moved, lower_ref[...]), moved)
    moved = jnp.where(kind >= 2, jnp.minimum(moved, upper_ref[...]), moved)
    next_ref[...] = moved
    copy = pltpu.make_async_copy(next_ref, next_hbm, sem)
    copy.start()
    aligned = blocks // 8 * 8
    if padded > aligned:
        extrap[pl.ds(aligned, padded - aligned), :] = jnp.zeros((padded - aligned, TILE), f32)
    extrap[pl.ds(0, blocks), :] = 2.0 * moved - primal
    right = extrap[...].astype(bf16)
    across = iota((TILE, padded), 1) + 1
    places = jnp.transpose(head).astype(i32)
    sent = [
        jnp.dot(where_one(across == places[:, c : c + 1]).astype(bf16), right, preferred_element_type=f32)
        for c in range(chunks)
    ]
    in_order[...] = jnp.concatenate(sent, axis=0).astype(bf16).reshape(in_order.shape)
    for n, target in enumerate(wanted):
        target[...] = in_order[place_of(me, n, n_row, back=True)]
    copy.wait()


def product_kernel(*refs):
    (rows_ref, slot_ref, tiles_ref, flag_ref), others_hbm, refs = refs[:4], refs[4:6], refs[6:]
    arrived, (out_ref, *others, in_order, sems) = refs[:-5], refs[-5:]
    me = lax.axis_index("row")
    for n, source in enumerate(arrived):
        in_order[place_of(me, n, len(arrived), back=False)] = source[...]
    later = started(others_hbm, others, sems)
    k_tiles = tiles_ref.shape[0]
    received = in_order[...].reshape(-1, TILE)
    across = iota((k_tiles, received.shape[0]), 1)
    slots = jnp.concatenate([slot_ref[...]] * (received.shape[0] // TILE), axis=1)
    block = jnp.dot(where_one(across == slots).astype(bf16), received, preferred_element_type=f32)
    down = jnp.transpose(block)
    lane = iota((TILE, k_tiles), 1)
    right = jnp.concatenate(
        [jnp.where(lane % 2 == 0, down, 0.0), jnp.where(lane % 2 == 1, down, 0.0)], axis=0
    ).astype(bf16)
    terms = jnp.zeros((TILE, k_tiles), f32)
    for g in range(k_tiles // 8):
        even = jnp.concatenate([tiles_ref[8 * g + m] for m in (0, 2, 4, 6)], axis=0)
        odd = jnp.concatenate([tiles_ref[8 * g + m] for m in (1, 3, 5, 7)], axis=0)
        products = jnp.dot(jnp.concatenate([even, odd], axis=1), right, preferred_element_type=f32)
        for p in range(4):
            terms = jnp.where(lane // 2 == 4 * g + p, products[p * TILE : (p + 1) * TILE], terms)
    whole, exponents = coded(jnp.transpose(terms))
    out_ref[pl.ds(0, k_tiles), :] = whole.astype(i16)
    line = iota((HEAD, TILE), 0)
    head = jnp.where(line == 0, rows_ref[...], jnp.transpose(exponents)[0:HEAD, :].astype(i32))
    head = jnp.where(line == 2, flag_ref[0:1, :].astype(i32), head)
    out_ref[pl.ds(k_tiles, HEAD), :] = head.astype(i16)
    for copy in later:
        copy.wait()


def dual_kernel(n_col, *refs):
    payloads, (duals_ref, right_ref, kind_ref, steps_ref, next_ref, flag_ref) = refs[:n_col], refs[n_col:]
    k_tiles = payloads[0].shape[0] - HEAD
    down = iota((duals_ref.shape[0], k_tiles), 0)
    masks, wholes = [], []
    flags = jnp.zeros((1, TILE), i32)
    for payload in payloads:
        head = payload[pl.ds(k_tiles, HEAD), :].astype(i32)
        masks.append(scaled_mask(down, head[0:1], head[1:2]))
        wholes.append(payload[pl.ds(0, k_tiles), :].astype(i32))
        flags += head[2:3]
    row_sums = picked_sums(masks, wholes)
    updated = duals_ref[...] + steps_ref[1] * (right_ref[...] - row_sums)
    next_ref[...] = jnp.where(kind_ref[...] == 1, jnp.maximum(updated, 0.0), updated)
    flag_ref[0] = jnp.max(flags)


def place_of(me, n, size, back):
    if size & (size - 1) == 0:
        return jnp.bitwise_xor(me, n)
    return lax.rem(me + (size - n if back else n), size)


def partners(axis):
    size = lax.axis_size(axis)
    if size & (size - 1) == 0:
        there = [[(i, i ^ n) for i in range(size)] for n in range(1, size)]
    else:
        there = [[(i, (i + n) % size) for i in range(size)] for n in range(1, size)]
    return [(pairs, [(j, i) for i, j in pairs]) for pairs in there]


def gathered_along(array, axis):
    return [array] + [lax.ppermute(array, axis, there) for there, _ in partners(axis)]


def sums_at(places, terms, blocks):
    mask = (jnp.arange(blocks)[:, None] == jnp.concatenate(places)[None, :]).astype(f32)
    return jnp.dot(mask, jnp.concatenate(terms), precision=lax.Precision.HIGHEST).reshape(-1)


def full_step(
    tiles, rows, cols, primal, duals, cost_vec, lower_bound, upper_bound, bound_kind, right_side, row_kind, steps
):
    col_blocks = primal.shape[0] // TILE
    row_blocks = duals.shape[0] // TILE
    wide = tiles.astype(f32)
    dual_blocks = duals.astype(bf16).astype(f32).reshape(row_blocks, TILE)[rows]
    col_terms = jnp.einsum("kij,ki->kj", wide, dual_blocks)
    first = lax.axis_index("row") * col_blocks
    places = [there - first for there in gathered_along(cols, "row")]
    places = [jnp.where((p >= 0) & (p < col_blocks), p, col_blocks) for p in places]
    col_sums = sums_at(places, gathered_along(col_terms, "row"), col_blocks)
    moved = primal - steps[0] * (cost_vec - col_sums)
    moved = jnp.where(bound_kind % 2 == 1, jnp.maximum(moved, lower_bound), moved)
    moved = jnp.where(bound_kind >= 2, jnp.minimum(moved, upper_bound), moved)
    extrap = (2.0 * moved - primal).astype(bf16).reshape(col_blocks, TILE)
    wanted = [
        jnp.where((p < col_blocks)[:, None], extrap[jnp.minimum(p, col_blocks - 1)], jnp.zeros((), bf16))
        for p in places
    ]
    blocks = wanted[0].astype(f32)
    for block, (_, back) in zip(wanted[1:], partners("row")):
        blocks += lax.ppermute(block, "row", back).astype(f32)
    row_terms = jnp.einsum("kij,kj->ki", wide, blocks)
    row_sums = sums_at(gathered_along(rows, "col"), gathered_along(row_terms, "col"), row_blocks)
    updated = duals + steps[1] * (right_side - row_sums)
    return moved, jnp.where(row_kind == 1, jnp.maximum(updated, 0.0), updated)


def local(
    block_tiles,
    tile_row,
    tile_col,
    primal,
    duals,
    cost_vec,
    lower_bound,
    upper_bound,
    bound_kind,
    right_side,
    row_kind,
    step_sizes,
):
    k_tiles = block_tiles.shape[2]
    tiles = block_tiles.reshape(k_tiles, TILE, TILE)
    rows = tile_row.reshape(-1)
    cols = tile_col.reshape(-1)
    n_row = lax.axis_size("row")
    n_col = lax.axis_size("col")
    col_blocks = primal.shape[0] // TILE
    row_blocks = duals.shape[0] // TILE
    padded = -(-col_blocks // TILE) * TILE
    in_hbm = lambda array: pltpu.with_memory_space_constraint(array, pltpu.HBM)
    by_block = lambda array: in_hbm(array.reshape(-1, TILE))
    shape_of = lambda array: jax.ShapeDtypeStruct(array.shape, array.dtype)
    params = pltpu.CompilerParams(vmem_limit_bytes=32 * 1024 * 1024)
    primal_side = [a.reshape(-1, TILE) for a in (primal, cost_vec, lower_bound, upper_bound, bound_kind)]
    dual_side = [by_block(a) for a in (right_side, row_kind)]
    own = [by_block(duals), in_hbm(tiles)]

    col_terms, slots, duals_kept, tiles_kept = pl.pallas_call(
        functools.partial(transpose_product_kernel, col_blocks),
        out_shape=(
            jax.ShapeDtypeStruct((n_row, SLOTS, TILE), i16),
            jax.ShapeDtypeStruct((k_tiles, TILE), i32),
            *[shape_of(a) for a in own],
        ),
        in_specs=[HBM] * 4,
        out_specs=(VMEM,) * 4,
        scratch_shapes=[
            pltpu.SMEM((k_tiles,), i32),
            pltpu.VMEM((1, k_tiles), i32),
            pltpu.VMEM((k_tiles, TILE), f32),
            pltpu.VMEM((k_tiles, TILE), f32),
            pltpu.SemaphoreType.DMA((3,)),
            pltpu.SemaphoreType.DMA((k_tiles // CHUNK,)),
        ],
        compiler_params=params,
        name="transpose_product",
    )(in_hbm(rows), in_hbm(cols.reshape(1, k_tiles)), *own)
    primal_next, flag, *wanted = pl.pallas_call(
        primal_kernel,
        out_shape=(
            jax.ShapeDtypeStruct((col_blocks, TILE), f32),
            jax.ShapeDtypeStruct((8, TILE), f32),
            *[jax.ShapeDtypeStruct((SLOTS, TILE), bf16)] * n_row,
        ),
        in_specs=[VMEM] * 6 + [SMEM],
        out_specs=(HBM, *[VMEM] * (n_row + 1)),
        scratch_shapes=[
            pltpu.VMEM((col_blocks, TILE), f32),
            pltpu.VMEM((padded, TILE), f32),
            pltpu.VMEM((n_row, SLOTS, TILE), bf16),
            pltpu.SemaphoreType.DMA,
        ],
        compiler_params=params,
        name="primal_step",
    )(lax.all_to_all(col_terms, "row", 0, 0), *primal_side, step_sizes)
    row_terms, *dual_kept = pl.pallas_call(
        product_kernel,
        out_shape=(
            jax.ShapeDtypeStruct((k_tiles + HEAD, TILE), i16),
            *[shape_of(a) for a in dual_side],
        ),
        in_specs=[VMEM] * 4 + [HBM] * 2 + [VMEM] * n_row,
        out_specs=(VMEM,) * 3,
        scratch_shapes=[pltpu.VMEM((n_row, SLOTS, TILE), bf16), pltpu.SemaphoreType.DMA((2,))],
        compiler_params=params,
        name="product",
    )(
        rows.reshape(1, k_tiles),
        slots,
        tiles_kept,
        flag,
        *dual_side,
        wanted[0],
        *[lax.ppermute(w, "row", back) for w, (_, back) in zip(wanted[1:], partners("row"))],
    )
    dual_next, too_many = pl.pallas_call(
        functools.partial(dual_kernel, n_col),
        out_shape=(jax.ShapeDtypeStruct((row_blocks, TILE), f32), jax.ShapeDtypeStruct((1,), i32)),
        in_specs=[VMEM] * (n_col + 3) + [SMEM],
        out_specs=(VMEM, SMEM),
        compiler_params=params,
        name="dual_step",
    )(*gathered_along(row_terms, "col"), duals_kept, *dual_kept, step_sizes)
    vectors = (primal, duals, cost_vec, lower_bound, upper_bound, bound_kind, right_side, row_kind, step_sizes)
    return lax.cond(
        too_many[0] > 0,
        lambda done: full_step(tiles, rows, cols, *vectors),
        lambda done: done,
        (primal_next.reshape(-1), dual_next.reshape(-1)),
    )


def solution(mesh):
    return jax.shard_map(
        local,
        mesh=mesh,
        in_specs=(
            P("row", "col", None, None, None),
            P("row", "col", None),
            P("row", "col", None),
            P(("col", "row")),
            P("row"),
            P(("col", "row")),
            P(("col", "row")),
            P(("col", "row")),
            P(("col", "row")),
            P("row"),
            P("row"),
            P(),
        ),
        out_specs=(P(("col", "row")), P("row")),
        check_vma=False,
    )
```

```python
import functools
import jax
import jax.numpy as jnp
from jax import lax
from jax.experimental import pallas as pl
from jax.experimental.pallas import tpu as pltpu
from jax.sharding import PartitionSpec as P

TILE = 128
GROUP = 16
CHUNK = 32
SLOTS = 48
HEAD = 16
BITS = 14

f32 = jnp.float32
bf16 = jnp.bfloat16
i32 = jnp.int32
i16 = jnp.int16
VMEM = pl.BlockSpec(memory_space=pltpu.VMEM)
SMEM = pl.BlockSpec(memory_space=pltpu.SMEM)
HBM = pl.BlockSpec(memory_space=pltpu.HBM)


def iota(shape, axis):
    return lax.broadcasted_iota(i32, shape, axis)


def where_one(condition):
    return jnp.where(condition, 1.0, 0.0)


def one_row_of(block, position):
    return jnp.where(iota(block.shape, 0) == position, block, 0.0).astype(bf16)


def rounds_of(n_row):
    chunks = n_row * SLOTS // TILE
    return chunks, -(-(2 * chunks + 1) // 8) * 8


def coded(values):
    largest = jnp.maximum(jnp.max(jnp.abs(values), axis=1, keepdims=True), 1e-30)
    exponent = jnp.ceil(jnp.log2(largest))
    whole = jnp.floor(values * jnp.exp2(BITS - exponent) + 0.5).astype(i32)
    return whole, jnp.broadcast_to(exponent, values.shape)


def two_parts(whole):
    low = jnp.bitwise_and(whole, 255)
    parts = [(whole - low).astype(f32), low.astype(f32)]
    return jnp.concatenate(parts, axis=1).astype(bf16)


def picked_sums(masks, wholes):
    left = masks[0] if len(masks) == 1 else jnp.concatenate(masks, axis=1)
    both = jnp.dot(
        left.astype(bf16),
        jnp.concatenate([two_parts(w) for w in wholes], axis=0),
        preferred_element_type=f32,
    )
    return both[:, :TILE] + both[:, TILE:]


def scaled_mask(down, places, exponents):
    return jnp.where(down == places, jnp.exp2(exponents.astype(f32) - BITS), 0.0)


def started(sources, targets, sems):
    copies = [
        pltpu.make_async_copy(source, target, sems.at[n])
        for n, (source, target) in enumerate(zip(sources, targets))
    ]
    for copy in copies:
        copy.start()
    return copies


def transpose_product_kernel(owned, *refs):
    (rows_hbm, cols_hbm, duals_hbm, tiles_hbm), (out_ref, slot_ref, duals, tiles), refs = refs[:4], refs[4:8], refs[8:]
    rows, cols, picked, terms, small_sems, tile_sems = refs
    n_row = out_ref.shape[0]
    chunks, head_rows = rounds_of(n_row)
    most = SLOTS - head_rows
    k_tiles = tiles.shape[0]
    groups = [pl.ds(g * CHUNK, CHUNK) for g in range(k_tiles // CHUNK)]
    small = started([cols_hbm, rows_hbm, duals_hbm], [cols, rows, duals], small_sems)
    large = started([tiles_hbm.at[g] for g in groups], [tiles.at[g] for g in groups], tile_sems)

    for copy in small:
        copy.wait()
    for k in range(k_tiles):
        picked[pl.ds(k, 1), :] = duals[pl.ds(rows[k], 1), :]

    def products_of(chunk):
        large[chunk].wait()
        for first in range(chunk * CHUNK, (chunk + 1) * CHUNK, GROUP):
            group = pl.ds(first, GROUP)
            block = picked[group, :].astype(bf16).astype(f32)
            left = jnp.concatenate([one_row_of(block, m) for m in range(GROUP)], axis=1)
            terms[group, :] = jnp.dot(
                left, tiles[group].reshape(GROUP * TILE, TILE), preferred_element_type=f32
            )

    products_of(0)

    square = (k_tiles, k_tiles)
    col_across = cols[...]
    col_down = jnp.transpose(jnp.broadcast_to(col_across.astype(f32), square)).astype(i32)
    owner_across = sum((col_across >= o * owned).astype(i32) for o in range(1, n_row))
    owner_down = sum((col_down >= o * owned).astype(i32) for o in range(1, n_row))
    same = owner_down == owner_across
    earlier_down = iota(square, 0) < iota(square, 1)
    earlier_across = iota(square, 1) < iota(square, 0)
    rank_across = jnp.sum(where_one(same & earlier_down), axis=0, keepdims=True).astype(i32)
    rank_down = jnp.sum(where_one(same & earlier_across), axis=1, keepdims=True).astype(i32)
    slot_across = jnp.where(rank_across < most, owner_across * SLOTS + head_rows + rank_across, -1)
    slot_down = jnp.where(rank_down < most, owner_down * SLOTS + head_rows + rank_down, -1)
    slot_ref[...] = slot_down
    too_many = where_one(jnp.max(rank_across, axis=1, keepdims=True) >= most)
    to_slots = where_one(iota((n_row * SLOTS, k_tiles), 0) == slot_across)
    here = jnp.where(rank_down < most, lax.axis_index("row") * SLOTS + head_rows + rank_down, -1)
    to_lanes = where_one(iota((k_tiles, n_row * SLOTS), 1) == here)
    of_owner = where_one(iota((n_row, k_tiles), 0) == owner_across)
    place = col_across - owner_across * owned + 1
    place_low = jnp.bitwise_and(place, 255)
    head_left = jnp.concatenate(
        [of_owner * (place - place_low).astype(f32), of_owner * place_low.astype(f32), of_owner], axis=0
    ).astype(bf16)

    for chunk in range(1, len(large)):
        products_of(chunk)
    whole, exponents = coded(terms[...])

    scaled = [to_lanes, to_lanes * jnp.concatenate([exponents] * chunks, axis=1)]
    heads = jnp.dot(head_left, jnp.concatenate(scaled, axis=1).astype(bf16), preferred_element_type=f32)
    width = n_row * SLOTS
    places = heads[:n_row, :width] + heads[n_row : 2 * n_row, :width]
    scales = heads[2 * n_row :, width:]
    both = jnp.dot(to_slots.astype(bf16), two_parts(whole), preferred_element_type=f32)
    body = both[:, :TILE] + both[:, TILE:]
    line = iota((head_rows, TILE), 0)
    for o in range(n_row):
        head = jnp.where(line == 2 * chunks, too_many, 0.0)
        for c in range(chunks):
            lanes = slice(c * TILE, (c + 1) * TILE)
            head = jnp.where(line == c, places[o : o + 1, lanes], head)
            head = jnp.where(line == chunks + c, scales[o : o + 1, lanes], head)
        rows_of = body[o * SLOTS + head_rows : (o + 1) * SLOTS]
        out_ref[o] = jnp.concatenate([head, rows_of], axis=0).astype(i32).astype(i16)


def primal_kernel(
    payloads, primal_ref, cost_ref, lower_ref, upper_ref, kind_ref, steps_ref, next_hbm, flag_ref, *refs
):
    wanted, next_ref, extrap, sem = refs
    n_row = payloads.shape[0]
    chunks, head_rows = rounds_of(n_row)
    blocks = primal_ref.shape[0]
    padded = extrap.shape[0]
    head = jnp.zeros((head_rows, TILE), f32)
    for s in range(n_row):
        head += payloads[s].astype(i32)[:head_rows].astype(f32)
    flag_ref[...] = jnp.broadcast_to(head[2 * chunks : 2 * chunks + 1], flag_ref.shape)
    whole = payloads[...].reshape(n_row * SLOTS, TILE).astype(i32)
    down = iota((blocks, TILE), 0) + 1
    head_whole = head.astype(i32)
    masks, wholes = [], []
    for c in range(chunks):
        masks.append(scaled_mask(down, head_whole[c : c + 1], head_whole[chunks + c : chunks + c + 1]))
        wholes.append(whole[c * TILE : (c + 1) * TILE])
    col_sums = picked_sums(masks, wholes)
    primal = primal_ref[...]
    kind = kind_ref[...]
    moved = primal - steps_ref[0] * (cost_ref[...] - col_sums)
    moved = jnp.where(kind % 2 == 1, jnp.maximum(moved, lower_ref[...]), moved)
    moved = jnp.where(kind >= 2, jnp.minimum(moved, upper_ref[...]), moved)
    next_ref[...] = moved
    copy = pltpu.make_async_copy(next_ref, next_hbm, sem)
    copy.start()
    aligned = blocks // 8 * 8
    if padded > aligned:
        extrap[pl.ds(aligned, padded - aligned), :] = jnp.zeros((padded - aligned, TILE), f32)
    extrap[pl.ds(0, blocks), :] = 2.0 * moved - primal
    right = extrap[...].astype(bf16)
    across = iota((TILE, padded), 1) + 1
    places = jnp.transpose(head).astype(i32)
    sent = [
        jnp.dot(where_one(across == places[:, c : c + 1]).astype(bf16), right, preferred_element_type=f32)
        for c in range(chunks)
    ]
    wanted[...] = jnp.concatenate(sent, axis=0).astype(bf16).reshape(wanted.shape)
    copy.wait()


def product_kernel(*refs):
    (rows_ref, slot_ref, tiles_ref, arrived, flag_ref), others_hbm, refs = refs[:5], refs[5:7], refs[7:]
    out_ref, others, sems = refs[0], refs[1:3], refs[3]
    later = started(others_hbm, others, sems)
    k_tiles = tiles_ref.shape[0]
    received = arrived[...].reshape(-1, TILE)
    across = iota((k_tiles, received.shape[0]), 1)
    slots = jnp.concatenate([slot_ref[...]] * (received.shape[0] // TILE), axis=1)
    block = jnp.dot(where_one(across == slots).astype(bf16), received, preferred_element_type=f32)
    down = jnp.transpose(block)
    lane = iota((TILE, k_tiles), 1)
    right = jnp.concatenate(
        [jnp.where(lane % 2 == 0, down, 0.0), jnp.where(lane % 2 == 1, down, 0.0)], axis=0
    ).astype(bf16)
    terms = jnp.zeros((TILE, k_tiles), f32)
    for g in range(k_tiles // 8):
        even = jnp.concatenate([tiles_ref[8 * g + m] for m in (0, 2, 4, 6)], axis=0)
        odd = jnp.concatenate([tiles_ref[8 * g + m] for m in (1, 3, 5, 7)], axis=0)
        products = jnp.dot(jnp.concatenate([even, odd], axis=1), right, preferred_element_type=f32)
        for p in range(4):
            terms = jnp.where(lane // 2 == 4 * g + p, products[p * TILE : (p + 1) * TILE], terms)
    whole, exponents = coded(jnp.transpose(terms))
    out_ref[pl.ds(0, k_tiles), :] = whole.astype(i16)
    line = iota((HEAD, TILE), 0)
    head = jnp.where(line == 0, rows_ref[...], jnp.transpose(exponents)[0:HEAD, :].astype(i32))
    head = jnp.where(line == 2, flag_ref[0:1, :].astype(i32), head)
    out_ref[pl.ds(k_tiles, HEAD), :] = head.astype(i16)
    for copy in later:
        copy.wait()


def dual_kernel(n_col, *refs):
    payloads, (duals_ref, right_ref, kind_ref, steps_ref, next_ref, flag_ref) = refs[:n_col], refs[n_col:]
    k_tiles = payloads[0].shape[0] - HEAD
    down = iota((duals_ref.shape[0], k_tiles), 0)
    masks, wholes = [], []
    flags = jnp.zeros((1, TILE), i32)
    for payload in payloads:
        head = payload[pl.ds(k_tiles, HEAD), :].astype(i32)
        masks.append(scaled_mask(down, head[0:1], head[1:2]))
        wholes.append(payload[pl.ds(0, k_tiles), :].astype(i32))
        flags += head[2:3]
    row_sums = picked_sums(masks, wholes)
    updated = duals_ref[...] + steps_ref[1] * (right_ref[...] - row_sums)
    next_ref[...] = jnp.where(kind_ref[...] == 1, jnp.maximum(updated, 0.0), updated)
    flag_ref[0] = jnp.max(flags)


def partners(axis):
    size = lax.axis_size(axis)
    if size & (size - 1) == 0:
        there = [[(i, i ^ n) for i in range(size)] for n in range(1, size)]
    else:
        there = [[(i, (i + n) % size) for i in range(size)] for n in range(1, size)]
    return [(pairs, [(j, i) for i, j in pairs]) for pairs in there]


def gathered_along(array, axis):
    return [array] + [lax.ppermute(array, axis, there) for there, _ in partners(axis)]


def sums_at(places, terms, blocks):
    mask = (jnp.arange(blocks)[:, None] == jnp.concatenate(places)[None, :]).astype(f32)
    return jnp.dot(mask, jnp.concatenate(terms), precision=lax.Precision.HIGHEST).reshape(-1)


def full_step(
    tiles, rows, cols, primal, duals, cost_vec, lower_bound, upper_bound, bound_kind, right_side, row_kind, steps
):
    col_blocks = primal.shape[0] // TILE
    row_blocks = duals.shape[0] // TILE
    wide = tiles.astype(f32)
    dual_blocks = duals.astype(bf16).astype(f32).reshape(row_blocks, TILE)[rows]
    col_terms = jnp.einsum("kij,ki->kj", wide, dual_blocks)
    first = lax.axis_index("row") * col_blocks
    places = [there - first for there in gathered_along(cols, "row")]
    places = [jnp.where((p >= 0) & (p < col_blocks), p, col_blocks) for p in places]
    col_sums = sums_at(places, gathered_along(col_terms, "row"), col_blocks)
    moved = primal - steps[0] * (cost_vec - col_sums)
    moved = jnp.where(bound_kind % 2 == 1, jnp.maximum(moved, lower_bound), moved)
    moved = jnp.where(bound_kind >= 2, jnp.minimum(moved, upper_bound), moved)
    extrap = (2.0 * moved - primal).astype(bf16).reshape(col_blocks, TILE)
    wanted = [
        jnp.where((p < col_blocks)[:, None], extrap[jnp.minimum(p, col_blocks - 1)], jnp.zeros((), bf16))
        for p in places
    ]
    blocks = wanted[0].astype(f32)
    for block, (_, back) in zip(wanted[1:], partners("row")):
        blocks += lax.ppermute(block, "row", back).astype(f32)
    row_terms = jnp.einsum("kij,kj->ki", wide, blocks)
    row_sums = sums_at(gathered_along(rows, "col"), gathered_along(row_terms, "col"), row_blocks)
    updated = duals + steps[1] * (right_side - row_sums)
    return moved, jnp.where(row_kind == 1, jnp.maximum(updated, 0.0), updated)


def local(
    block_tiles,
    tile_row,
    tile_col,
    primal,
    duals,
    cost_vec,
    lower_bound,
    upper_bound,
    bound_kind,
    right_side,
    row_kind,
    step_sizes,
):
    k_tiles = block_tiles.shape[2]
    tiles = block_tiles.reshape(k_tiles, TILE, TILE)
    rows = tile_row.reshape(-1)
    cols = tile_col.reshape(-1)
    n_row = lax.axis_size("row")
    n_col = lax.axis_size("col")
    col_blocks = primal.shape[0] // TILE
    row_blocks = duals.shape[0] // TILE
    padded = -(-col_blocks // TILE) * TILE
    in_hbm = lambda array: pltpu.with_memory_space_constraint(array, pltpu.HBM)
    by_block = lambda array: in_hbm(array.reshape(-1, TILE))
    shape_of = lambda array: jax.ShapeDtypeStruct(array.shape, array.dtype)
    params = pltpu.CompilerParams(vmem_limit_bytes=32 * 1024 * 1024)
    primal_side = [a.reshape(-1, TILE) for a in (primal, cost_vec, lower_bound, upper_bound, bound_kind)]
    dual_side = [by_block(a) for a in (right_side, row_kind)]
    own = [by_block(duals), in_hbm(tiles)]

    col_terms, slots, duals_kept, tiles_kept = pl.pallas_call(
        functools.partial(transpose_product_kernel, col_blocks),
        out_shape=(
            jax.ShapeDtypeStruct((n_row, SLOTS, TILE), i16),
            jax.ShapeDtypeStruct((k_tiles, TILE), i32),
            *[shape_of(a) for a in own],
        ),
        in_specs=[HBM] * 4,
        out_specs=(VMEM,) * 4,
        scratch_shapes=[
            pltpu.SMEM((k_tiles,), i32),
            pltpu.VMEM((1, k_tiles), i32),
            pltpu.VMEM((k_tiles, TILE), f32),
            pltpu.VMEM((k_tiles, TILE), f32),
            pltpu.SemaphoreType.DMA((3,)),
            pltpu.SemaphoreType.DMA((k_tiles // CHUNK,)),
        ],
        compiler_params=params,
        name="transpose_product",
    )(in_hbm(rows), in_hbm(cols.reshape(1, k_tiles)), *own)
    primal_next, flag, wanted = pl.pallas_call(
        primal_kernel,
        out_shape=(
            jax.ShapeDtypeStruct((col_blocks, TILE), f32),
            jax.ShapeDtypeStruct((8, TILE), f32),
            jax.ShapeDtypeStruct((n_row, SLOTS, TILE), bf16),
        ),
        in_specs=[VMEM] * 6 + [SMEM],
        out_specs=(HBM, VMEM, VMEM),
        scratch_shapes=[
            pltpu.VMEM((col_blocks, TILE), f32),
            pltpu.VMEM((padded, TILE), f32),
            pltpu.SemaphoreType.DMA,
        ],
        compiler_params=params,
        name="primal_step",
    )(lax.all_to_all(col_terms, "row", 0, 0), *primal_side, step_sizes)
    row_terms, *dual_kept = pl.pallas_call(
        product_kernel,
        out_shape=(
            jax.ShapeDtypeStruct((k_tiles + HEAD, TILE), i16),
            *[shape_of(a) for a in dual_side],
        ),
        in_specs=[VMEM] * 5 + [HBM] * 2,
        out_specs=(VMEM,) * 3,
        scratch_shapes=[pltpu.SemaphoreType.DMA((2,))],
        compiler_params=params,
        name="product",
    )(rows.reshape(1, k_tiles), slots, tiles_kept, lax.all_to_all(wanted, "row", 0, 0), flag, *dual_side)
    dual_next, too_many = pl.pallas_call(
        functools.partial(dual_kernel, n_col),
        out_shape=(jax.ShapeDtypeStruct((row_blocks, TILE), f32), jax.ShapeDtypeStruct((1,), i32)),
        in_specs=[VMEM] * (n_col + 3) + [SMEM],
        out_specs=(VMEM, SMEM),
        compiler_params=params,
        name="dual_step",
    )(*gathered_along(row_terms, "col"), duals_kept, *dual_kept, step_sizes)
    vectors = (primal, duals, cost_vec, lower_bound, upper_bound, bound_kind, right_side, row_kind, step_sizes)
    return lax.cond(
        too_many[0] > 0,
        lambda done: full_step(tiles, rows, cols, *vectors),
        lambda done: done,
        (primal_next.reshape(-1), dual_next.reshape(-1)),
    )


def solution(mesh):
    return jax.shard_map(
        local,
        mesh=mesh,
        in_specs=(
            P("row", "col", None, None, None),
            P("row", "col", None),
            P("row", "col", None),
            P(("col", "row")),
            P("row"),
            P(("col", "row")),
            P(("col", "row")),
            P(("col", "row")),
            P(("col", "row")),
            P("row"),
            P("row"),
            P(),
        ),
        out_specs=(P(("col", "row")), P("row")),
        check_vma=False,
    )
```

```python
import functools
import jax
import jax.numpy as jnp
from jax import lax
from jax.experimental import pallas as pl
from jax.experimental.pallas import tpu as pltpu
from jax.sharding import PartitionSpec as P

TILE = 128
GROUP = 16
CHUNK = 16
SLOTS = 40
HEAD = 16
BITS = 14
LEAST = -60

f32 = jnp.float32
bf16 = jnp.bfloat16
i32 = jnp.int32
i16 = jnp.int16
VMEM = pl.BlockSpec(memory_space=pltpu.VMEM)
SMEM = pl.BlockSpec(memory_space=pltpu.SMEM)
HBM = pl.BlockSpec(memory_space=pltpu.HBM)


def iota(shape, axis):
    return lax.broadcasted_iota(i32, shape, axis)


def where_one(condition):
    return jnp.where(condition, 1.0, 0.0)


def one_row_of(block, position):
    return jnp.where(iota(block.shape, 0) == position, block, 0.0).astype(bf16)


def rounds_of(n_row):
    chunks = -(-n_row * SLOTS // TILE)
    return chunks, chunks + 1


def coded(values):
    largest = jnp.maximum(jnp.max(jnp.abs(values), axis=1, keepdims=True), 1e-30)
    exponent = jnp.maximum(jnp.ceil(jnp.log2(largest)), LEAST)
    whole = jnp.floor(values * jnp.exp2(BITS - exponent) + 0.5).astype(i32)
    return whole, jnp.broadcast_to(exponent, values.shape)


def two_parts(whole):
    low = jnp.bitwise_and(whole, 255)
    parts = [(whole - low).astype(f32), low.astype(f32)]
    return jnp.concatenate(parts, axis=1).astype(bf16)


def picked_sums(masks, wholes):
    left = masks[0] if len(masks) == 1 else jnp.concatenate(masks, axis=1)
    both = jnp.dot(
        left.astype(bf16),
        jnp.concatenate([two_parts(w) for w in wholes], axis=0),
        preferred_element_type=f32,
    )
    return both[:, :TILE] + both[:, TILE:]


def scaled_mask(down, places, exponents):
    return jnp.where(down == places, jnp.exp2(exponents.astype(f32) - BITS), 0.0)


def padded_rows(blocks, rows):
    missing = rows - sum(b.shape[0] for b in blocks)
    return jnp.concatenate(blocks + [jnp.zeros((missing, TILE), blocks[0].dtype)] * (missing > 0), axis=0)


def started(sources, targets, sems):
    copies = [
        pltpu.make_async_copy(source, target, sems.at[n])
        for n, (source, target) in enumerate(zip(sources, targets))
    ]
    for copy in copies:
        copy.start()
    return copies


def transpose_product_kernel(owned, *refs):
    (rows_hbm, cols_hbm, duals_hbm, tiles_hbm), (out_ref, slot_ref, duals, tiles), refs = refs[:4], refs[4:8], refs[8:]
    rows, cols, picked, terms, small_sems, tile_sems = refs
    n_row = out_ref.shape[0]
    chunks, head_rows = rounds_of(n_row)
    most = SLOTS - head_rows
    k_tiles = tiles.shape[0]
    groups = [pl.ds(g * CHUNK, CHUNK) for g in range(k_tiles // CHUNK)]
    small = started([cols_hbm, rows_hbm, duals_hbm], [cols, rows, duals], small_sems)
    large = started([tiles_hbm.at[g] for g in groups], [tiles.at[g] for g in groups], tile_sems)

    for copy in small:
        copy.wait()
    for k in range(k_tiles):
        picked[pl.ds(k, 1), :] = duals[pl.ds(rows[k], 1), :]

    def products_of(chunk):
        large[chunk].wait()
        for first in range(chunk * CHUNK, (chunk + 1) * CHUNK, GROUP):
            group = pl.ds(first, GROUP)
            block = picked[group, :].astype(bf16).astype(f32)
            left = jnp.concatenate([one_row_of(block, m) for m in range(GROUP)], axis=1)
            terms[group, :] = jnp.dot(
                left, tiles[group].reshape(GROUP * TILE, TILE), preferred_element_type=f32
            )

    products_of(0)

    square = (k_tiles, k_tiles)
    col_across = cols[...]
    col_down = jnp.transpose(jnp.broadcast_to(col_across.astype(f32), square)).astype(i32)
    owner_across = sum((col_across >= o * owned).astype(i32) for o in range(1, n_row))
    owner_down = sum((col_down >= o * owned).astype(i32) for o in range(1, n_row))
    same = owner_down == owner_across
    earlier_down = iota(square, 0) < iota(square, 1)
    earlier_across = iota(square, 1) < iota(square, 0)
    rank_across = jnp.sum(where_one(same & earlier_down), axis=0, keepdims=True).astype(i32)
    rank_down = jnp.sum(where_one(same & earlier_across), axis=1, keepdims=True).astype(i32)
    slot_across = jnp.where(rank_across < most, owner_across * SLOTS + head_rows + rank_across, -1)
    slot_down = jnp.where(rank_down < most, owner_down * SLOTS + head_rows + rank_down, -1)
    slot_ref[...] = slot_down
    too_many = where_one(jnp.max(rank_across, axis=1, keepdims=True) >= most)
    to_slots = where_one(iota((n_row * SLOTS, k_tiles), 0) == slot_across)
    here = jnp.where(rank_down < most, lax.axis_index("row") * SLOTS + head_rows + rank_down, -1)
    width = chunks * TILE
    to_lanes = where_one(iota((k_tiles, width), 1) == here)
    of_owner = where_one(iota((n_row, k_tiles), 0) == owner_across)
    place = col_across - owner_across * owned + 1
    place_low = jnp.bitwise_and(place, 255)
    head_left = jnp.concatenate(
        [of_owner * (place - place_low).astype(f32), of_owner * place_low.astype(f32), of_owner], axis=0
    ).astype(bf16)

    for chunk in range(1, len(large)):
        products_of(chunk)
    whole, exponents = coded(terms[...])

    scaled = [to_lanes, to_lanes * jnp.concatenate([exponents] * chunks, axis=1)]
    heads = jnp.dot(head_left, jnp.concatenate(scaled, axis=1).astype(bf16), preferred_element_type=f32)
    places = heads[:n_row, :width] + heads[n_row : 2 * n_row, :width]
    packed = heads[2 * n_row :, width:] * place_range(owned) + places
    both = jnp.dot(to_slots.astype(bf16), two_parts(whole), preferred_element_type=f32)
    body = both[:, :TILE] + both[:, TILE:]
    top = -(-head_rows // 8) * 8
    line = iota((top, TILE), 0)
    for o in range(n_row):
        head = jnp.where(line == chunks, too_many, body[o * SLOTS : o * SLOTS + top])
        for c in range(chunks):
            head = jnp.where(line == c, packed[o : o + 1, c * TILE : (c + 1) * TILE], head)
        rows_of = body[o * SLOTS + top : (o + 1) * SLOTS]
        out_ref[o] = jnp.concatenate([head, rows_of], axis=0).astype(i32).astype(i16)


def place_range(owned):
    return 1 << owned.bit_length()


def primal_kernel(
    payloads, primal_ref, cost_ref, lower_ref, upper_ref, kind_ref, steps_ref, next_hbm, flag_ref, *refs
):
    wanted, next_ref, extrap, sem = refs
    n_row = payloads.shape[0]
    chunks, head_rows = rounds_of(n_row)
    blocks = primal_ref.shape[0]
    padded = extrap.shape[0]
    wholes = [payloads[s].astype(i32) for s in range(n_row)]
    top = -(-head_rows // 8) * 8
    head = sum(w[:top] for w in wholes)
    flag_ref[...] = jnp.broadcast_to(head[chunks:head_rows], flag_ref.shape)
    whole = padded_rows(wholes, chunks * TILE)
    down = iota((blocks, TILE), 0) + 1
    places = jnp.bitwise_and(head, place_range(blocks) - 1)
    scales = lax.shift_right_arithmetic(head, blocks.bit_length())
    masks, wholes = [], []
    for c in range(chunks):
        masks.append(scaled_mask(down, places[c : c + 1], scales[c : c + 1]))
        wholes.append(whole[c * TILE : (c + 1) * TILE])
    col_sums = picked_sums(masks, wholes)
    primal = primal_ref[...]
    kind = kind_ref[...]
    moved = primal - steps_ref[0] * (cost_ref[...] - col_sums)
    moved = jnp.where(kind % 2 == 1, jnp.maximum(moved, lower_ref[...]), moved)
    moved = jnp.where(kind >= 2, jnp.minimum(moved, upper_ref[...]), moved)
    next_ref[...] = moved
    copy = pltpu.make_async_copy(next_ref, next_hbm, sem)
    copy.start()
    aligned = blocks // 8 * 8
    if padded > aligned:
        extrap[pl.ds(aligned, padded - aligned), :] = jnp.zeros((padded - aligned, TILE), f32)
    extrap[pl.ds(0, blocks), :] = 2.0 * moved - primal
    right = extrap[...].astype(bf16)
    across = iota((TILE, padded), 1) + 1
    places = jnp.transpose(places.astype(f32)).astype(i32)
    sent = [
        jnp.dot(where_one(across == places[:, c : c + 1]).astype(bf16), right, preferred_element_type=f32)
        for c in range(chunks)
    ]
    sent = jnp.concatenate(sent, axis=0)
    for s in range(n_row):
        wanted[s] = sent[s * SLOTS : (s + 1) * SLOTS].astype(bf16)
    copy.wait()


def product_kernel(*refs):
    (rows_ref, slot_ref, tiles_ref, arrived, flag_ref), others_hbm, refs = refs[:5], refs[5:7], refs[7:]
    out_ref, others, sems = refs[0], refs[1:3], refs[3]
    later = started(others_hbm, others, sems)
    k_tiles = tiles_ref.shape[0]
    chunks, _ = rounds_of(arrived.shape[0])
    blocks = [arrived[s].astype(f32) for s in range(arrived.shape[0])]
    received = padded_rows(blocks, chunks * TILE).astype(bf16)
    across = iota((k_tiles, received.shape[0]), 1)
    slots = jnp.concatenate([slot_ref[...]] * (received.shape[0] // TILE), axis=1)
    block = jnp.dot(where_one(across == slots).astype(bf16), received, preferred_element_type=f32)
    down = jnp.transpose(block)
    lane = iota((TILE, k_tiles), 1)
    right = jnp.concatenate(
        [jnp.where(lane % 2 == 0, down, 0.0), jnp.where(lane % 2 == 1, down, 0.0)], axis=0
    ).astype(bf16)
    terms = jnp.zeros((TILE, k_tiles), f32)
    for g in range(k_tiles // 8):
        even = jnp.concatenate([tiles_ref[8 * g + m] for m in (0, 2, 4, 6)], axis=0)
        odd = jnp.concatenate([tiles_ref[8 * g + m] for m in (1, 3, 5, 7)], axis=0)
        products = jnp.dot(jnp.concatenate([even, odd], axis=1), right, preferred_element_type=f32)
        for p in range(4):
            terms = jnp.where(lane // 2 == 4 * g + p, products[p * TILE : (p + 1) * TILE], terms)
    whole, exponents = coded(jnp.transpose(terms))
    out_ref[pl.ds(0, k_tiles), :] = whole.astype(i16)
    line = iota((HEAD, TILE), 0)
    head = jnp.where(line == 0, rows_ref[...], jnp.transpose(exponents)[0:HEAD, :].astype(i32))
    head = jnp.where(line == 2, flag_ref[0:1, :], head)
    out_ref[pl.ds(k_tiles, HEAD), :] = head.astype(i16)
    for copy in later:
        copy.wait()


def dual_kernel(n_col, *refs):
    payloads, (duals_ref, right_ref, kind_ref, steps_ref, next_ref, flag_ref) = refs[:n_col], refs[n_col:]
    k_tiles = payloads[0].shape[0] - HEAD
    down = iota((duals_ref.shape[0], k_tiles), 0)
    masks, wholes = [], []
    flags = jnp.zeros((1, TILE), i32)
    for payload in payloads:
        head = payload[pl.ds(k_tiles, HEAD), :].astype(i32)
        masks.append(scaled_mask(down, head[0:1], head[1:2]))
        wholes.append(payload[pl.ds(0, k_tiles), :].astype(i32))
        flags += head[2:3]
    row_sums = picked_sums(masks, wholes)
    updated = duals_ref[...] + steps_ref[1] * (right_ref[...] - row_sums)
    next_ref[...] = jnp.where(kind_ref[...] == 1, jnp.maximum(updated, 0.0), updated)
    flag_ref[0] = jnp.max(flags)


def partners(axis):
    size = lax.axis_size(axis)
    if size & (size - 1) == 0:
        there = [[(i, i ^ n) for i in range(size)] for n in range(1, size)]
    else:
        there = [[(i, (i + n) % size) for i in range(size)] for n in range(1, size)]
    return [(pairs, [(j, i) for i, j in pairs]) for pairs in there]


def gathered_along(array, axis):
    return [array] + [lax.ppermute(array, axis, there) for there, _ in partners(axis)]


def sums_at(places, terms, blocks):
    mask = (jnp.arange(blocks)[:, None] == jnp.concatenate(places)[None, :]).astype(f32)
    return jnp.dot(mask, jnp.concatenate(terms), precision=lax.Precision.HIGHEST).reshape(-1)


def full_step(
    tiles, rows, cols, primal, duals, cost_vec, lower_bound, upper_bound, bound_kind, right_side, row_kind, steps
):
    col_blocks = primal.shape[0] // TILE
    row_blocks = duals.shape[0] // TILE
    wide = tiles.astype(f32)
    dual_blocks = duals.astype(bf16).astype(f32).reshape(row_blocks, TILE)[rows]
    col_terms = jnp.einsum("kij,ki->kj", wide, dual_blocks)
    first = lax.axis_index("row") * col_blocks
    places = [there - first for there in gathered_along(cols, "row")]
    places = [jnp.where((p >= 0) & (p < col_blocks), p, col_blocks) for p in places]
    col_sums = sums_at(places, gathered_along(col_terms, "row"), col_blocks)
    moved = primal - steps[0] * (cost_vec - col_sums)
    moved = jnp.where(bound_kind % 2 == 1, jnp.maximum(moved, lower_bound), moved)
    moved = jnp.where(bound_kind >= 2, jnp.minimum(moved, upper_bound), moved)
    extrap = (2.0 * moved - primal).astype(bf16).reshape(col_blocks, TILE)
    wanted = [
        jnp.where((p < col_blocks)[:, None], extrap[jnp.minimum(p, col_blocks - 1)], jnp.zeros((), bf16))
        for p in places
    ]
    blocks = wanted[0].astype(f32)
    for block, (_, back) in zip(wanted[1:], partners("row")):
        blocks += lax.ppermute(block, "row", back).astype(f32)
    row_terms = jnp.einsum("kij,kj->ki", wide, blocks)
    row_sums = sums_at(gathered_along(rows, "col"), gathered_along(row_terms, "col"), row_blocks)
    updated = duals + steps[1] * (right_side - row_sums)
    return moved, jnp.where(row_kind == 1, jnp.maximum(updated, 0.0), updated)


def local(
    block_tiles,
    tile_row,
    tile_col,
    primal,
    duals,
    cost_vec,
    lower_bound,
    upper_bound,
    bound_kind,
    right_side,
    row_kind,
    step_sizes,
):
    k_tiles = block_tiles.shape[2]
    tiles = block_tiles.reshape(k_tiles, TILE, TILE)
    rows = tile_row.reshape(-1)
    cols = tile_col.reshape(-1)
    n_row = lax.axis_size("row")
    n_col = lax.axis_size("col")
    col_blocks = primal.shape[0] // TILE
    row_blocks = duals.shape[0] // TILE
    padded = -(-col_blocks // TILE) * TILE
    in_hbm = lambda array: pltpu.with_memory_space_constraint(array, pltpu.HBM)
    by_block = lambda array: in_hbm(array.reshape(-1, TILE))
    shape_of = lambda array: jax.ShapeDtypeStruct(array.shape, array.dtype)
    params = pltpu.CompilerParams(vmem_limit_bytes=32 * 1024 * 1024)
    primal_side = [a.reshape(-1, TILE) for a in (primal, cost_vec, lower_bound, upper_bound, bound_kind)]
    dual_side = [by_block(a) for a in (right_side, row_kind)]
    own = [by_block(duals), in_hbm(tiles)]

    col_terms, slots, duals_kept, tiles_kept = pl.pallas_call(
        functools.partial(transpose_product_kernel, col_blocks),
        out_shape=(
            jax.ShapeDtypeStruct((n_row, SLOTS, TILE), i16),
            jax.ShapeDtypeStruct((k_tiles, TILE), i32),
            *[shape_of(a) for a in own],
        ),
        in_specs=[HBM] * 4,
        out_specs=(VMEM,) * 4,
        scratch_shapes=[
            pltpu.SMEM((k_tiles,), i32),
            pltpu.VMEM((1, k_tiles), i32),
            pltpu.VMEM((k_tiles, TILE), f32),
            pltpu.VMEM((k_tiles, TILE), f32),
            pltpu.SemaphoreType.DMA((3,)),
            pltpu.SemaphoreType.DMA((k_tiles // CHUNK,)),
        ],
        compiler_params=params,
        name="transpose_product",
    )(in_hbm(rows), in_hbm(cols.reshape(1, k_tiles)), *own)
    primal_next, flag, wanted = pl.pallas_call(
        primal_kernel,
        out_shape=(
            jax.ShapeDtypeStruct((col_blocks, TILE), f32),
            jax.ShapeDtypeStruct((8, TILE), i32),
            jax.ShapeDtypeStruct((n_row, SLOTS, TILE), bf16),
        ),
        in_specs=[VMEM] * 6 + [SMEM],
        out_specs=(HBM, VMEM, VMEM),
        scratch_shapes=[
            pltpu.VMEM((col_blocks, TILE), f32),
            pltpu.VMEM((padded, TILE), f32),
            pltpu.SemaphoreType.DMA,
        ],
        compiler_params=params,
        name="primal_step",
    )(lax.all_to_all(col_terms, "row", 0, 0), *primal_side, step_sizes)
    row_terms, *dual_kept = pl.pallas_call(
        product_kernel,
        out_shape=(
            jax.ShapeDtypeStruct((k_tiles + HEAD, TILE), i16),
            *[shape_of(a) for a in dual_side],
        ),
        in_specs=[VMEM] * 5 + [HBM] * 2,
        out_specs=(VMEM,) * 3,
        scratch_shapes=[pltpu.SemaphoreType.DMA((2,))],
        compiler_params=params,
        name="product",
    )(rows.reshape(1, k_tiles), slots, tiles_kept, lax.all_to_all(wanted, "row", 0, 0), flag, *dual_side)
    dual_next, too_many = pl.pallas_call(
        functools.partial(dual_kernel, n_col),
        out_shape=(jax.ShapeDtypeStruct((row_blocks, TILE), f32), jax.ShapeDtypeStruct((1,), i32)),
        in_specs=[VMEM] * (n_col + 3) + [SMEM],
        out_specs=(VMEM, SMEM),
        compiler_params=params,
        name="dual_step",
    )(*gathered_along(row_terms, "col"), duals_kept, *dual_kept, step_sizes)
    vectors = (primal, duals, cost_vec, lower_bound, upper_bound, bound_kind, right_side, row_kind, step_sizes)
    return lax.cond(
        too_many[0] > 0,
        lambda done: full_step(tiles, rows, cols, *vectors),
        lambda done: done,
        (primal_next.reshape(-1), dual_next.reshape(-1)),
    )


def solution(mesh):
    return jax.shard_map(
        local,
        mesh=mesh,
        in_specs=(
            P("row", "col", None, None, None),
            P("row", "col", None),
            P("row", "col", None),
            P(("col", "row")),
            P("row"),
            P(("col", "row")),
            P(("col", "row")),
            P(("col", "row")),
            P(("col", "row")),
            P("row"),
            P("row"),
            P(),
        ),
        out_specs=(P(("col", "row")), P("row")),
        check_vma=False,
    )
```

```python
import functools
import jax
import jax.numpy as jnp
from jax import lax
from jax.experimental import pallas as pl
from jax.experimental.pallas import tpu as pltpu
from jax.sharding import PartitionSpec as P

TILE = 128
GROUP = 16
CHUNK = 32
SLOTS = 40
HEAD = 16
BITS = 14
LEAST = -60

f32 = jnp.float32
bf16 = jnp.bfloat16
i32 = jnp.int32
i16 = jnp.int16
VMEM = pl.BlockSpec(memory_space=pltpu.VMEM)
SMEM = pl.BlockSpec(memory_space=pltpu.SMEM)
HBM = pl.BlockSpec(memory_space=pltpu.HBM)


def iota(shape, axis):
    return lax.broadcasted_iota(i32, shape, axis)


def where_one(condition):
    return jnp.where(condition, 1.0, 0.0)


def one_row_of(block, position):
    return jnp.where(iota(block.shape, 0) == position, block, 0.0).astype(bf16)


def rounds_of(n_row):
    chunks = -(-n_row * SLOTS // TILE)
    return chunks, chunks + 1


def coded(values):
    largest = jnp.maximum(jnp.max(jnp.abs(values), axis=1, keepdims=True), 1e-30)
    exponent = jnp.maximum(jnp.ceil(jnp.log2(largest)), LEAST)
    whole = jnp.floor(values * jnp.exp2(BITS - exponent) + 0.5).astype(i32)
    return whole, jnp.broadcast_to(exponent, values.shape)


def two_parts(whole):
    low = jnp.bitwise_and(whole, 255)
    parts = [(whole - low).astype(f32), low.astype(f32)]
    return jnp.concatenate(parts, axis=1).astype(bf16)


def picked_sums(masks, wholes):
    left = masks[0] if len(masks) == 1 else jnp.concatenate(masks, axis=1)
    both = jnp.dot(
        left.astype(bf16),
        jnp.concatenate([two_parts(w) for w in wholes], axis=0),
        preferred_element_type=f32,
    )
    return both[:, :TILE] + both[:, TILE:]


def scaled_mask(down, places, exponents):
    return jnp.where(down == places, jnp.exp2(exponents.astype(f32) - BITS), 0.0)


def padded_rows(blocks, rows):
    missing = rows - sum(b.shape[0] for b in blocks)
    return jnp.concatenate(blocks + [jnp.zeros((missing, TILE), blocks[0].dtype)] * (missing > 0), axis=0)


def started(sources, targets, sems):
    copies = [
        pltpu.make_async_copy(source, target, sems.at[n])
        for n, (source, target) in enumerate(zip(sources, targets))
    ]
    for copy in copies:
        copy.start()
    return copies


def transpose_product_kernel(owned, *refs):
    (rows_hbm, cols_hbm, duals_hbm, tiles_hbm), (out_ref, slot_ref, duals, tiles), refs = refs[:4], refs[4:8], refs[8:]
    rows, cols, picked, small_sems, tile_sems = refs
    n_row = out_ref.shape[0]
    chunks, head_rows = rounds_of(n_row)
    most = SLOTS - head_rows
    k_tiles = tiles.shape[0]
    groups = [pl.ds(g * CHUNK, CHUNK) for g in range(k_tiles // CHUNK)]
    small = started([cols_hbm, rows_hbm, duals_hbm], [cols, rows, duals], small_sems)
    large = started([tiles_hbm.at[g] for g in groups], [tiles.at[g] for g in groups], tile_sems)

    for copy in small:
        copy.wait()
    for k in range(k_tiles):
        picked[pl.ds(k, 1), :] = duals[pl.ds(rows[k], 1), :]

    terms = []

    def products_of(chunk):
        large[chunk].wait()
        for first in range(chunk * CHUNK, (chunk + 1) * CHUNK, GROUP):
            group = pl.ds(first, GROUP)
            block = picked[group, :].astype(bf16).astype(f32)
            left = jnp.concatenate([one_row_of(block, m) for m in range(GROUP)], axis=1)
            terms.append(
                jnp.dot(left, tiles[group].reshape(GROUP * TILE, TILE), preferred_element_type=f32)
            )

    products_of(0)

    square = (k_tiles, k_tiles)
    col_across = cols[...]
    col_down = jnp.transpose(jnp.broadcast_to(col_across.astype(f32), square)).astype(i32)
    owner_across = sum((col_across >= o * owned).astype(i32) for o in range(1, n_row))
    owner_down = sum((col_down >= o * owned).astype(i32) for o in range(1, n_row))
    same = owner_down == owner_across
    earlier_down = iota(square, 0) < iota(square, 1)
    earlier_across = iota(square, 1) < iota(square, 0)
    rank_across = jnp.sum(where_one(same & earlier_down), axis=0, keepdims=True).astype(i32)
    rank_down = jnp.sum(where_one(same & earlier_across), axis=1, keepdims=True).astype(i32)
    slot_across = jnp.where(rank_across < most, owner_across * SLOTS + head_rows + rank_across, -1)
    slot_down = jnp.where(rank_down < most, owner_down * SLOTS + head_rows + rank_down, -1)
    slot_ref[...] = slot_down
    too_many = where_one(jnp.max(rank_across, axis=1, keepdims=True) >= most)
    to_slots = where_one(iota((n_row * SLOTS, k_tiles), 0) == slot_across)
    here = jnp.where(rank_down < most, lax.axis_index("row") * SLOTS + head_rows + rank_down, -1)
    width = chunks * TILE
    to_lanes = where_one(iota((k_tiles, width), 1) == here)
    of_owner = where_one(iota((n_row, k_tiles), 0) == owner_across)
    place = col_across - owner_across * owned + 1
    place_low = jnp.bitwise_and(place, 255)
    head_left = jnp.concatenate(
        [of_owner * (place - place_low).astype(f32), of_owner * place_low.astype(f32), of_owner], axis=0
    ).astype(bf16)

    for chunk in range(1, len(large)):
        products_of(chunk)
    whole, exponents = coded(jnp.concatenate(terms, axis=0))

    scaled = [to_lanes, to_lanes * jnp.concatenate([exponents] * chunks, axis=1)]
    heads = jnp.dot(head_left, jnp.concatenate(scaled, axis=1).astype(bf16), preferred_element_type=f32)
    places = heads[:n_row, :width] + heads[n_row : 2 * n_row, :width]
    packed = heads[2 * n_row :, width:] * place_range(owned) + places
    both = jnp.dot(to_slots.astype(bf16), two_parts(whole), preferred_element_type=f32)
    body = both[:, :TILE] + both[:, TILE:]
    top = -(-head_rows // 8) * 8
    line = iota((top, TILE), 0)
    for o in range(n_row):
        head = jnp.where(line == chunks, too_many, body[o * SLOTS : o * SLOTS + top])
        for c in range(chunks):
            head = jnp.where(line == c, packed[o : o + 1, c * TILE : (c + 1) * TILE], head)
        rows_of = body[o * SLOTS + top : (o + 1) * SLOTS]
        out_ref[o] = jnp.concatenate([head, rows_of], axis=0).astype(i32).astype(i16)


def place_range(owned):
    return 1 << owned.bit_length()


def primal_kernel(
    payloads, primal_ref, cost_ref, lower_ref, upper_ref, kind_ref, steps_ref, next_hbm, flag_ref, *refs
):
    wanted, next_ref, extrap, sem = refs
    n_row = payloads.shape[0]
    chunks, head_rows = rounds_of(n_row)
    blocks = primal_ref.shape[0]
    padded = extrap.shape[0]
    wholes = [payloads[s].astype(i32) for s in range(n_row)]
    top = -(-head_rows // 8) * 8
    head = sum(w[:top] for w in wholes)
    flag_ref[...] = jnp.broadcast_to(head[chunks:head_rows], flag_ref.shape)
    whole = padded_rows(wholes, chunks * TILE)
    down = iota((blocks, TILE), 0) + 1
    places = jnp.bitwise_and(head, place_range(blocks) - 1)
    scales = lax.shift_right_arithmetic(head, blocks.bit_length())
    masks, wholes = [], []
    for c in range(chunks):
        masks.append(scaled_mask(down, places[c : c + 1], scales[c : c + 1]))
        wholes.append(whole[c * TILE : (c + 1) * TILE])
    col_sums = picked_sums(masks, wholes)
    primal = primal_ref[...]
    kind = kind_ref[...]
    moved = primal - steps_ref[0] * (cost_ref[...] - col_sums)
    moved = jnp.where(kind % 2 == 1, jnp.maximum(moved, lower_ref[...]), moved)
    moved = jnp.where(kind >= 2, jnp.minimum(moved, upper_ref[...]), moved)
    next_ref[...] = moved
    copy = pltpu.make_async_copy(next_ref, next_hbm, sem)
    copy.start()
    aligned = blocks // 8 * 8
    if padded > aligned:
        extrap[pl.ds(aligned, padded - aligned), :] = jnp.zeros((padded - aligned, TILE), f32)
    extrap[pl.ds(0, blocks), :] = 2.0 * moved - primal
    right = extrap[...].astype(bf16)
    across = iota((TILE, padded), 1) + 1
    places = jnp.transpose(places.astype(f32)).astype(i32)
    sent = [
        jnp.dot(where_one(across == places[:, c : c + 1]).astype(bf16), right, preferred_element_type=f32)
        for c in range(chunks)
    ]
    sent = jnp.concatenate(sent, axis=0)
    for s in range(n_row):
        wanted[s] = sent[s * SLOTS : (s + 1) * SLOTS].astype(bf16)
    copy.wait()


def product_kernel(*refs):
    (rows_ref, slot_ref, tiles_ref, arrived, flag_ref), others_hbm, refs = refs[:5], refs[5:7], refs[7:]
    out_ref, others, sems = refs[0], refs[1:3], refs[3]
    later = started(others_hbm, others, sems)
    k_tiles = tiles_ref.shape[0]
    chunks, _ = rounds_of(arrived.shape[0])
    blocks = [arrived[s].astype(f32) for s in range(arrived.shape[0])]
    received = padded_rows(blocks, chunks * TILE).astype(bf16)
    across = iota((k_tiles, received.shape[0]), 1)
    slots = jnp.concatenate([slot_ref[...]] * (received.shape[0] // TILE), axis=1)
    block = jnp.dot(where_one(across == slots).astype(bf16), received, preferred_element_type=f32)
    down = jnp.transpose(block)
    lane = iota((TILE, k_tiles), 1)
    right = jnp.concatenate(
        [jnp.where(lane % 2 == 0, down, 0.0), jnp.where(lane % 2 == 1, down, 0.0)], axis=0
    ).astype(bf16)
    terms = jnp.zeros((TILE, k_tiles), f32)
    for g in range(k_tiles // 8):
        even = jnp.concatenate([tiles_ref[8 * g + m] for m in (0, 2, 4, 6)], axis=0)
        odd = jnp.concatenate([tiles_ref[8 * g + m] for m in (1, 3, 5, 7)], axis=0)
        products = jnp.dot(jnp.concatenate([even, odd], axis=1), right, preferred_element_type=f32)
        for p in range(4):
            terms = jnp.where(lane // 2 == 4 * g + p, products[p * TILE : (p + 1) * TILE], terms)
    whole, exponents = coded(jnp.transpose(terms))
    out_ref[pl.ds(0, k_tiles), :] = whole.astype(i16)
    line = iota((HEAD, TILE), 0)
    head = jnp.where(line == 0, rows_ref[...], jnp.transpose(exponents)[0:HEAD, :].astype(i32))
    head = jnp.where(line == 2, flag_ref[0:1, :], head)
    out_ref[pl.ds(k_tiles, HEAD), :] = head.astype(i16)
    for copy in later:
        copy.wait()


def row_sums_of(payloads, blocks):
    k_tiles = payloads[0].shape[0] - HEAD
    down = iota((blocks, k_tiles), 0)
    masks, wholes = [], []
    flags = jnp.zeros((1, TILE), i32)
    for payload in payloads:
        head = payload[pl.ds(k_tiles, HEAD), :].astype(i32)
        masks.append(scaled_mask(down, head[0:1], head[1:2]))
        wholes.append(payload[pl.ds(0, k_tiles), :].astype(i32))
        flags += head[2:3]
    return picked_sums(masks, wholes), flags


def own_dual_kernel(payload, duals_ref, right_ref, steps_ref, part_ref):
    row_sums, _ = row_sums_of([payload], duals_ref.shape[0])
    part_ref[...] = duals_ref[...] + steps_ref[1] * (right_ref[...] - row_sums)


def dual_kernel(*refs):
    payloads, (part_ref, kind_ref, steps_ref, next_ref, flag_ref) = refs[:-5], refs[-5:]
    row_sums, flags = row_sums_of(payloads, part_ref.shape[0])
    updated = part_ref[...] - steps_ref[1] * row_sums
    next_ref[...] = jnp.where(kind_ref[...] == 1, jnp.maximum(updated, 0.0), updated)
    flag_ref[0] = jnp.max(flags)


def partners(axis):
    size = lax.axis_size(axis)
    if size & (size - 1) == 0:
        there = [[(i, i ^ n) for i in range(size)] for n in range(1, size)]
    else:
        there = [[(i, (i + n) % size) for i in range(size)] for n in range(1, size)]
    return [(pairs, [(j, i) for i, j in pairs]) for pairs in there]


def gathered_along(array, axis):
    return [array] + [lax.ppermute(array, axis, there) for there, _ in partners(axis)]


def sums_at(places, terms, blocks):
    mask = (jnp.arange(blocks)[:, None] == jnp.concatenate(places)[None, :]).astype(f32)
    return jnp.dot(mask, jnp.concatenate(terms), precision=lax.Precision.HIGHEST).reshape(-1)


def full_step(
    tiles, rows, cols, primal, duals, cost_vec, lower_bound, upper_bound, bound_kind, right_side, row_kind, steps
):
    col_blocks = primal.shape[0] // TILE
    row_blocks = duals.shape[0] // TILE
    wide = tiles.astype(f32)
    dual_blocks = duals.astype(bf16).astype(f32).reshape(row_blocks, TILE)[rows]
    col_terms = jnp.einsum("kij,ki->kj", wide, dual_blocks)
    first = lax.axis_index("row") * col_blocks
    places = [there - first for there in gathered_along(cols, "row")]
    places = [jnp.where((p >= 0) & (p < col_blocks), p, col_blocks) for p in places]
    col_sums = sums_at(places, gathered_along(col_terms, "row"), col_blocks)
    moved = primal - steps[0] * (cost_vec - col_sums)
    moved = jnp.where(bound_kind % 2 == 1, jnp.maximum(moved, lower_bound), moved)
    moved = jnp.where(bound_kind >= 2, jnp.minimum(moved, upper_bound), moved)
    extrap = (2.0 * moved - primal).astype(bf16).reshape(col_blocks, TILE)
    wanted = [
        jnp.where((p < col_blocks)[:, None], extrap[jnp.minimum(p, col_blocks - 1)], jnp.zeros((), bf16))
        for p in places
    ]
    blocks = wanted[0].astype(f32)
    for block, (_, back) in zip(wanted[1:], partners("row")):
        blocks += lax.ppermute(block, "row", back).astype(f32)
    row_terms = jnp.einsum("kij,kj->ki", wide, blocks)
    row_sums = sums_at(gathered_along(rows, "col"), gathered_along(row_terms, "col"), row_blocks)
    updated = duals + steps[1] * (right_side - row_sums)
    return moved, jnp.where(row_kind == 1, jnp.maximum(updated, 0.0), updated)


def local(
    block_tiles,
    tile_row,
    tile_col,
    primal,
    duals,
    cost_vec,
    lower_bound,
    upper_bound,
    bound_kind,
    right_side,
    row_kind,
    step_sizes,
):
    k_tiles = block_tiles.shape[2]
    tiles = block_tiles.reshape(k_tiles, TILE, TILE)
    rows = tile_row.reshape(-1)
    cols = tile_col.reshape(-1)
    n_row = lax.axis_size("row")
    n_col = lax.axis_size("col")
    col_blocks = primal.shape[0] // TILE
    row_blocks = duals.shape[0] // TILE
    padded = -(-col_blocks // TILE) * TILE
    in_hbm = lambda array: pltpu.with_memory_space_constraint(array, pltpu.HBM)
    by_block = lambda array: in_hbm(array.reshape(-1, TILE))
    shape_of = lambda array: jax.ShapeDtypeStruct(array.shape, array.dtype)
    params = pltpu.CompilerParams(vmem_limit_bytes=32 * 1024 * 1024)
    primal_side = [a.reshape(-1, TILE) for a in (primal, cost_vec, lower_bound, upper_bound, bound_kind)]
    dual_side = [by_block(a) for a in (right_side, row_kind)]
    own = [by_block(duals), in_hbm(tiles)]

    col_terms, slots, duals_kept, tiles_kept = pl.pallas_call(
        functools.partial(transpose_product_kernel, col_blocks),
        out_shape=(
            jax.ShapeDtypeStruct((n_row, SLOTS, TILE), i16),
            jax.ShapeDtypeStruct((k_tiles, TILE), i32),
            *[shape_of(a) for a in own],
        ),
        in_specs=[HBM] * 4,
        out_specs=(VMEM,) * 4,
        scratch_shapes=[
            pltpu.SMEM((k_tiles,), i32),
            pltpu.VMEM((1, k_tiles), i32),
            pltpu.VMEM((k_tiles, TILE), f32),
            pltpu.SemaphoreType.DMA((3,)),
            pltpu.SemaphoreType.DMA((k_tiles // CHUNK,)),
        ],
        compiler_params=params,
        name="transpose_product",
    )(in_hbm(rows), in_hbm(cols.reshape(1, k_tiles)), *own)
    primal_next, flag, wanted = pl.pallas_call(
        primal_kernel,
        out_shape=(
            jax.ShapeDtypeStruct((col_blocks, TILE), f32),
            jax.ShapeDtypeStruct((8, TILE), i32),
            jax.ShapeDtypeStruct((n_row, SLOTS, TILE), bf16),
        ),
        in_specs=[VMEM] * 6 + [SMEM],
        out_specs=(HBM, VMEM, VMEM),
        scratch_shapes=[
            pltpu.VMEM((col_blocks, TILE), f32),
            pltpu.VMEM((padded, TILE), f32),
            pltpu.SemaphoreType.DMA,
        ],
        compiler_params=params,
        name="primal_step",
    )(lax.all_to_all(col_terms, "row", 0, 0), *primal_side, step_sizes)
    row_terms, *dual_kept = pl.pallas_call(
        product_kernel,
        out_shape=(
            jax.ShapeDtypeStruct((k_tiles + HEAD, TILE), i16),
            *[shape_of(a) for a in dual_side],
        ),
        in_specs=[VMEM] * 5 + [HBM] * 2,
        out_specs=(VMEM,) * 3,
        scratch_shapes=[pltpu.SemaphoreType.DMA((2,))],
        compiler_params=params,
        name="product",
    )(rows.reshape(1, k_tiles), slots, tiles_kept, lax.all_to_all(wanted, "row", 0, 0), flag, *dual_side)
    _, *others = gathered_along(row_terms, "col")
    part = pl.pallas_call(
        own_dual_kernel,
        out_shape=jax.ShapeDtypeStruct((row_blocks, TILE), f32),
        in_specs=[VMEM] * 3 + [SMEM],
        out_specs=VMEM,
        compiler_params=params,
        cost_estimate=pl.CostEstimate(flops=4 * row_blocks * k_tiles * TILE, bytes_accessed=2**20, transcendentals=0),
        name="own_dual_step",
    )(row_terms, duals_kept, dual_kept[0], step_sizes)
    dual_next, too_many = pl.pallas_call(
        dual_kernel,
        out_shape=(jax.ShapeDtypeStruct((row_blocks, TILE), f32), jax.ShapeDtypeStruct((1,), i32)),
        in_specs=[VMEM] * (n_col + 1) + [SMEM],
        out_specs=(VMEM, SMEM),
        compiler_params=params,
        name="dual_step",
    )(*others, part, dual_kept[1], step_sizes)
    vectors = (primal, duals, cost_vec, lower_bound, upper_bound, bound_kind, right_side, row_kind, step_sizes)
    return lax.cond(
        too_many[0] > 0,
        lambda done: full_step(tiles, rows, cols, *vectors),
        lambda done: done,
        (primal_next.reshape(-1), dual_next.reshape(-1)),
    )


def solution(mesh):
    return jax.shard_map(
        local,
        mesh=mesh,
        in_specs=(
            P("row", "col", None, None, None),
            P("row", "col", None),
            P("row", "col", None),
            P(("col", "row")),
            P("row"),
            P(("col", "row")),
            P(("col", "row")),
            P(("col", "row")),
            P(("col", "row")),
            P("row"),
            P("row"),
            P(),
        ),
        out_specs=(P(("col", "row")), P("row")),
        check_vma=False,
    )
```

```python
import functools
import jax
import jax.numpy as jnp
from jax import lax
from jax.experimental import pallas as pl
from jax.experimental.pallas import tpu as pltpu
from jax.sharding import PartitionSpec as P

TILE = 128
GROUP = 16
CHUNK = 32
SLOTS = 40
HEAD = 16
BITS = 14
LEAST = -60

f32 = jnp.float32
bf16 = jnp.bfloat16
i32 = jnp.int32
i16 = jnp.int16
VMEM = pl.BlockSpec(memory_space=pltpu.VMEM)
SMEM = pl.BlockSpec(memory_space=pltpu.SMEM)
HBM = pl.BlockSpec(memory_space=pltpu.HBM)


def iota(shape, axis):
    return lax.broadcasted_iota(i32, shape, axis)


def where_one(condition):
    return jnp.where(condition, 1.0, 0.0)


def one_row_of(block, position):
    return jnp.where(iota(block.shape, 0) == position, block, 0.0).astype(bf16)


def rounds_of(n_row):
    chunks = -(-n_row * SLOTS // TILE)
    return chunks, chunks + 1


def coded(values):
    largest = jnp.maximum(jnp.max(jnp.abs(values), axis=1, keepdims=True), 1e-30)
    exponent = jnp.maximum(jnp.ceil(jnp.log2(largest)), LEAST)
    whole = jnp.floor(values * jnp.exp2(BITS - exponent) + 0.5).astype(i32)
    return whole, jnp.broadcast_to(exponent, values.shape)


def two_parts(whole):
    low = jnp.bitwise_and(whole, 255)
    parts = [(whole - low).astype(f32), low.astype(f32)]
    return jnp.concatenate(parts, axis=1).astype(bf16)


def picked_sums(masks, wholes):
    left = masks[0] if len(masks) == 1 else jnp.concatenate(masks, axis=1)
    both = jnp.dot(
        left.astype(bf16),
        jnp.concatenate([two_parts(w) for w in wholes], axis=0),
        preferred_element_type=f32,
    )
    return both[:, :TILE] + both[:, TILE:]


def scaled_mask(down, places, exponents):
    return jnp.where(down == places, jnp.exp2(exponents.astype(f32) - BITS), 0.0)


def padded_rows(blocks, rows):
    missing = rows - sum(b.shape[0] for b in blocks)
    return jnp.concatenate(blocks + [jnp.zeros((missing, TILE), blocks[0].dtype)] * (missing > 0), axis=0)


def started(sources, targets, sems):
    copies = [
        pltpu.make_async_copy(source, target, sems.at[n])
        for n, (source, target) in enumerate(zip(sources, targets))
    ]
    for copy in copies:
        copy.start()
    return copies


def transpose_product_kernel(owned, *refs):
    (rows_hbm, cols_hbm, duals_hbm, tiles_hbm), others_hbm, refs = refs[:4], refs[4:9], refs[9:]
    (out_ref, slot_ref, duals, tiles), others, refs = refs[:4], refs[4:9], refs[9:]
    rows, cols, picked, small_sems, tile_sems, other_sems = refs
    n_row = out_ref.shape[0]
    chunks, head_rows = rounds_of(n_row)
    most = SLOTS - head_rows
    k_tiles = tiles.shape[0]
    groups = [pl.ds(g * CHUNK, CHUNK) for g in range(k_tiles // CHUNK)]
    small = started([cols_hbm, rows_hbm, duals_hbm], [cols, rows, duals], small_sems)
    large = started([tiles_hbm.at[g] for g in groups], [tiles.at[g] for g in groups], tile_sems)

    for copy in small:
        copy.wait()
    for k in range(k_tiles):
        picked[pl.ds(k, 1), :] = duals[pl.ds(rows[k], 1), :]

    terms = []

    def products_of(chunk):
        large[chunk].wait()
        for first in range(chunk * CHUNK, (chunk + 1) * CHUNK, GROUP):
            group = pl.ds(first, GROUP)
            block = picked[group, :].astype(bf16).astype(f32)
            left = jnp.concatenate([one_row_of(block, m) for m in range(GROUP)], axis=1)
            terms.append(
                jnp.dot(left, tiles[group].reshape(GROUP * TILE, TILE), preferred_element_type=f32)
            )

    products_of(0)

    square = (k_tiles, k_tiles)
    col_across = cols[...]
    col_down = jnp.transpose(jnp.broadcast_to(col_across.astype(f32), square)).astype(i32)
    owner_across = sum((col_across >= o * owned).astype(i32) for o in range(1, n_row))
    owner_down = sum((col_down >= o * owned).astype(i32) for o in range(1, n_row))
    same = owner_down == owner_across
    earlier_down = iota(square, 0) < iota(square, 1)
    earlier_across = iota(square, 1) < iota(square, 0)
    rank_across = jnp.sum(where_one(same & earlier_down), axis=0, keepdims=True).astype(i32)
    rank_down = jnp.sum(where_one(same & earlier_across), axis=1, keepdims=True).astype(i32)
    slot_across = jnp.where(rank_across < most, owner_across * SLOTS + head_rows + rank_across, -1)
    slot_down = jnp.where(rank_down < most, owner_down * SLOTS + head_rows + rank_down, -1)
    slot_ref[...] = slot_down
    too_many = where_one(jnp.max(rank_across, axis=1, keepdims=True) >= most)
    to_slots = where_one(iota((n_row * SLOTS, k_tiles), 0) == slot_across)
    here = jnp.where(rank_down < most, lax.axis_index("row") * SLOTS + head_rows + rank_down, -1)
    width = chunks * TILE
    to_lanes = where_one(iota((k_tiles, width), 1) == here)
    of_owner = where_one(iota((n_row, k_tiles), 0) == owner_across)
    place = col_across - owner_across * owned + 1
    place_low = jnp.bitwise_and(place, 255)
    head_left = jnp.concatenate(
        [of_owner * (place - place_low).astype(f32), of_owner * place_low.astype(f32), of_owner], axis=0
    ).astype(bf16)

    for chunk in range(1, len(large) - 1):
        products_of(chunk)
    later = started(others_hbm, others, other_sems)
    products_of(len(large) - 1)
    whole, exponents = coded(jnp.concatenate(terms, axis=0))

    scaled = [to_lanes, to_lanes * jnp.concatenate([exponents] * chunks, axis=1)]
    heads = jnp.dot(head_left, jnp.concatenate(scaled, axis=1).astype(bf16), preferred_element_type=f32)
    places = heads[:n_row, :width] + heads[n_row : 2 * n_row, :width]
    packed = heads[2 * n_row :, width:] * place_range(owned) + places
    both = jnp.dot(to_slots.astype(bf16), two_parts(whole), preferred_element_type=f32)
    body = both[:, :TILE] + both[:, TILE:]
    top = -(-head_rows // 8) * 8
    line = iota((top, TILE), 0)
    for o in range(n_row):
        head = jnp.where(line == chunks, too_many, body[o * SLOTS : o * SLOTS + top])
        for c in range(chunks):
            head = jnp.where(line == c, packed[o : o + 1, c * TILE : (c + 1) * TILE], head)
        rows_of = body[o * SLOTS + top : (o + 1) * SLOTS]
        out_ref[o] = jnp.concatenate([head, rows_of], axis=0).astype(i32).astype(i16)
    for copy in later:
        copy.wait()


def place_range(owned):
    return 1 << owned.bit_length()


def primal_kernel(
    payloads, primal_ref, cost_ref, lower_ref, upper_ref, kind_ref, steps_ref, next_hbm, flag_ref, *refs
):
    wanted, next_ref, extrap, sem = refs
    n_row = payloads.shape[0]
    chunks, head_rows = rounds_of(n_row)
    blocks = primal_ref.shape[0]
    padded = extrap.shape[0]
    wholes = [payloads[s].astype(i32) for s in range(n_row)]
    top = -(-head_rows // 8) * 8
    head = sum(w[:top] for w in wholes)
    flag_ref[...] = jnp.broadcast_to(head[chunks:head_rows], flag_ref.shape)
    whole = padded_rows(wholes, chunks * TILE)
    down = iota((blocks, TILE), 0) + 1
    places = jnp.bitwise_and(head, place_range(blocks) - 1)
    scales = lax.shift_right_arithmetic(head, blocks.bit_length())
    masks, wholes = [], []
    for c in range(chunks):
        masks.append(scaled_mask(down, places[c : c + 1], scales[c : c + 1]))
        wholes.append(whole[c * TILE : (c + 1) * TILE])
    col_sums = picked_sums(masks, wholes)
    primal = primal_ref[...]
    kind = kind_ref[...]
    moved = primal - steps_ref[0] * (cost_ref[...] - col_sums)
    moved = jnp.where(kind % 2 == 1, jnp.maximum(moved, lower_ref[...]), moved)
    moved = jnp.where(kind >= 2, jnp.minimum(moved, upper_ref[...]), moved)
    next_ref[...] = moved
    copy = pltpu.make_async_copy(next_ref, next_hbm, sem)
    copy.start()
    aligned = blocks // 8 * 8
    if padded > aligned:
        extrap[pl.ds(aligned, padded - aligned), :] = jnp.zeros((padded - aligned, TILE), f32)
    extrap[pl.ds(0, blocks), :] = 2.0 * moved - primal
    right = extrap[...].astype(bf16)
    across = iota((TILE, padded), 1) + 1
    places = jnp.transpose(places.astype(f32)).astype(i32)
    sent = [
        jnp.dot(where_one(across == places[:, c : c + 1]).astype(bf16), right, preferred_element_type=f32)
        for c in range(chunks)
    ]
    sent = jnp.concatenate(sent, axis=0)
    for s in range(n_row):
        wanted[s] = sent[s * SLOTS : (s + 1) * SLOTS].astype(bf16)
    copy.wait()


def product_kernel(*refs):
    (rows_ref, slot_ref, tiles_ref, arrived, flag_ref), others_hbm, refs = refs[:5], refs[5:7], refs[7:]
    out_ref, others, sems = refs[0], refs[1:3], refs[3]
    later = started(others_hbm, others, sems)
    k_tiles = tiles_ref.shape[0]
    chunks, _ = rounds_of(arrived.shape[0])
    blocks = [arrived[s].astype(f32) for s in range(arrived.shape[0])]
    received = padded_rows(blocks, chunks * TILE).astype(bf16)
    across = iota((k_tiles, received.shape[0]), 1)
    slots = jnp.concatenate([slot_ref[...]] * (received.shape[0] // TILE), axis=1)
    block = jnp.dot(where_one(across == slots).astype(bf16), received, preferred_element_type=f32)
    down = jnp.transpose(block)
    lane = iota((TILE, k_tiles), 1)
    right = jnp.concatenate(
        [jnp.where(lane % 2 == 0, down, 0.0), jnp.where(lane % 2 == 1, down, 0.0)], axis=0
    ).astype(bf16)
    terms = jnp.zeros((TILE, k_tiles), f32)
    for g in range(k_tiles // 8):
        even = jnp.concatenate([tiles_ref[8 * g + m] for m in (0, 2, 4, 6)], axis=0)
        odd = jnp.concatenate([tiles_ref[8 * g + m] for m in (1, 3, 5, 7)], axis=0)
        products = jnp.dot(jnp.concatenate([even, odd], axis=1), right, preferred_element_type=f32)
        for p in range(4):
            terms = jnp.where(lane // 2 == 4 * g + p, products[p * TILE : (p + 1) * TILE], terms)
    whole, exponents = coded(jnp.transpose(terms))
    out_ref[pl.ds(0, k_tiles), :] = whole.astype(i16)
    line = iota((HEAD, TILE), 0)
    head = jnp.where(line == 0, rows_ref[...], jnp.transpose(exponents)[0:HEAD, :].astype(i32))
    head = jnp.where(line == 2, flag_ref[0:1, :], head)
    out_ref[pl.ds(k_tiles, HEAD), :] = head.astype(i16)
    for copy in later:
        copy.wait()


def coded_rows(payloads):
    k_tiles = payloads[0].shape[0] - HEAD
    heads = [payload[pl.ds(k_tiles, HEAD), :].astype(i32) for payload in payloads]
    rows = [two_parts(payload[pl.ds(0, k_tiles), :].astype(i32)) for payload in payloads]
    return heads, jnp.concatenate(rows, axis=0)


def row_sums_of(heads, rows, first, blocks):
    down = iota((blocks, TILE), 0) + first
    masks = [scaled_mask(down, head[0:1], head[1:2]) for head in heads]
    both = jnp.dot(jnp.concatenate(masks, axis=1).astype(bf16), rows, preferred_element_type=f32)
    return both[:, :TILE] + both[:, TILE:]


def own_dual_kernel(payload, duals_ref, right_ref, steps_ref, part_ref):
    row_sums = row_sums_of(*coded_rows([payload]), 0, duals_ref.shape[0])
    part_ref[...] = duals_ref[...] + steps_ref[1] * (right_ref[...] - row_sums)


def dual_kernel(*refs):
    payloads, (part_ref, kind_ref, steps_ref, next_hbm, flag_ref, next_ref, sems) = refs[:-7], refs[-7:]
    heads, rows = coded_rows(payloads)
    flag_ref[0] = jnp.max(sum(head[2:3] for head in heads))
    blocks = part_ref.shape[0]
    half = blocks // 16 * 8
    copies = []
    for n, (first, count) in enumerate([(0, half), (half, blocks - half)]):
        here = pl.ds(first, count)
        updated = part_ref[here, :] - steps_ref[1] * row_sums_of(heads, rows, first, count)
        next_ref[here, :] = jnp.where(kind_ref[here, :] == 1, jnp.maximum(updated, 0.0), updated)
        copies.append(pltpu.make_async_copy(next_ref.at[here], next_hbm.at[here], sems.at[n]))
        copies[-1].start()
    for copy in copies:
        copy.wait()


def partners(axis):
    size = lax.axis_size(axis)
    if size & (size - 1) == 0:
        there = [[(i, i ^ n) for i in range(size)] for n in range(1, size)]
    else:
        there = [[(i, (i + n) % size) for i in range(size)] for n in range(1, size)]
    return [(pairs, [(j, i) for i, j in pairs]) for pairs in there]


def gathered_along(array, axis):
    return [array] + [lax.ppermute(array, axis, there) for there, _ in partners(axis)]


def sums_at(places, terms, blocks):
    mask = (jnp.arange(blocks)[:, None] == jnp.concatenate(places)[None, :]).astype(f32)
    return jnp.dot(mask, jnp.concatenate(terms), precision=lax.Precision.HIGHEST).reshape(-1)


def full_step(
    tiles, rows, cols, primal, duals, cost_vec, lower_bound, upper_bound, bound_kind, right_side, row_kind, steps
):
    col_blocks = primal.shape[0] // TILE
    row_blocks = duals.shape[0] // TILE
    wide = tiles.astype(f32)
    dual_blocks = duals.astype(bf16).astype(f32).reshape(row_blocks, TILE)[rows]
    col_terms = jnp.einsum("kij,ki->kj", wide, dual_blocks)
    first = lax.axis_index("row") * col_blocks
    places = [there - first for there in gathered_along(cols, "row")]
    places = [jnp.where((p >= 0) & (p < col_blocks), p, col_blocks) for p in places]
    col_sums = sums_at(places, gathered_along(col_terms, "row"), col_blocks)
    moved = primal - steps[0] * (cost_vec - col_sums)
    moved = jnp.where(bound_kind % 2 == 1, jnp.maximum(moved, lower_bound), moved)
    moved = jnp.where(bound_kind >= 2, jnp.minimum(moved, upper_bound), moved)
    extrap = (2.0 * moved - primal).astype(bf16).reshape(col_blocks, TILE)
    wanted = [
        jnp.where((p < col_blocks)[:, None], extrap[jnp.minimum(p, col_blocks - 1)], jnp.zeros((), bf16))
        for p in places
    ]
    blocks = wanted[0].astype(f32)
    for block, (_, back) in zip(wanted[1:], partners("row")):
        blocks += lax.ppermute(block, "row", back).astype(f32)
    row_terms = jnp.einsum("kij,kj->ki", wide, blocks)
    row_sums = sums_at(gathered_along(rows, "col"), gathered_along(row_terms, "col"), row_blocks)
    updated = duals + steps[1] * (right_side - row_sums)
    return moved, jnp.where(row_kind == 1, jnp.maximum(updated, 0.0), updated)


def local(
    block_tiles,
    tile_row,
    tile_col,
    primal,
    duals,
    cost_vec,
    lower_bound,
    upper_bound,
    bound_kind,
    right_side,
    row_kind,
    step_sizes,
):
    k_tiles = block_tiles.shape[2]
    tiles = block_tiles.reshape(k_tiles, TILE, TILE)
    rows = tile_row.reshape(-1)
    cols = tile_col.reshape(-1)
    n_row = lax.axis_size("row")
    n_col = lax.axis_size("col")
    col_blocks = primal.shape[0] // TILE
    row_blocks = duals.shape[0] // TILE
    padded = -(-col_blocks // TILE) * TILE
    in_hbm = lambda array: pltpu.with_memory_space_constraint(array, pltpu.HBM)
    by_block = lambda array: in_hbm(array.reshape(-1, TILE))
    shape_of = lambda array: jax.ShapeDtypeStruct(array.shape, array.dtype)
    params = pltpu.CompilerParams(vmem_limit_bytes=32 * 1024 * 1024)
    primal_side = [by_block(a) for a in (primal, cost_vec, lower_bound, upper_bound, bound_kind)]
    dual_side = [by_block(a) for a in (right_side, row_kind)]
    own = [by_block(duals), in_hbm(tiles)]

    col_terms, slots, duals_kept, tiles_kept, *primal_kept = pl.pallas_call(
        functools.partial(transpose_product_kernel, col_blocks),
        out_shape=(
            jax.ShapeDtypeStruct((n_row, SLOTS, TILE), i16),
            jax.ShapeDtypeStruct((k_tiles, TILE), i32),
            *[shape_of(a) for a in own + primal_side],
        ),
        in_specs=[HBM] * 9,
        out_specs=(VMEM,) * 9,
        scratch_shapes=[
            pltpu.SMEM((k_tiles,), i32),
            pltpu.VMEM((1, k_tiles), i32),
            pltpu.VMEM((k_tiles, TILE), f32),
            pltpu.SemaphoreType.DMA((3,)),
            pltpu.SemaphoreType.DMA((k_tiles // CHUNK,)),
            pltpu.SemaphoreType.DMA((5,)),
        ],
        compiler_params=params,
        name="transpose_product",
    )(in_hbm(rows), in_hbm(cols.reshape(1, k_tiles)), *own, *primal_side)
    primal_next, flag, wanted = pl.pallas_call(
        primal_kernel,
        out_shape=(
            jax.ShapeDtypeStruct((col_blocks, TILE), f32),
            jax.ShapeDtypeStruct((8, TILE), i32),
            jax.ShapeDtypeStruct((n_row, SLOTS, TILE), bf16),
        ),
        in_specs=[VMEM] * 6 + [SMEM],
        out_specs=(HBM, VMEM, VMEM),
        scratch_shapes=[
            pltpu.VMEM((col_blocks, TILE), f32),
            pltpu.VMEM((padded, TILE), f32),
            pltpu.SemaphoreType.DMA,
        ],
        compiler_params=params,
        name="primal_step",
    )(lax.all_to_all(col_terms, "row", 0, 0), *primal_kept, step_sizes)
    row_terms, *dual_kept = pl.pallas_call(
        product_kernel,
        out_shape=(
            jax.ShapeDtypeStruct((k_tiles + HEAD, TILE), i16),
            *[shape_of(a) for a in dual_side],
        ),
        in_specs=[VMEM] * 5 + [HBM] * 2,
        out_specs=(VMEM,) * 3,
        scratch_shapes=[pltpu.SemaphoreType.DMA((2,))],
        compiler_params=params,
        name="product",
    )(rows.reshape(1, k_tiles), slots, tiles_kept, lax.all_to_all(wanted, "row", 0, 0), flag, *dual_side)
    _, *others = gathered_along(row_terms, "col")
    part = pl.pallas_call(
        own_dual_kernel,
        out_shape=jax.ShapeDtypeStruct((row_blocks, TILE), f32),
        in_specs=[VMEM] * 3 + [SMEM],
        out_specs=VMEM,
        compiler_params=params,
        cost_estimate=pl.CostEstimate(flops=4 * row_blocks * k_tiles * TILE, bytes_accessed=2**20, transcendentals=0),
        name="own_dual_step",
    )(row_terms, duals_kept, dual_kept[0], step_sizes)
    dual_next, too_many = pl.pallas_call(
        dual_kernel,
        out_shape=(jax.ShapeDtypeStruct((row_blocks, TILE), f32), jax.ShapeDtypeStruct((1,), i32)),
        in_specs=[VMEM] * (n_col + 1) + [SMEM],
        out_specs=(HBM, SMEM),
        scratch_shapes=[pltpu.VMEM((row_blocks, TILE), f32), pltpu.SemaphoreType.DMA((2,))],
        compiler_params=params,
        name="dual_step",
    )(*others, part, dual_kept[1], step_sizes)
    vectors = (primal, duals, cost_vec, lower_bound, upper_bound, bound_kind, right_side, row_kind, step_sizes)
    return lax.cond(
        too_many[0] > 0,
        lambda done: full_step(tiles, rows, cols, *vectors),
        lambda done: done,
        (primal_next.reshape(-1), dual_next.reshape(-1)),
    )


def solution(mesh):
    return jax.shard_map(
        local,
        mesh=mesh,
        in_specs=(
            P("row", "col", None, None, None),
            P("row", "col", None),
            P("row", "col", None),
            P(("col", "row")),
            P("row"),
            P(("col", "row")),
            P(("col", "row")),
            P(("col", "row")),
            P(("col", "row")),
            P("row"),
            P("row"),
            P(),
        ),
        out_specs=(P(("col", "row")), P("row")),
        check_vma=False,
    )
```

```python
import functools
import jax
import jax.numpy as jnp
from jax import lax
from jax.experimental import pallas as pl
from jax.experimental.pallas import tpu as pltpu
from jax.sharding import PartitionSpec as P

TILE = 128
GROUP = 16
CHUNK = 64
SLOTS = 40
HEAD = 16
BITS = 14
LEAST = -60

f32 = jnp.float32
bf16 = jnp.bfloat16
i32 = jnp.int32
i16 = jnp.int16
VMEM = pl.BlockSpec(memory_space=pltpu.VMEM)
SMEM = pl.BlockSpec(memory_space=pltpu.SMEM)
HBM = pl.BlockSpec(memory_space=pltpu.HBM)


def iota(shape, axis):
    return lax.broadcasted_iota(i32, shape, axis)


def where_one(condition):
    return jnp.where(condition, 1.0, 0.0)


def one_row_of(block, position):
    return jnp.where(iota(block.shape, 0) == position, block, 0.0).astype(bf16)


def rounds_of(n_row):
    chunks = -(-n_row * SLOTS // TILE)
    return chunks, chunks + 1


def coded(values):
    largest = jnp.maximum(jnp.max(jnp.abs(values), axis=1, keepdims=True), 1e-30)
    exponent = jnp.maximum(jnp.ceil(jnp.log2(largest)), LEAST)
    whole = jnp.floor(values * jnp.exp2(BITS - exponent) + 0.5).astype(i32)
    return whole, jnp.broadcast_to(exponent, values.shape)


def two_parts(whole):
    low = jnp.bitwise_and(whole, 255)
    parts = [(whole - low).astype(f32), low.astype(f32)]
    return jnp.concatenate(parts, axis=1).astype(bf16)


def picked_sums(masks, wholes):
    left = masks[0] if len(masks) == 1 else jnp.concatenate(masks, axis=1)
    both = jnp.dot(
        left.astype(bf16),
        jnp.concatenate([two_parts(w) for w in wholes], axis=0),
        preferred_element_type=f32,
    )
    return both[:, :TILE] + both[:, TILE:]


def scaled_mask(down, places, exponents):
    return jnp.where(down == places, jnp.exp2(exponents.astype(f32) - BITS), 0.0)


def padded_rows(blocks, rows):
    missing = rows - sum(b.shape[0] for b in blocks)
    return jnp.concatenate(blocks + [jnp.zeros((missing, TILE), blocks[0].dtype)] * (missing > 0), axis=0)


def started(sources, targets, sems):
    copies = [
        pltpu.make_async_copy(source, target, sems.at[n])
        for n, (source, target) in enumerate(zip(sources, targets))
    ]
    for copy in copies:
        copy.start()
    return copies


def transpose_product_kernel(owned, *refs):
    (rows_hbm, cols_hbm, duals_hbm, tiles_hbm), (out_ref, slot_ref, duals, tiles), refs = refs[:4], refs[4:8], refs[8:]
    rows, cols, picked, small_sems, tile_sems = refs
    n_row = out_ref.shape[0]
    chunks, head_rows = rounds_of(n_row)
    most = SLOTS - head_rows
    k_tiles = tiles.shape[0]
    groups = [pl.ds(g * CHUNK, CHUNK) for g in range(k_tiles // CHUNK)]
    small = started([cols_hbm, rows_hbm, duals_hbm], [cols, rows, duals], small_sems)
    large = started([tiles_hbm.at[g] for g in groups], [tiles.at[g] for g in groups], tile_sems)

    for copy in small:
        copy.wait()
    for k in range(k_tiles):
        picked[pl.ds(k, 1), :] = duals[pl.ds(rows[k], 1), :]

    terms = []

    def products_of(chunk):
        large[chunk].wait()
        for first in range(chunk * CHUNK, (chunk + 1) * CHUNK, GROUP):
            group = pl.ds(first, GROUP)
            block = picked[group, :].astype(bf16).astype(f32)
            left = jnp.concatenate([one_row_of(block, m) for m in range(GROUP)], axis=1)
            terms.append(
                jnp.dot(left, tiles[group].reshape(GROUP * TILE, TILE), preferred_element_type=f32)
            )

    products_of(0)

    square = (k_tiles, k_tiles)
    col_across = cols[...]
    col_down = jnp.transpose(jnp.broadcast_to(col_across.astype(f32), square)).astype(i32)
    owner_across = sum((col_across >= o * owned).astype(i32) for o in range(1, n_row))
    owner_down = sum((col_down >= o * owned).astype(i32) for o in range(1, n_row))
    same = owner_down == owner_across
    earlier_down = iota(square, 0) < iota(square, 1)
    earlier_across = iota(square, 1) < iota(square, 0)
    rank_across = jnp.sum(where_one(same & earlier_down), axis=0, keepdims=True).astype(i32)
    rank_down = jnp.sum(where_one(same & earlier_across), axis=1, keepdims=True).astype(i32)
    slot_across = jnp.where(rank_across < most, owner_across * SLOTS + head_rows + rank_across, -1)
    slot_down = jnp.where(rank_down < most, owner_down * SLOTS + head_rows + rank_down, -1)
    slot_ref[...] = slot_down
    too_many = where_one(jnp.max(rank_across, axis=1, keepdims=True) >= most)
    to_slots = where_one(iota((n_row * SLOTS, k_tiles), 0) == slot_across)
    here = jnp.where(rank_down < most, lax.axis_index("row") * SLOTS + head_rows + rank_down, -1)
    width = chunks * TILE
    to_lanes = where_one(iota((k_tiles, width), 1) == here)
    of_owner = where_one(iota((n_row, k_tiles), 0) == owner_across)
    place = col_across - owner_across * owned + 1
    place_low = jnp.bitwise_and(place, 255)
    head_left = jnp.concatenate(
        [of_owner * (place - place_low).astype(f32), of_owner * place_low.astype(f32), of_owner], axis=0
    ).astype(bf16)

    for chunk in range(1, len(large)):
        products_of(chunk)
    whole, exponents = coded(jnp.concatenate(terms, axis=0))

    scaled = [to_lanes, to_lanes * jnp.concatenate([exponents] * chunks, axis=1)]
    heads = jnp.dot(head_left, jnp.concatenate(scaled, axis=1).astype(bf16), preferred_element_type=f32)
    places = heads[:n_row, :width] + heads[n_row : 2 * n_row, :width]
    packed = heads[2 * n_row :, width:] * place_range(owned) + places
    both = jnp.dot(to_slots.astype(bf16), two_parts(whole), preferred_element_type=f32)
    body = both[:, :TILE] + both[:, TILE:]
    top = -(-head_rows // 8) * 8
    line = iota((top, TILE), 0)
    for o in range(n_row):
        head = jnp.where(line == chunks, too_many, body[o * SLOTS : o * SLOTS + top])
        for c in range(chunks):
            head = jnp.where(line == c, packed[o : o + 1, c * TILE : (c + 1) * TILE], head)
        rows_of = body[o * SLOTS + top : (o + 1) * SLOTS]
        out_ref[o] = jnp.concatenate([head, rows_of], axis=0).astype(i32).astype(i16)


def place_range(owned):
    return 1 << owned.bit_length()


def primal_kernel(
    payloads, primal_ref, cost_ref, lower_ref, upper_ref, kind_ref, steps_ref, next_hbm, flag_ref, *refs
):
    wanted, next_ref, extrap, sem = refs
    n_row = payloads.shape[0]
    chunks, head_rows = rounds_of(n_row)
    blocks = primal_ref.shape[0]
    padded = extrap.shape[0]
    wholes = [payloads[s].astype(i32) for s in range(n_row)]
    top = -(-head_rows // 8) * 8
    head = sum(w[:top] for w in wholes)
    flag_ref[...] = jnp.broadcast_to(head[chunks:head_rows], flag_ref.shape)
    whole = padded_rows(wholes, chunks * TILE)
    down = iota((blocks, TILE), 0) + 1
    places = jnp.bitwise_and(head, place_range(blocks) - 1)
    scales = lax.shift_right_arithmetic(head, blocks.bit_length())
    masks, wholes = [], []
    for c in range(chunks):
        masks.append(scaled_mask(down, places[c : c + 1], scales[c : c + 1]))
        wholes.append(whole[c * TILE : (c + 1) * TILE])
    col_sums = picked_sums(masks, wholes)
    primal = primal_ref[...]
    kind = kind_ref[...]
    moved = primal - steps_ref[0] * (cost_ref[...] - col_sums)
    moved = jnp.where(kind % 2 == 1, jnp.maximum(moved, lower_ref[...]), moved)
    moved = jnp.where(kind >= 2, jnp.minimum(moved, upper_ref[...]), moved)
    next_ref[...] = moved
    copy = pltpu.make_async_copy(next_ref, next_hbm, sem)
    copy.start()
    aligned = blocks // 8 * 8
    if padded > aligned:
        extrap[pl.ds(aligned, padded - aligned), :] = jnp.zeros((padded - aligned, TILE), f32)
    extrap[pl.ds(0, blocks), :] = 2.0 * moved - primal
    right = extrap[...].astype(bf16)
    across = iota((TILE, padded), 1) + 1
    places = jnp.transpose(places.astype(f32)).astype(i32)
    sent = [
        jnp.dot(where_one(across == places[:, c : c + 1]).astype(bf16), right, preferred_element_type=f32)
        for c in range(chunks)
    ]
    sent = jnp.concatenate(sent, axis=0)
    for s in range(n_row):
        wanted[s] = sent[s * SLOTS : (s + 1) * SLOTS].astype(bf16)
    copy.wait()


def product_kernel(*refs):
    (rows_ref, slot_ref, tiles_ref, arrived, flag_ref), others_hbm, refs = refs[:5], refs[5:7], refs[7:]
    out_ref, others, sems = refs[0], refs[1:3], refs[3]
    later = started(others_hbm, others, sems)
    k_tiles = tiles_ref.shape[0]
    chunks, _ = rounds_of(arrived.shape[0])
    blocks = [arrived[s].astype(f32) for s in range(arrived.shape[0])]
    received = padded_rows(blocks, chunks * TILE).astype(bf16)
    across = iota((k_tiles, received.shape[0]), 1)
    slots = jnp.concatenate([slot_ref[...]] * (received.shape[0] // TILE), axis=1)
    block = jnp.dot(where_one(across == slots).astype(bf16), received, preferred_element_type=f32)
    down = jnp.transpose(block)
    lane = iota((TILE, k_tiles), 1)
    right = jnp.concatenate(
        [jnp.where(lane % 2 == 0, down, 0.0), jnp.where(lane % 2 == 1, down, 0.0)], axis=0
    ).astype(bf16)
    terms = jnp.zeros((TILE, k_tiles), f32)
    for g in range(k_tiles // 8):
        even = jnp.concatenate([tiles_ref[8 * g + m] for m in (0, 2, 4, 6)], axis=0)
        odd = jnp.concatenate([tiles_ref[8 * g + m] for m in (1, 3, 5, 7)], axis=0)
        products = jnp.dot(jnp.concatenate([even, odd], axis=1), right, preferred_element_type=f32)
        for p in range(4):
            terms = jnp.where(lane // 2 == 4 * g + p, products[p * TILE : (p + 1) * TILE], terms)
    whole, exponents = coded(jnp.transpose(terms))
    out_ref[pl.ds(0, k_tiles), :] = whole.astype(i16)
    line = iota((HEAD, TILE), 0)
    head = jnp.where(line == 0, rows_ref[...], jnp.transpose(exponents)[0:HEAD, :].astype(i32))
    head = jnp.where(line == 2, flag_ref[0:1, :], head)
    out_ref[pl.ds(k_tiles, HEAD), :] = head.astype(i16)
    for copy in later:
        copy.wait()


def row_sums_of(payloads, blocks):
    k_tiles = payloads[0].shape[0] - HEAD
    down = iota((blocks, k_tiles), 0)
    masks, wholes = [], []
    flags = jnp.zeros((1, TILE), i32)
    for payload in payloads:
        head = payload[pl.ds(k_tiles, HEAD), :].astype(i32)
        masks.append(scaled_mask(down, head[0:1], head[1:2]))
        wholes.append(payload[pl.ds(0, k_tiles), :].astype(i32))
        flags += head[2:3]
    return picked_sums(masks, wholes), flags


def own_dual_kernel(payload, duals_ref, right_ref, steps_ref, part_ref):
    row_sums, _ = row_sums_of([payload], duals_ref.shape[0])
    part_ref[...] = duals_ref[...] + steps_ref[1] * (right_ref[...] - row_sums)


def dual_kernel(*refs):
    payloads, (part_ref, kind_ref, steps_ref, next_ref, flag_ref) = refs[:-5], refs[-5:]
    row_sums, flags = row_sums_of(payloads, part_ref.shape[0])
    updated = part_ref[...] - steps_ref[1] * row_sums
    next_ref[...] = jnp.where(kind_ref[...] == 1, jnp.maximum(updated, 0.0), updated)
    flag_ref[0] = jnp.max(flags)


def partners(axis):
    size = lax.axis_size(axis)
    if size & (size - 1) == 0:
        there = [[(i, i ^ n) for i in range(size)] for n in range(1, size)]
    else:
        there = [[(i, (i + n) % size) for i in range(size)] for n in range(1, size)]
    return [(pairs, [(j, i) for i, j in pairs]) for pairs in there]


def gathered_along(array, axis):
    return [array] + [lax.ppermute(array, axis, there) for there, _ in partners(axis)]


def sums_at(places, terms, blocks):
    mask = (jnp.arange(blocks)[:, None] == jnp.concatenate(places)[None, :]).astype(f32)
    return jnp.dot(mask, jnp.concatenate(terms), precision=lax.Precision.HIGHEST).reshape(-1)


def full_step(
    tiles, rows, cols, primal, duals, cost_vec, lower_bound, upper_bound, bound_kind, right_side, row_kind, steps
):
    col_blocks = primal.shape[0] // TILE
    row_blocks = duals.shape[0] // TILE
    wide = tiles.astype(f32)
    dual_blocks = duals.astype(bf16).astype(f32).reshape(row_blocks, TILE)[rows]
    col_terms = jnp.einsum("kij,ki->kj", wide, dual_blocks)
    first = lax.axis_index("row") * col_blocks
    places = [there - first for there in gathered_along(cols, "row")]
    places = [jnp.where((p >= 0) & (p < col_blocks), p, col_blocks) for p in places]
    col_sums = sums_at(places, gathered_along(col_terms, "row"), col_blocks)
    moved = primal - steps[0] * (cost_vec - col_sums)
    moved = jnp.where(bound_kind % 2 == 1, jnp.maximum(moved, lower_bound), moved)
    moved = jnp.where(bound_kind >= 2, jnp.minimum(moved, upper_bound), moved)
    extrap = (2.0 * moved - primal).astype(bf16).reshape(col_blocks, TILE)
    wanted = [
        jnp.where((p < col_blocks)[:, None], extrap[jnp.minimum(p, col_blocks - 1)], jnp.zeros((), bf16))
        for p in places
    ]
    blocks = wanted[0].astype(f32)
    for block, (_, back) in zip(wanted[1:], partners("row")):
        blocks += lax.ppermute(block, "row", back).astype(f32)
    row_terms = jnp.einsum("kij,kj->ki", wide, blocks)
    row_sums = sums_at(gathered_along(rows, "col"), gathered_along(row_terms, "col"), row_blocks)
    updated = duals + steps[1] * (right_side - row_sums)
    return moved, jnp.where(row_kind == 1, jnp.maximum(updated, 0.0), updated)


def local(
    block_tiles,
    tile_row,
    tile_col,
    primal,
    duals,
    cost_vec,
    lower_bound,
    upper_bound,
    bound_kind,
    right_side,
    row_kind,
    step_sizes,
):
    k_tiles = block_tiles.shape[2]
    tiles = block_tiles.reshape(k_tiles, TILE, TILE)
    rows = tile_row.reshape(-1)
    cols = tile_col.reshape(-1)
    n_row = lax.axis_size("row")
    n_col = lax.axis_size("col")
    col_blocks = primal.shape[0] // TILE
    row_blocks = duals.shape[0] // TILE
    padded = -(-col_blocks // TILE) * TILE
    in_hbm = lambda array: pltpu.with_memory_space_constraint(array, pltpu.HBM)
    by_block = lambda array: in_hbm(array.reshape(-1, TILE))
    shape_of = lambda array: jax.ShapeDtypeStruct(array.shape, array.dtype)
    params = pltpu.CompilerParams(vmem_limit_bytes=32 * 1024 * 1024)
    primal_side = [a.reshape(-1, TILE) for a in (primal, cost_vec, lower_bound, upper_bound, bound_kind)]
    dual_side = [by_block(a) for a in (right_side, row_kind)]
    own = [by_block(duals), in_hbm(tiles)]

    col_terms, slots, duals_kept, tiles_kept = pl.pallas_call(
        functools.partial(transpose_product_kernel, col_blocks),
        out_shape=(
            jax.ShapeDtypeStruct((n_row, SLOTS, TILE), i16),
            jax.ShapeDtypeStruct((k_tiles, TILE), i32),
            *[shape_of(a) for a in own],
        ),
        in_specs=[HBM] * 4,
        out_specs=(VMEM,) * 4,
        scratch_shapes=[
            pltpu.SMEM((k_tiles,), i32),
            pltpu.VMEM((1, k_tiles), i32),
            pltpu.VMEM((k_tiles, TILE), f32),
            pltpu.SemaphoreType.DMA((3,)),
            pltpu.SemaphoreType.DMA((k_tiles // CHUNK,)),
        ],
        compiler_params=params,
        name="transpose_product",
    )(in_hbm(rows), in_hbm(cols.reshape(1, k_tiles)), *own)
    primal_next, flag, wanted = pl.pallas_call(
        primal_kernel,
        out_shape=(
            jax.ShapeDtypeStruct((col_blocks, TILE), f32),
            jax.ShapeDtypeStruct((8, TILE), i32),
            jax.ShapeDtypeStruct((n_row, SLOTS, TILE), bf16),
        ),
        in_specs=[VMEM] * 6 + [SMEM],
        out_specs=(HBM, VMEM, VMEM),
        scratch_shapes=[
            pltpu.VMEM((col_blocks, TILE), f32),
            pltpu.VMEM((padded, TILE), f32),
            pltpu.SemaphoreType.DMA,
        ],
        compiler_params=params,
        name="primal_step",
    )(lax.all_to_all(col_terms, "row", 0, 0), *primal_side, step_sizes)
    row_terms, *dual_kept = pl.pallas_call(
        product_kernel,
        out_shape=(
            jax.ShapeDtypeStruct((k_tiles + HEAD, TILE), i16),
            *[shape_of(a) for a in dual_side],
        ),
        in_specs=[VMEM] * 5 + [HBM] * 2,
        out_specs=(VMEM,) * 3,
        scratch_shapes=[pltpu.SemaphoreType.DMA((2,))],
        compiler_params=params,
        name="product",
    )(rows.reshape(1, k_tiles), slots, tiles_kept, lax.all_to_all(wanted, "row", 0, 0), flag, *dual_side)
    _, *others = gathered_along(row_terms, "col")
    part = pl.pallas_call(
        own_dual_kernel,
        out_shape=jax.ShapeDtypeStruct((row_blocks, TILE), f32),
        in_specs=[VMEM] * 3 + [SMEM],
        out_specs=VMEM,
        compiler_params=params,
        cost_estimate=pl.CostEstimate(flops=4 * row_blocks * k_tiles * TILE, bytes_accessed=2**20, transcendentals=0),
        name="own_dual_step",
    )(row_terms, duals_kept, dual_kept[0], step_sizes)
    dual_next, too_many = pl.pallas_call(
        dual_kernel,
        out_shape=(jax.ShapeDtypeStruct((row_blocks, TILE), f32), jax.ShapeDtypeStruct((1,), i32)),
        in_specs=[VMEM] * (n_col + 1) + [SMEM],
        out_specs=(VMEM, SMEM),
        compiler_params=params,
        name="dual_step",
    )(*others, part, dual_kept[1], step_sizes)
    vectors = (primal, duals, cost_vec, lower_bound, upper_bound, bound_kind, right_side, row_kind, step_sizes)
    return lax.cond(
        too_many[0] > 0,
        lambda done: full_step(tiles, rows, cols, *vectors),
        lambda done: done,
        (primal_next.reshape(-1), dual_next.reshape(-1)),
    )


def solution(mesh):
    return jax.shard_map(
        local,
        mesh=mesh,
        in_specs=(
            P("row", "col", None, None, None),
            P("row", "col", None),
            P("row", "col", None),
            P(("col", "row")),
            P("row"),
            P(("col", "row")),
            P(("col", "row")),
            P(("col", "row")),
            P(("col", "row")),
            P("row"),
            P("row"),
            P(),
        ),
        out_specs=(P(("col", "row")), P("row")),
        check_vma=False,
    )
```

```python
import functools
import jax
import jax.numpy as jnp
from jax import lax
from jax.experimental import pallas as pl
from jax.experimental.pallas import tpu as pltpu
from jax.sharding import PartitionSpec as P

TILE = 128
GROUP = 16
CHUNK = 64
SLOTS = 40
HEAD = 16
BITS = 14
LEAST = -60

f32 = jnp.float32
bf16 = jnp.bfloat16
i32 = jnp.int32
i16 = jnp.int16
VMEM = pl.BlockSpec(memory_space=pltpu.VMEM)
SMEM = pl.BlockSpec(memory_space=pltpu.SMEM)
HBM = pl.BlockSpec(memory_space=pltpu.HBM)


def iota(shape, axis):
    return lax.broadcasted_iota(i32, shape, axis)


def where_one(condition):
    return jnp.where(condition, 1.0, 0.0)


def one_row_of(block, position):
    return jnp.where(iota(block.shape, 0) == position, block, 0.0).astype(bf16)


def rounds_of(n_row):
    chunks = -(-n_row * SLOTS // TILE)
    return chunks, chunks + 1


def coded(values):
    largest = jnp.maximum(jnp.max(jnp.abs(values), axis=1, keepdims=True), 1e-30)
    exponent = jnp.maximum(jnp.ceil(jnp.log2(largest)), LEAST)
    whole = jnp.floor(values * jnp.exp2(BITS - exponent) + 0.5).astype(i32)
    return whole, jnp.broadcast_to(exponent, values.shape)


def two_parts(whole):
    low = jnp.bitwise_and(whole, 255)
    parts = [(whole - low).astype(f32), low.astype(f32)]
    return jnp.concatenate(parts, axis=1).astype(bf16)


def picked_sums(masks, wholes):
    left = masks[0] if len(masks) == 1 else jnp.concatenate(masks, axis=1)
    both = jnp.dot(
        left.astype(bf16),
        jnp.concatenate([two_parts(w) for w in wholes], axis=0),
        preferred_element_type=f32,
    )
    return both[:, :TILE] + both[:, TILE:]


def scaled_mask(down, places, exponents):
    return jnp.where(down == places, jnp.exp2(exponents.astype(f32) - BITS), 0.0)


def padded_rows(blocks, rows):
    missing = rows - sum(b.shape[0] for b in blocks)
    return jnp.concatenate(blocks + [jnp.zeros((missing, TILE), blocks[0].dtype)] * (missing > 0), axis=0)


def started(sources, targets, sems):
    copies = [
        pltpu.make_async_copy(source, target, sems.at[n])
        for n, (source, target) in enumerate(zip(sources, targets))
    ]
    for copy in copies:
        copy.start()
    return copies


def transpose_product_kernel(owned, *refs):
    (rows_hbm, cols_hbm, duals_hbm, tiles_hbm), (out_ref, slot_ref, duals, tiles), refs = refs[:4], refs[4:8], refs[8:]
    rows, cols, picked, small_sems, tile_sems = refs
    n_row = out_ref.shape[0]
    chunks, head_rows = rounds_of(n_row)
    most = SLOTS - head_rows
    k_tiles = tiles.shape[0]
    groups = [pl.ds(g * CHUNK, CHUNK) for g in range(k_tiles // CHUNK)]
    small = started([cols_hbm, rows_hbm, duals_hbm], [cols, rows, duals], small_sems)
    large = started([tiles_hbm.at[g] for g in groups], [tiles.at[g] for g in groups], tile_sems)

    for copy in small:
        copy.wait()
    for k in range(k_tiles):
        picked[pl.ds(k, 1), :] = duals[pl.ds(rows[k], 1), :]

    terms = []

    def products_of(chunk):
        large[chunk].wait()
        for first in range(chunk * CHUNK, (chunk + 1) * CHUNK, GROUP):
            group = pl.ds(first, GROUP)
            block = picked[group, :].astype(bf16).astype(f32)
            left = jnp.concatenate([one_row_of(block, m) for m in range(GROUP)], axis=1)
            terms.append(
                jnp.dot(left, tiles[group].reshape(GROUP * TILE, TILE), preferred_element_type=f32)
            )

    products_of(0)

    square = (k_tiles, k_tiles)
    col_across = cols[...]
    col_down = jnp.transpose(jnp.broadcast_to(col_across.astype(f32), square)).astype(i32)
    owner_across = sum((col_across >= o * owned).astype(i32) for o in range(1, n_row))
    owner_down = sum((col_down >= o * owned).astype(i32) for o in range(1, n_row))
    same = owner_down == owner_across
    earlier_down = iota(square, 0) < iota(square, 1)
    earlier_across = iota(square, 1) < iota(square, 0)
    rank_across = jnp.sum(where_one(same & earlier_down), axis=0, keepdims=True).astype(i32)
    rank_down = jnp.sum(where_one(same & earlier_across), axis=1, keepdims=True).astype(i32)
    slot_across = jnp.where(rank_across < most, owner_across * SLOTS + head_rows + rank_across, -1)
    slot_down = jnp.where(rank_down < most, owner_down * SLOTS + head_rows + rank_down, -1)
    slot_ref[...] = slot_down
    too_many = where_one(jnp.max(rank_across, axis=1, keepdims=True) >= most)
    to_slots = where_one(iota((n_row * SLOTS, k_tiles), 0) == slot_across)
    here = jnp.where(rank_down < most, lax.axis_index("row") * SLOTS + head_rows + rank_down, -1)
    width = chunks * TILE
    to_lanes = where_one(iota((k_tiles, width), 1) == here)
    of_owner = where_one(iota((n_row, k_tiles), 0) == owner_across)
    place = place_coded(col_across - owner_across * owned)
    packed = jnp.dot((of_owner * place).astype(bf16), to_lanes.astype(bf16), preferred_element_type=f32)

    for chunk in range(1, len(large)):
        products_of(chunk)
    products = jnp.concatenate(terms, axis=0).astype(bf16)
    body = jnp.dot(to_slots.astype(bf16), products, preferred_element_type=f32)
    top = -(-head_rows // 8) * 8
    line = iota((top, TILE), 0)
    for o in range(n_row):
        head = jnp.where(line == chunks, too_many, body[o * SLOTS : o * SLOTS + top])
        for c in range(chunks):
            head = jnp.where(line == c, packed[o : o + 1, c * TILE : (c + 1) * TILE], head)
        rows_of = body[o * SLOTS + top : (o + 1) * SLOTS]
        out_ref[o] = jnp.concatenate([head, rows_of], axis=0).astype(bf16)


def place_coded(place):
    high = lax.shift_right_logical(place, 7)
    return jnp.exp2((8 * high).astype(f32)) * (128 + jnp.bitwise_and(place, 127)).astype(f32)


def place_of(number, blocks):
    place = number - 129.0 + where_one(number >= 128.0)
    for high in range(1, -(-blocks // TILE)):
        place = jnp.where(number >= 2.0 ** (7 + 8 * high), number * 2.0 ** (-8 * high) - 128.0 + 128.0 * high, place)
    return place.astype(i32)


def primal_kernel(
    payloads, primal_ref, cost_ref, lower_ref, upper_ref, kind_ref, steps_ref, next_hbm, flag_ref, *refs
):
    wanted, next_ref, extrap, sem = refs
    n_row = payloads.shape[0]
    chunks, head_rows = rounds_of(n_row)
    blocks = primal_ref.shape[0]
    padded = extrap.shape[0]
    arrived = [payloads[s].astype(f32) for s in range(n_row)]
    top = -(-head_rows // 8) * 8
    head = sum(a[:top] for a in arrived)
    flag_ref[...] = jnp.broadcast_to(head[chunks:head_rows], flag_ref.shape).astype(i32)
    places = place_of(head, blocks)
    down = iota((blocks, TILE), 0)
    masks = [where_one(down == places[c : c + 1]) for c in range(chunks)]
    col_sums = jnp.dot(
        jnp.concatenate(masks, axis=1).astype(bf16),
        padded_rows(arrived, chunks * TILE).astype(bf16),
        preferred_element_type=f32,
    )
    primal = primal_ref[...]
    kind = kind_ref[...]
    moved = primal - steps_ref[0] * (cost_ref[...] - col_sums)
    moved = jnp.where(kind % 2 == 1, jnp.maximum(moved, lower_ref[...]), moved)
    moved = jnp.where(kind >= 2, jnp.minimum(moved, upper_ref[...]), moved)
    next_ref[...] = moved
    copy = pltpu.make_async_copy(next_ref, next_hbm, sem)
    copy.start()
    aligned = blocks // 8 * 8
    if padded > aligned:
        extrap[pl.ds(aligned, padded - aligned), :] = jnp.zeros((padded - aligned, TILE), f32)
    extrap[pl.ds(0, blocks), :] = 2.0 * moved - primal
    right = extrap[...].astype(bf16)
    across = iota((TILE, padded), 1)
    places = jnp.transpose(places.astype(f32)).astype(i32)
    sent = [
        jnp.dot(where_one(across == places[:, c : c + 1]).astype(bf16), right, preferred_element_type=f32)
        for c in range(chunks)
    ]
    sent = jnp.concatenate(sent, axis=0)
    for s in range(n_row):
        wanted[s] = sent[s * SLOTS : (s + 1) * SLOTS].astype(bf16)
    copy.wait()


def product_kernel(*refs):
    (rows_ref, slot_ref, tiles_ref, arrived, flag_ref), others_hbm, refs = refs[:5], refs[5:7], refs[7:]
    out_ref, others, sems = refs[0], refs[1:3], refs[3]
    later = started(others_hbm, others, sems)
    k_tiles = tiles_ref.shape[0]
    chunks, _ = rounds_of(arrived.shape[0])
    blocks = [arrived[s].astype(f32) for s in range(arrived.shape[0])]
    received = padded_rows(blocks, chunks * TILE).astype(bf16)
    across = iota((k_tiles, received.shape[0]), 1)
    slots = jnp.concatenate([slot_ref[...]] * (received.shape[0] // TILE), axis=1)
    block = jnp.dot(where_one(across == slots).astype(bf16), received, preferred_element_type=f32)
    down = jnp.transpose(block)
    lane = iota((TILE, k_tiles), 1)
    right = jnp.concatenate(
        [jnp.where(lane % 2 == 0, down, 0.0), jnp.where(lane % 2 == 1, down, 0.0)], axis=0
    ).astype(bf16)
    terms = jnp.zeros((TILE, k_tiles), f32)
    for g in range(k_tiles // 8):
        even = jnp.concatenate([tiles_ref[8 * g + m] for m in (0, 2, 4, 6)], axis=0)
        odd = jnp.concatenate([tiles_ref[8 * g + m] for m in (1, 3, 5, 7)], axis=0)
        products = jnp.dot(jnp.concatenate([even, odd], axis=1), right, preferred_element_type=f32)
        for p in range(4):
            terms = jnp.where(lane // 2 == 4 * g + p, products[p * TILE : (p + 1) * TILE], terms)
    whole, exponents = coded(jnp.transpose(terms))
    out_ref[pl.ds(0, k_tiles), :] = whole.astype(i16)
    line = iota((HEAD, TILE), 0)
    head = jnp.where(line == 0, rows_ref[...], jnp.transpose(exponents)[0:HEAD, :].astype(i32))
    head = jnp.where(line == 2, flag_ref[0:1, :], head)
    out_ref[pl.ds(k_tiles, HEAD), :] = head.astype(i16)
    for copy in later:
        copy.wait()


def row_sums_of(payloads, blocks):
    k_tiles = payloads[0].shape[0] - HEAD
    down = iota((blocks, k_tiles), 0)
    masks, wholes = [], []
    flags = jnp.zeros((1, TILE), i32)
    for payload in payloads:
        head = payload[pl.ds(k_tiles, HEAD), :].astype(i32)
        masks.append(scaled_mask(down, head[0:1], head[1:2]))
        wholes.append(payload[pl.ds(0, k_tiles), :].astype(i32))
        flags += head[2:3]
    return picked_sums(masks, wholes), flags


def own_dual_kernel(payload, duals_ref, right_ref, steps_ref, part_ref):
    row_sums, _ = row_sums_of([payload], duals_ref.shape[0])
    part_ref[...] = duals_ref[...] + steps_ref[1] * (right_ref[...] - row_sums)


def dual_kernel(*refs):
    payloads, (part_ref, kind_ref, steps_ref, next_ref, flag_ref) = refs[:-5], refs[-5:]
    row_sums, flags = row_sums_of(payloads, part_ref.shape[0])
    updated = part_ref[...] - steps_ref[1] * row_sums
    next_ref[...] = jnp.where(kind_ref[...] == 1, jnp.maximum(updated, 0.0), updated)
    flag_ref[0] = jnp.max(flags)


def partners(axis):
    size = lax.axis_size(axis)
    if size & (size - 1) == 0:
        there = [[(i, i ^ n) for i in range(size)] for n in range(1, size)]
    else:
        there = [[(i, (i + n) % size) for i in range(size)] for n in range(1, size)]
    return [(pairs, [(j, i) for i, j in pairs]) for pairs in there]


def gathered_along(array, axis):
    return [array] + [lax.ppermute(array, axis, there) for there, _ in partners(axis)]


def sums_at(places, terms, blocks):
    mask = (jnp.arange(blocks)[:, None] == jnp.concatenate(places)[None, :]).astype(f32)
    return jnp.dot(mask, jnp.concatenate(terms), precision=lax.Precision.HIGHEST).reshape(-1)


def full_step(
    tiles, rows, cols, primal, duals, cost_vec, lower_bound, upper_bound, bound_kind, right_side, row_kind, steps
):
    col_blocks = primal.shape[0] // TILE
    row_blocks = duals.shape[0] // TILE
    wide = tiles.astype(f32)
    dual_blocks = duals.astype(bf16).astype(f32).reshape(row_blocks, TILE)[rows]
    col_terms = jnp.einsum("kij,ki->kj", wide, dual_blocks)
    first = lax.axis_index("row") * col_blocks
    places = [there - first for there in gathered_along(cols, "row")]
    places = [jnp.where((p >= 0) & (p < col_blocks), p, col_blocks) for p in places]
    col_sums = sums_at(places, gathered_along(col_terms, "row"), col_blocks)
    moved = primal - steps[0] * (cost_vec - col_sums)
    moved = jnp.where(bound_kind % 2 == 1, jnp.maximum(moved, lower_bound), moved)
    moved = jnp.where(bound_kind >= 2, jnp.minimum(moved, upper_bound), moved)
    extrap = (2.0 * moved - primal).astype(bf16).reshape(col_blocks, TILE)
    wanted = [
        jnp.where((p < col_blocks)[:, None], extrap[jnp.minimum(p, col_blocks - 1)], jnp.zeros((), bf16))
        for p in places
    ]
    blocks = wanted[0].astype(f32)
    for block, (_, back) in zip(wanted[1:], partners("row")):
        blocks += lax.ppermute(block, "row", back).astype(f32)
    row_terms = jnp.einsum("kij,kj->ki", wide, blocks)
    row_sums = sums_at(gathered_along(rows, "col"), gathered_along(row_terms, "col"), row_blocks)
    updated = duals + steps[1] * (right_side - row_sums)
    return moved, jnp.where(row_kind == 1, jnp.maximum(updated, 0.0), updated)


def local(
    block_tiles,
    tile_row,
    tile_col,
    primal,
    duals,
    cost_vec,
    lower_bound,
    upper_bound,
    bound_kind,
    right_side,
    row_kind,
    step_sizes,
):
    k_tiles = block_tiles.shape[2]
    tiles = block_tiles.reshape(k_tiles, TILE, TILE)
    rows = tile_row.reshape(-1)
    cols = tile_col.reshape(-1)
    n_row = lax.axis_size("row")
    n_col = lax.axis_size("col")
    col_blocks = primal.shape[0] // TILE
    row_blocks = duals.shape[0] // TILE
    padded = -(-col_blocks // TILE) * TILE
    in_hbm = lambda array: pltpu.with_memory_space_constraint(array, pltpu.HBM)
    by_block = lambda array: in_hbm(array.reshape(-1, TILE))
    shape_of = lambda array: jax.ShapeDtypeStruct(array.shape, array.dtype)
    params = pltpu.CompilerParams(vmem_limit_bytes=32 * 1024 * 1024)
    primal_side = [a.reshape(-1, TILE) for a in (primal, cost_vec, lower_bound, upper_bound, bound_kind)]
    dual_side = [by_block(a) for a in (right_side, row_kind)]
    own = [by_block(duals), in_hbm(tiles)]

    col_terms, slots, duals_kept, tiles_kept = pl.pallas_call(
        functools.partial(transpose_product_kernel, col_blocks),
        out_shape=(
            jax.ShapeDtypeStruct((n_row, SLOTS, TILE), bf16),
            jax.ShapeDtypeStruct((k_tiles, TILE), i32),
            *[shape_of(a) for a in own],
        ),
        in_specs=[HBM] * 4,
        out_specs=(VMEM,) * 4,
        scratch_shapes=[
            pltpu.SMEM((k_tiles,), i32),
            pltpu.VMEM((1, k_tiles), i32),
            pltpu.VMEM((k_tiles, TILE), f32),
            pltpu.SemaphoreType.DMA((3,)),
            pltpu.SemaphoreType.DMA((k_tiles // CHUNK,)),
        ],
        compiler_params=params,
        name="transpose_product",
    )(in_hbm(rows), in_hbm(cols.reshape(1, k_tiles)), *own)
    primal_next, flag, wanted = pl.pallas_call(
        primal_kernel,
        out_shape=(
            jax.ShapeDtypeStruct((col_blocks, TILE), f32),
            jax.ShapeDtypeStruct((8, TILE), i32),
            jax.ShapeDtypeStruct((n_row, SLOTS, TILE), bf16),
        ),
        in_specs=[VMEM] * 6 + [SMEM],
        out_specs=(HBM, VMEM, VMEM),
        scratch_shapes=[
            pltpu.VMEM((col_blocks, TILE), f32),
            pltpu.VMEM((padded, TILE), f32),
            pltpu.SemaphoreType.DMA,
        ],
        compiler_params=params,
        name="primal_step",
    )(lax.all_to_all(col_terms, "row", 0, 0), *primal_side, step_sizes)
    row_terms, *dual_kept = pl.pallas_call(
        product_kernel,
        out_shape=(
            jax.ShapeDtypeStruct((k_tiles + HEAD, TILE), i16),
            *[shape_of(a) for a in dual_side],
        ),
        in_specs=[VMEM] * 5 + [HBM] * 2,
        out_specs=(VMEM,) * 3,
        scratch_shapes=[pltpu.SemaphoreType.DMA((2,))],
        compiler_params=params,
        name="product",
    )(rows.reshape(1, k_tiles), slots, tiles_kept, lax.all_to_all(wanted, "row", 0, 0), flag, *dual_side)
    _, *others = gathered_along(row_terms, "col")
    part = pl.pallas_call(
        own_dual_kernel,
        out_shape=jax.ShapeDtypeStruct((row_blocks, TILE), f32),
        in_specs=[VMEM] * 3 + [SMEM],
        out_specs=VMEM,
        compiler_params=params,
        cost_estimate=pl.CostEstimate(flops=4 * row_blocks * k_tiles * TILE, bytes_accessed=2**20, transcendentals=0),
        name="own_dual_step",
    )(row_terms, duals_kept, dual_kept[0], step_sizes)
    dual_next, too_many = pl.pallas_call(
        dual_kernel,
        out_shape=(jax.ShapeDtypeStruct((row_blocks, TILE), f32), jax.ShapeDtypeStruct((1,), i32)),
        in_specs=[VMEM] * (n_col + 1) + [SMEM],
        out_specs=(VMEM, SMEM),
        compiler_params=params,
        name="dual_step",
    )(*others, part, dual_kept[1], step_sizes)
    vectors = (primal, duals, cost_vec, lower_bound, upper_bound, bound_kind, right_side, row_kind, step_sizes)
    return lax.cond(
        too_many[0] > 0,
        lambda done: full_step(tiles, rows, cols, *vectors),
        lambda done: done,
        (primal_next.reshape(-1), dual_next.reshape(-1)),
    )


def solution(mesh):
    return jax.shard_map(
        local,
        mesh=mesh,
        in_specs=(
            P("row", "col", None, None, None),
            P("row", "col", None),
            P("row", "col", None),
            P(("col", "row")),
            P("row"),
            P(("col", "row")),
            P(("col", "row")),
            P(("col", "row")),
            P(("col", "row")),
            P("row"),
            P("row"),
            P(),
        ),
        out_specs=(P(("col", "row")), P("row")),
        check_vma=False,
    )
```

```python
import functools
import jax
import jax.numpy as jnp
from jax import lax
from jax.experimental import pallas as pl
from jax.experimental.pallas import tpu as pltpu
from jax.sharding import PartitionSpec as P

TILE = 128
GROUP = 16
CHUNK = 128
SLOTS = 40
HEAD = 16
BITS = 14
LEAST = -60

f32 = jnp.float32
bf16 = jnp.bfloat16
i32 = jnp.int32
i16 = jnp.int16
VMEM = pl.BlockSpec(memory_space=pltpu.VMEM)
SMEM = pl.BlockSpec(memory_space=pltpu.SMEM)
HBM = pl.BlockSpec(memory_space=pltpu.HBM)


def iota(shape, axis):
    return lax.broadcasted_iota(i32, shape, axis)


def where_one(condition):
    return jnp.where(condition, 1.0, 0.0)


def one_row_of(block, position):
    return jnp.where(iota(block.shape, 0) == position, block, 0.0).astype(bf16)


def rounds_of(n_row):
    chunks = -(-n_row * SLOTS // TILE)
    return chunks, chunks + 1


def coded(values):
    largest = jnp.maximum(jnp.max(jnp.abs(values), axis=1, keepdims=True), 1e-30)
    exponent = jnp.maximum(jnp.ceil(jnp.log2(largest)), LEAST)
    whole = jnp.floor(values * jnp.exp2(BITS - exponent) + 0.5).astype(i32)
    return whole, jnp.broadcast_to(exponent, values.shape)


def two_parts(whole):
    low = jnp.bitwise_and(whole, 255)
    parts = [(whole - low).astype(f32), low.astype(f32)]
    return jnp.concatenate(parts, axis=1).astype(bf16)


def picked_sums(masks, wholes):
    left = masks[0] if len(masks) == 1 else jnp.concatenate(masks, axis=1)
    both = jnp.dot(
        left.astype(bf16),
        jnp.concatenate([two_parts(w) for w in wholes], axis=0),
        preferred_element_type=f32,
    )
    return both[:, :TILE] + both[:, TILE:]


def scaled_mask(down, places, exponents):
    return jnp.where(down == places, jnp.exp2(exponents.astype(f32) - BITS), 0.0)


def padded_rows(blocks, rows):
    missing = rows - sum(b.shape[0] for b in blocks)
    return jnp.concatenate(blocks + [jnp.zeros((missing, TILE), blocks[0].dtype)] * (missing > 0), axis=0)


def started(sources, targets, sems):
    copies = [
        pltpu.make_async_copy(source, target, sems.at[n])
        for n, (source, target) in enumerate(zip(sources, targets))
    ]
    for copy in copies:
        copy.start()
    return copies


def transpose_product_kernel(owned, *refs):
    (rows_hbm, cols_hbm, duals_hbm, tiles_hbm), (out_ref, slot_ref, duals, tiles), refs = refs[:4], refs[4:8], refs[8:]
    rows, cols, picked, small_sems, tile_sems = refs
    n_row = out_ref.shape[0]
    chunks, head_rows = rounds_of(n_row)
    most = SLOTS - head_rows
    k_tiles = tiles.shape[0]
    groups = [pl.ds(g * CHUNK, CHUNK) for g in range(k_tiles // CHUNK)]
    small = started([cols_hbm, rows_hbm, duals_hbm], [cols, rows, duals], small_sems)
    large = started([tiles_hbm.at[g] for g in groups], [tiles.at[g] for g in groups], tile_sems)

    for copy in small:
        copy.wait()
    for k in range(k_tiles):
        picked[pl.ds(k, 1), :] = duals[pl.ds(rows[k], 1), :]

    terms = []

    def products_of(chunk):
        large[chunk].wait()
        for first in range(chunk * CHUNK, (chunk + 1) * CHUNK, GROUP):
            group = pl.ds(first, GROUP)
            block = picked[group, :].astype(bf16).astype(f32)
            left = jnp.concatenate([one_row_of(block, m) for m in range(GROUP)], axis=1)
            terms.append(
                jnp.dot(left, tiles[group].reshape(GROUP * TILE, TILE), preferred_element_type=f32)
            )

    products_of(0)

    square = (k_tiles, k_tiles)
    col_across = cols[...]
    col_down = jnp.transpose(jnp.broadcast_to(col_across.astype(f32), square)).astype(i32)
    owner_across = sum((col_across >= o * owned).astype(i32) for o in range(1, n_row))
    owner_down = sum((col_down >= o * owned).astype(i32) for o in range(1, n_row))
    same = owner_down == owner_across
    earlier_down = iota(square, 0) < iota(square, 1)
    earlier_across = iota(square, 1) < iota(square, 0)
    rank_across = jnp.sum(where_one(same & earlier_down), axis=0, keepdims=True).astype(i32)
    rank_down = jnp.sum(where_one(same & earlier_across), axis=1, keepdims=True).astype(i32)
    slot_across = jnp.where(rank_across < most, owner_across * SLOTS + head_rows + rank_across, -1)
    slot_down = jnp.where(rank_down < most, owner_down * SLOTS + head_rows + rank_down, -1)
    slot_ref[...] = slot_down
    too_many = where_one(jnp.max(rank_across, axis=1, keepdims=True) >= most)
    to_slots = where_one(iota((n_row * SLOTS, k_tiles), 0) == slot_across)
    here = jnp.where(rank_down < most, lax.axis_index("row") * SLOTS + head_rows + rank_down, -1)
    width = chunks * TILE
    to_lanes = where_one(iota((k_tiles, width), 1) == here)
    of_owner = where_one(iota((n_row, k_tiles), 0) == owner_across)
    place = col_across - owner_across * owned + 1
    place_low = jnp.bitwise_and(place, 255)
    head_left = jnp.concatenate(
        [of_owner * (place - place_low).astype(f32), of_owner * place_low.astype(f32), of_owner], axis=0
    ).astype(bf16)

    for chunk in range(1, len(large)):
        products_of(chunk)
    whole, exponents = coded(jnp.concatenate(terms, axis=0))

    scaled = [to_lanes, to_lanes * jnp.concatenate([exponents] * chunks, axis=1)]
    heads = jnp.dot(head_left, jnp.concatenate(scaled, axis=1).astype(bf16), preferred_element_type=f32)
    places = heads[:n_row, :width] + heads[n_row : 2 * n_row, :width]
    packed = heads[2 * n_row :, width:] * place_range(owned) + places
    both = jnp.dot(to_slots.astype(bf16), two_parts(whole), preferred_element_type=f32)
    body = both[:, :TILE] + both[:, TILE:]
    top = -(-head_rows // 8) * 8
    line = iota((top, TILE), 0)
    for o in range(n_row):
        head = jnp.where(line == chunks, too_many, body[o * SLOTS : o * SLOTS + top])
        for c in range(chunks):
            head = jnp.where(line == c, packed[o : o + 1, c * TILE : (c + 1) * TILE], head)
        rows_of = body[o * SLOTS + top : (o + 1) * SLOTS]
        out_ref[o] = jnp.concatenate([head, rows_of], axis=0).astype(i32).astype(i16)


def place_range(owned):
    return 1 << owned.bit_length()


def primal_kernel(
    payloads, primal_ref, cost_ref, lower_ref, upper_ref, kind_ref, steps_ref, next_hbm, flag_ref, *refs
):
    wanted, next_ref, extrap, sem = refs
    n_row = payloads.shape[0]
    chunks, head_rows = rounds_of(n_row)
    blocks = primal_ref.shape[0]
    padded = extrap.shape[0]
    wholes = [payloads[s].astype(i32) for s in range(n_row)]
    top = -(-head_rows // 8) * 8
    head = sum(w[:top] for w in wholes)
    flag_ref[...] = jnp.broadcast_to(head[chunks:head_rows], flag_ref.shape)
    whole = padded_rows(wholes, chunks * TILE)
    down = iota((blocks, TILE), 0) + 1
    places = jnp.bitwise_and(head, place_range(blocks) - 1)
    scales = lax.shift_right_arithmetic(head, blocks.bit_length())
    masks, wholes = [], []
    for c in range(chunks):
        masks.append(scaled_mask(down, places[c : c + 1], scales[c : c + 1]))
        wholes.append(whole[c * TILE : (c + 1) * TILE])
    col_sums = picked_sums(masks, wholes)
    primal = primal_ref[...]
    kind = kind_ref[...]
    moved = primal - steps_ref[0] * (cost_ref[...] - col_sums)
    moved = jnp.where(kind % 2 == 1, jnp.maximum(moved, lower_ref[...]), moved)
    moved = jnp.where(kind >= 2, jnp.minimum(moved, upper_ref[...]), moved)
    next_ref[...] = moved
    copy = pltpu.make_async_copy(next_ref, next_hbm, sem)
    copy.start()
    aligned = blocks // 8 * 8
    if padded > aligned:
        extrap[pl.ds(aligned, padded - aligned), :] = jnp.zeros((padded - aligned, TILE), f32)
    extrap[pl.ds(0, blocks), :] = 2.0 * moved - primal
    right = extrap[...].astype(bf16)
    across = iota((TILE, padded), 1) + 1
    places = jnp.transpose(places.astype(f32)).astype(i32)
    sent = [
        jnp.dot(where_one(across == places[:, c : c + 1]).astype(bf16), right, preferred_element_type=f32)
        for c in range(chunks)
    ]
    sent = jnp.concatenate(sent, axis=0)
    for s in range(n_row):
        wanted[s] = sent[s * SLOTS : (s + 1) * SLOTS].astype(bf16)
    copy.wait()


def product_kernel(*refs):
    (rows_ref, slot_ref, tiles_ref, arrived, flag_ref), others_hbm, refs = refs[:5], refs[5:7], refs[7:]
    out_ref, others, sems = refs[0], refs[1:3], refs[3]
    later = started(others_hbm, others, sems)
    k_tiles = tiles_ref.shape[0]
    chunks, _ = rounds_of(arrived.shape[0])
    blocks = [arrived[s].astype(f32) for s in range(arrived.shape[0])]
    received = padded_rows(blocks, chunks * TILE).astype(bf16)
    across = iota((k_tiles, received.shape[0]), 1)
    slots = jnp.concatenate([slot_ref[...]] * (received.shape[0] // TILE), axis=1)
    block = jnp.dot(where_one(across == slots).astype(bf16), received, preferred_element_type=f32)
    down = jnp.transpose(block)
    lane = iota((TILE, k_tiles), 1)
    right = jnp.concatenate(
        [jnp.where(lane % 2 == 0, down, 0.0), jnp.where(lane % 2 == 1, down, 0.0)], axis=0
    ).astype(bf16)
    terms = jnp.zeros((TILE, k_tiles), f32)
    for g in range(k_tiles // 8):
        even = jnp.concatenate([tiles_ref[8 * g + m] for m in (0, 2, 4, 6)], axis=0)
        odd = jnp.concatenate([tiles_ref[8 * g + m] for m in (1, 3, 5, 7)], axis=0)
        products = jnp.dot(jnp.concatenate([even, odd], axis=1), right, preferred_element_type=f32)
        for p in range(4):
            terms = jnp.where(lane // 2 == 4 * g + p, products[p * TILE : (p + 1) * TILE], terms)
    whole, exponents = coded(jnp.transpose(terms))
    out_ref[pl.ds(0, k_tiles), :] = whole.astype(i16)
    line = iota((HEAD, TILE), 0)
    head = jnp.where(line == 0, rows_ref[...], jnp.transpose(exponents)[0:HEAD, :].astype(i32))
    head = jnp.where(line == 2, flag_ref[0:1, :], head)
    out_ref[pl.ds(k_tiles, HEAD), :] = head.astype(i16)
    for copy in later:
        copy.wait()


def row_sums_of(payloads, blocks):
    k_tiles = payloads[0].shape[0] - HEAD
    down = iota((blocks, k_tiles), 0)
    masks, wholes = [], []
    flags = jnp.zeros((1, TILE), i32)
    for payload in payloads:
        head = payload[pl.ds(k_tiles, HEAD), :].astype(i32)
        masks.append(scaled_mask(down, head[0:1], head[1:2]))
        wholes.append(payload[pl.ds(0, k_tiles), :].astype(i32))
        flags += head[2:3]
    return picked_sums(masks, wholes), flags


def own_dual_kernel(payload, duals_ref, right_ref, steps_ref, part_ref):
    row_sums, _ = row_sums_of([payload], duals_ref.shape[0])
    part_ref[...] = duals_ref[...] + steps_ref[1] * (right_ref[...] - row_sums)


def dual_kernel(*refs):
    payloads, (part_ref, kind_ref, steps_ref, next_ref, flag_ref) = refs[:-5], refs[-5:]
    row_sums, flags = row_sums_of(payloads, part_ref.shape[0])
    updated = part_ref[...] - steps_ref[1] * row_sums
    next_ref[...] = jnp.where(kind_ref[...] == 1, jnp.maximum(updated, 0.0), updated)
    flag_ref[0] = jnp.max(flags)


def partners(axis):
    size = lax.axis_size(axis)
    if size & (size - 1) == 0:
        there = [[(i, i ^ n) for i in range(size)] for n in range(1, size)]
    else:
        there = [[(i, (i + n) % size) for i in range(size)] for n in range(1, size)]
    return [(pairs, [(j, i) for i, j in pairs]) for pairs in there]


def gathered_along(array, axis):
    return [array] + [lax.ppermute(array, axis, there) for there, _ in partners(axis)]


def sums_at(places, terms, blocks):
    mask = (jnp.arange(blocks)[:, None] == jnp.concatenate(places)[None, :]).astype(f32)
    return jnp.dot(mask, jnp.concatenate(terms), precision=lax.Precision.HIGHEST).reshape(-1)


def full_step(
    tiles, rows, cols, primal, duals, cost_vec, lower_bound, upper_bound, bound_kind, right_side, row_kind, steps
):
    col_blocks = primal.shape[0] // TILE
    row_blocks = duals.shape[0] // TILE
    wide = tiles.astype(f32)
    dual_blocks = duals.astype(bf16).astype(f32).reshape(row_blocks, TILE)[rows]
    col_terms = jnp.einsum("kij,ki->kj", wide, dual_blocks)
    first = lax.axis_index("row") * col_blocks
    places = [there - first for there in gathered_along(cols, "row")]
    places = [jnp.where((p >= 0) & (p < col_blocks), p, col_blocks) for p in places]
    col_sums = sums_at(places, gathered_along(col_terms, "row"), col_blocks)
    moved = primal - steps[0] * (cost_vec - col_sums)
    moved = jnp.where(bound_kind % 2 == 1, jnp.maximum(moved, lower_bound), moved)
    moved = jnp.where(bound_kind >= 2, jnp.minimum(moved, upper_bound), moved)
    extrap = (2.0 * moved - primal).astype(bf16).reshape(col_blocks, TILE)
    wanted = [
        jnp.where((p < col_blocks)[:, None], extrap[jnp.minimum(p, col_blocks - 1)], jnp.zeros((), bf16))
        for p in places
    ]
    blocks = wanted[0].astype(f32)
    for block, (_, back) in zip(wanted[1:], partners("row")):
        blocks += lax.ppermute(block, "row", back).astype(f32)
    row_terms = jnp.einsum("kij,kj->ki", wide, blocks)
    row_sums = sums_at(gathered_along(rows, "col"), gathered_along(row_terms, "col"), row_blocks)
    updated = duals + steps[1] * (right_side - row_sums)
    return moved, jnp.where(row_kind == 1, jnp.maximum(updated, 0.0), updated)


def local(
    block_tiles,
    tile_row,
    tile_col,
    primal,
    duals,
    cost_vec,
    lower_bound,
    upper_bound,
    bound_kind,
    right_side,
    row_kind,
    step_sizes,
):
    k_tiles = block_tiles.shape[2]
    tiles = block_tiles.reshape(k_tiles, TILE, TILE)
    rows = tile_row.reshape(-1)
    cols = tile_col.reshape(-1)
    n_row = lax.axis_size("row")
    n_col = lax.axis_size("col")
    col_blocks = primal.shape[0] // TILE
    row_blocks = duals.shape[0] // TILE
    padded = -(-col_blocks // TILE) * TILE
    in_hbm = lambda array: pltpu.with_memory_space_constraint(array, pltpu.HBM)
    by_block = lambda array: in_hbm(array.reshape(-1, TILE))
    shape_of = lambda array: jax.ShapeDtypeStruct(array.shape, array.dtype)
    params = pltpu.CompilerParams(vmem_limit_bytes=32 * 1024 * 1024)
    primal_side = [a.reshape(-1, TILE) for a in (primal, cost_vec, lower_bound, upper_bound, bound_kind)]
    dual_side = [by_block(a) for a in (right_side, row_kind)]
    own = [by_block(duals), in_hbm(tiles)]

    col_terms, slots, duals_kept, tiles_kept = pl.pallas_call(
        functools.partial(transpose_product_kernel, col_blocks),
        out_shape=(
            jax.ShapeDtypeStruct((n_row, SLOTS, TILE), i16),
            jax.ShapeDtypeStruct((k_tiles, TILE), i32),
            *[shape_of(a) for a in own],
        ),
        in_specs=[HBM] * 4,
        out_specs=(VMEM,) * 4,
        scratch_shapes=[
            pltpu.SMEM((k_tiles,), i32),
            pltpu.VMEM((1, k_tiles), i32),
            pltpu.VMEM((k_tiles, TILE), f32),
            pltpu.SemaphoreType.DMA((3,)),
            pltpu.SemaphoreType.DMA((k_tiles // CHUNK,)),
        ],
        compiler_params=params,
        name="transpose_product",
    )(in_hbm(rows), in_hbm(cols.reshape(1, k_tiles)), *own)
    primal_next, flag, wanted = pl.pallas_call(
        primal_kernel,
        out_shape=(
            jax.ShapeDtypeStruct((col_blocks, TILE), f32),
            jax.ShapeDtypeStruct((8, TILE), i32),
            jax.ShapeDtypeStruct((n_row, SLOTS, TILE), bf16),
        ),
        in_specs=[VMEM] * 6 + [SMEM],
        out_specs=(HBM, VMEM, VMEM),
        scratch_shapes=[
            pltpu.VMEM((col_blocks, TILE), f32),
            pltpu.VMEM((padded, TILE), f32),
            pltpu.SemaphoreType.DMA,
        ],
        compiler_params=params,
        name="primal_step",
    )(lax.all_to_all(col_terms, "row", 0, 0), *primal_side, step_sizes)
    row_terms, *dual_kept = pl.pallas_call(
        product_kernel,
        out_shape=(
            jax.ShapeDtypeStruct((k_tiles + HEAD, TILE), i16),
            *[shape_of(a) for a in dual_side],
        ),
        in_specs=[VMEM] * 5 + [HBM] * 2,
        out_specs=(VMEM,) * 3,
        scratch_shapes=[pltpu.SemaphoreType.DMA((2,))],
        compiler_params=params,
        name="product",
    )(rows.reshape(1, k_tiles), slots, tiles_kept, lax.all_to_all(wanted, "row", 0, 0), flag, *dual_side)
    _, *others = gathered_along(row_terms, "col")
    part = pl.pallas_call(
        own_dual_kernel,
        out_shape=jax.ShapeDtypeStruct((row_blocks, TILE), f32),
        in_specs=[VMEM] * 3 + [SMEM],
        out_specs=VMEM,
        compiler_params=params,
        cost_estimate=pl.CostEstimate(flops=4 * row_blocks * k_tiles * TILE, bytes_accessed=2**20, transcendentals=0),
        name="own_dual_step",
    )(row_terms, duals_kept, dual_kept[0], step_sizes)
    dual_next, too_many = pl.pallas_call(
        dual_kernel,
        out_shape=(jax.ShapeDtypeStruct((row_blocks, TILE), f32), jax.ShapeDtypeStruct((1,), i32)),
        in_specs=[VMEM] * (n_col + 1) + [SMEM],
        out_specs=(VMEM, SMEM),
        compiler_params=params,
        name="dual_step",
    )(*others, part, dual_kept[1], step_sizes)
    vectors = (primal, duals, cost_vec, lower_bound, upper_bound, bound_kind, right_side, row_kind, step_sizes)
    return lax.cond(
        too_many[0] > 0,
        lambda done: full_step(tiles, rows, cols, *vectors),
        lambda done: done,
        (primal_next.reshape(-1), dual_next.reshape(-1)),
    )


def solution(mesh):
    return jax.shard_map(
        local,
        mesh=mesh,
        in_specs=(
            P("row", "col", None, None, None),
            P("row", "col", None),
            P("row", "col", None),
            P(("col", "row")),
            P("row"),
            P(("col", "row")),
            P(("col", "row")),
            P(("col", "row")),
            P(("col", "row")),
            P("row"),
            P("row"),
            P(),
        ),
        out_specs=(P(("col", "row")), P("row")),
        check_vma=False,
    )
```

```python
import functools
import jax
import jax.numpy as jnp
from jax import lax
from jax.experimental import pallas as pl
from jax.experimental.pallas import tpu as pltpu
from jax.sharding import PartitionSpec as P

TILE = 128
GROUP = 16
CHUNK = 64
SLOTS = 40
HEAD = 16
BITS = 14
LEAST = -60

f32 = jnp.float32
bf16 = jnp.bfloat16
i32 = jnp.int32
i16 = jnp.int16
VMEM = pl.BlockSpec(memory_space=pltpu.VMEM)
SMEM = pl.BlockSpec(memory_space=pltpu.SMEM)
HBM = pl.BlockSpec(memory_space=pltpu.HBM)


def iota(shape, axis):
    return lax.broadcasted_iota(i32, shape, axis)


def where_one(condition):
    return jnp.where(condition, 1.0, 0.0)


def one_row_of(block, position):
    return jnp.where(iota(block.shape, 0) == position, block, 0.0).astype(bf16)


def rounds_of(n_row):
    chunks = -(-n_row * SLOTS // TILE)
    return chunks, chunks + 1


def coded(values):
    largest = jnp.maximum(jnp.max(jnp.abs(values), axis=1, keepdims=True), 1e-30)
    exponent = jnp.maximum(jnp.ceil(jnp.log2(largest)), LEAST)
    whole = jnp.floor(values * jnp.exp2(BITS - exponent) + 0.5).astype(i32)
    return whole, jnp.broadcast_to(exponent, values.shape)


def two_parts(whole):
    low = jnp.bitwise_and(whole, 255)
    parts = [(whole - low).astype(f32), low.astype(f32)]
    return jnp.concatenate(parts, axis=1).astype(bf16)


def picked_sums(masks, wholes):
    left = masks[0] if len(masks) == 1 else jnp.concatenate(masks, axis=1)
    both = jnp.dot(
        left.astype(bf16),
        jnp.concatenate([two_parts(w) for w in wholes], axis=0),
        preferred_element_type=f32,
    )
    return both[:, :TILE] + both[:, TILE:]


def scaled_mask(down, places, exponents):
    return jnp.where(down == places, jnp.exp2(exponents.astype(f32) - BITS), 0.0)


def padded_rows(blocks, rows):
    missing = rows - sum(b.shape[0] for b in blocks)
    return jnp.concatenate(blocks + [jnp.zeros((missing, TILE), blocks[0].dtype)] * (missing > 0), axis=0)


def started(sources, targets, sems):
    copies = [
        pltpu.make_async_copy(source, target, sems.at[n])
        for n, (source, target) in enumerate(zip(sources, targets))
    ]
    for copy in copies:
        copy.start()
    return copies


def transpose_product_kernel(owned, *refs):
    (rows_hbm, cols_hbm, duals_hbm, tiles_hbm), (out_ref, slot_ref, duals, tiles), refs = refs[:4], refs[4:8], refs[8:]
    rows, cols, picked, small_sems, tile_sems = refs
    n_row = out_ref.shape[0]
    chunks, head_rows = rounds_of(n_row)
    most = SLOTS - head_rows
    k_tiles = tiles.shape[0]
    groups = [pl.ds(g * CHUNK, CHUNK) for g in range(k_tiles // CHUNK)]
    small = started([cols_hbm, rows_hbm, duals_hbm], [cols, rows, duals], small_sems)
    large = started([tiles_hbm.at[g] for g in groups], [tiles.at[g] for g in groups], tile_sems)

    for copy in small:
        copy.wait()
    for k in range(k_tiles):
        picked[pl.ds(k, 1), :] = duals[pl.ds(rows[k], 1), :]

    terms = []

    def products_of(chunk):
        large[chunk].wait()
        for first in range(chunk * CHUNK, (chunk + 1) * CHUNK, GROUP):
            group = pl.ds(first, GROUP)
            block = picked[group, :].astype(bf16).astype(f32)
            left = jnp.concatenate([one_row_of(block, m) for m in range(GROUP)], axis=1)
            terms.append(
                jnp.dot(left, tiles[group].reshape(GROUP * TILE, TILE), preferred_element_type=f32)
            )

    products_of(0)

    square = (k_tiles, k_tiles)
    col_across = cols[...]
    col_down = jnp.transpose(jnp.broadcast_to(col_across.astype(f32), square)).astype(i32)
    owner_across = sum((col_across >= o * owned).astype(i32) for o in range(1, n_row))
    owner_down = sum((col_down >= o * owned).astype(i32) for o in range(1, n_row))
    same = owner_down == owner_across
    earlier_down = iota(square, 0) < iota(square, 1)
    earlier_across = iota(square, 1) < iota(square, 0)
    rank_across = jnp.sum(where_one(same & earlier_down), axis=0, keepdims=True).astype(i32)
    rank_down = jnp.sum(where_one(same & earlier_across), axis=1, keepdims=True).astype(i32)
    slot_across = jnp.where(rank_across < most, owner_across * SLOTS + head_rows + rank_across, -1)
    slot_down = jnp.where(rank_down < most, owner_down * SLOTS + head_rows + rank_down, -1)
    slot_ref[...] = slot_down
    too_many = where_one(jnp.max(rank_across, axis=1, keepdims=True) >= most)
    to_slots = where_one(iota((n_row * SLOTS, k_tiles), 0) == slot_across)
    here = jnp.where(rank_down < most, lax.axis_index("row") * SLOTS + head_rows + rank_down, -1)
    width = chunks * TILE
    to_lanes = where_one(iota((k_tiles, width), 1) == here)
    of_owner = where_one(iota((n_row, k_tiles), 0) == owner_across)
    place = col_across - owner_across * owned + 1
    place_low = jnp.bitwise_and(place, 255)
    head_left = jnp.concatenate(
        [of_owner * (place - place_low).astype(f32), of_owner * place_low.astype(f32), of_owner], axis=0
    ).astype(bf16)

    for chunk in range(1, len(large)):
        products_of(chunk)
    whole, exponents = coded(jnp.concatenate(terms, axis=0))

    scaled = [to_lanes, to_lanes * jnp.concatenate([exponents] * chunks, axis=1)]
    heads = jnp.dot(head_left, jnp.concatenate(scaled, axis=1).astype(bf16), preferred_element_type=f32)
    places = heads[:n_row, :width] + heads[n_row : 2 * n_row, :width]
    packed = heads[2 * n_row :, width:] * place_range(owned) + places
    both = jnp.dot(to_slots.astype(bf16), two_parts(whole), preferred_element_type=f32)
    body = both[:, :TILE] + both[:, TILE:]
    top = -(-head_rows // 8) * 8
    line = iota((top, TILE), 0)
    for o in range(n_row):
        head = jnp.where(line == chunks, too_many, body[o * SLOTS : o * SLOTS + top])
        for c in range(chunks):
            head = jnp.where(line == c, packed[o : o + 1, c * TILE : (c + 1) * TILE], head)
        rows_of = body[o * SLOTS + top : (o + 1) * SLOTS]
        out_ref[o] = jnp.concatenate([head, rows_of], axis=0).astype(i32).astype(i16)


def place_range(owned):
    return 1 << owned.bit_length()


def primal_kernel(
    payloads, primal_ref, cost_ref, lower_ref, upper_ref, kind_ref, steps_ref, next_hbm, flag_ref, *refs
):
    wanted, next_ref, extrap, sem = refs
    n_row = payloads.shape[0]
    chunks, head_rows = rounds_of(n_row)
    blocks = primal_ref.shape[0]
    padded = extrap.shape[0]
    wholes = [payloads[s].astype(i32) for s in range(n_row)]
    top = -(-head_rows // 8) * 8
    head = sum(w[:top] for w in wholes)
    flag_ref[...] = jnp.broadcast_to(head[chunks:head_rows], flag_ref.shape)
    whole = padded_rows(wholes, chunks * TILE)
    down = iota((blocks, TILE), 0) + 1
    places = jnp.bitwise_and(head, place_range(blocks) - 1)
    scales = lax.shift_right_arithmetic(head, blocks.bit_length())
    masks, wholes = [], []
    for c in range(chunks):
        masks.append(scaled_mask(down, places[c : c + 1], scales[c : c + 1]))
        wholes.append(whole[c * TILE : (c + 1) * TILE])
    col_sums = picked_sums(masks, wholes)
    primal = primal_ref[...]
    kind = kind_ref[...]
    moved = primal - steps_ref[0] * (cost_ref[...] - col_sums)
    moved = jnp.where(kind % 2 == 1, jnp.maximum(moved, lower_ref[...]), moved)
    moved = jnp.where(kind >= 2, jnp.minimum(moved, upper_ref[...]), moved)
    next_ref[...] = moved
    copy = pltpu.make_async_copy(next_ref, next_hbm, sem)
    copy.start()
    aligned = blocks // 8 * 8
    if padded > aligned:
        extrap[pl.ds(aligned, padded - aligned), :] = jnp.zeros((padded - aligned, TILE), f32)
    extrap[pl.ds(0, blocks), :] = 2.0 * moved - primal
    right = extrap[...].astype(bf16)
    across = iota((TILE, padded), 1) + 1
    places = jnp.transpose(places.astype(f32)).astype(i32)
    sent = [
        jnp.dot(where_one(across == places[:, c : c + 1]).astype(bf16), right, preferred_element_type=f32)
        for c in range(chunks)
    ]
    sent = jnp.concatenate(sent, axis=0)
    for s in range(n_row):
        wanted[s] = sent[s * SLOTS : (s + 1) * SLOTS].astype(bf16)
    copy.wait()


def product_kernel(*refs):
    (rows_ref, slot_ref, tiles_ref, arrived, flag_ref), others_hbm, refs = refs[:5], refs[5:7], refs[7:]
    out_ref, others, sems = refs[0], refs[1:3], refs[3]
    later = started(others_hbm, others, sems)
    k_tiles = tiles_ref.shape[0]
    chunks, _ = rounds_of(arrived.shape[0])
    blocks = [arrived[s].astype(f32) for s in range(arrived.shape[0])]
    received = padded_rows(blocks, chunks * TILE).astype(bf16)
    across = iota((k_tiles, received.shape[0]), 1)
    slots = jnp.concatenate([slot_ref[...]] * (received.shape[0] // TILE), axis=1)
    block = jnp.dot(where_one(across == slots).astype(bf16), received, preferred_element_type=f32)
    down = jnp.transpose(block)
    lane = iota((TILE, k_tiles), 1)
    right = jnp.concatenate(
        [jnp.where(lane % 2 == 0, down, 0.0), jnp.where(lane % 2 == 1, down, 0.0)], axis=0
    ).astype(bf16)
    terms = jnp.zeros((TILE, k_tiles), f32)
    for g in range(k_tiles // 8):
        even = jnp.concatenate([tiles_ref[8 * g + m] for m in (0, 2, 4, 6)], axis=0)
        odd = jnp.concatenate([tiles_ref[8 * g + m] for m in (1, 3, 5, 7)], axis=0)
        products = jnp.dot(jnp.concatenate([even, odd], axis=1), right, preferred_element_type=f32)
        for p in range(4):
            terms = jnp.where(lane // 2 == 4 * g + p, products[p * TILE : (p + 1) * TILE], terms)
    whole, exponents = coded(jnp.transpose(terms))
    out_ref[pl.ds(0, k_tiles), :] = whole.astype(i16)
    line = iota((HEAD, TILE), 0)
    head = jnp.where(line == 0, rows_ref[...], jnp.transpose(exponents)[0:HEAD, :].astype(i32))
    head = jnp.where(line == 2, flag_ref[0:1, :], head)
    out_ref[pl.ds(k_tiles, HEAD), :] = head.astype(i16)
    for copy in later:
        copy.wait()


def row_sums_of(payloads, blocks):
    k_tiles = payloads[0].shape[0] - HEAD
    down = iota((blocks, k_tiles), 0)
    masks, wholes = [], []
    flags = jnp.zeros((1, TILE), i32)
    for payload in payloads:
        head = payload[pl.ds(k_tiles, HEAD), :].astype(i32)
        masks.append(scaled_mask(down, head[0:1], head[1:2]))
        wholes.append(payload[pl.ds(0, k_tiles), :].astype(i32))
        flags += head[2:3]
    return picked_sums(masks, wholes), flags


def own_dual_kernel(payload, duals_ref, right_ref, steps_ref, part_ref):
    row_sums, _ = row_sums_of([payload], duals_ref.shape[0])
    part_ref[...] = duals_ref[...] + steps_ref[1] * (right_ref[...] - row_sums)


def dual_kernel(*refs):
    payloads, (part_ref, kind_ref, own_flag_ref, steps_ref, next_ref, flag_ref) = refs[:-6], refs[-6:]
    row_sums, flags = row_sums_of(payloads, part_ref.shape[0])
    updated = part_ref[...] - steps_ref[1] * row_sums
    next_ref[...] = jnp.where(kind_ref[...] == 1, jnp.maximum(updated, 0.0), updated)
    flag_ref[0] = jnp.max(flags + own_flag_ref[0:1, :])


def partners(axis):
    size = lax.axis_size(axis)
    if size & (size - 1) == 0:
        there = [[(i, i ^ n) for i in range(size)] for n in range(1, size)]
    else:
        there = [[(i, (i + n) % size) for i in range(size)] for n in range(1, size)]
    return [(pairs, [(j, i) for i, j in pairs]) for pairs in there]


def gathered_along(array, axis):
    return [array] + [lax.ppermute(array, axis, there) for there, _ in partners(axis)]


def sums_at(places, terms, blocks):
    mask = (jnp.arange(blocks)[:, None] == jnp.concatenate(places)[None, :]).astype(f32)
    return jnp.dot(mask, jnp.concatenate(terms), precision=lax.Precision.HIGHEST).reshape(-1)


def full_step(
    tiles, rows, cols, primal, duals, cost_vec, lower_bound, upper_bound, bound_kind, right_side, row_kind, steps
):
    col_blocks = primal.shape[0] // TILE
    row_blocks = duals.shape[0] // TILE
    wide = tiles.astype(f32)
    dual_blocks = duals.astype(bf16).astype(f32).reshape(row_blocks, TILE)[rows]
    col_terms = jnp.einsum("kij,ki->kj", wide, dual_blocks)
    first = lax.axis_index("row") * col_blocks
    places = [there - first for there in gathered_along(cols, "row")]
    places = [jnp.where((p >= 0) & (p < col_blocks), p, col_blocks) for p in places]
    col_sums = sums_at(places, gathered_along(col_terms, "row"), col_blocks)
    moved = primal - steps[0] * (cost_vec - col_sums)
    moved = jnp.where(bound_kind % 2 == 1, jnp.maximum(moved, lower_bound), moved)
    moved = jnp.where(bound_kind >= 2, jnp.minimum(moved, upper_bound), moved)
    extrap = (2.0 * moved - primal).astype(bf16).reshape(col_blocks, TILE)
    wanted = [
        jnp.where((p < col_blocks)[:, None], extrap[jnp.minimum(p, col_blocks - 1)], jnp.zeros((), bf16))
        for p in places
    ]
    blocks = wanted[0].astype(f32)
    for block, (_, back) in zip(wanted[1:], partners("row")):
        blocks += lax.ppermute(block, "row", back).astype(f32)
    row_terms = jnp.einsum("kij,kj->ki", wide, blocks)
    row_sums = sums_at(gathered_along(rows, "col"), gathered_along(row_terms, "col"), row_blocks)
    updated = duals + steps[1] * (right_side - row_sums)
    return moved, jnp.where(row_kind == 1, jnp.maximum(updated, 0.0), updated)


def local(
    block_tiles,
    tile_row,
    tile_col,
    primal,
    duals,
    cost_vec,
    lower_bound,
    upper_bound,
    bound_kind,
    right_side,
    row_kind,
    step_sizes,
):
    k_tiles = block_tiles.shape[2]
    tiles = block_tiles.reshape(k_tiles, TILE, TILE)
    rows = tile_row.reshape(-1)
    cols = tile_col.reshape(-1)
    n_row = lax.axis_size("row")
    n_col = lax.axis_size("col")
    col_blocks = primal.shape[0] // TILE
    row_blocks = duals.shape[0] // TILE
    padded = -(-col_blocks // TILE) * TILE
    in_hbm = lambda array: pltpu.with_memory_space_constraint(array, pltpu.HBM)
    by_block = lambda array: in_hbm(array.reshape(-1, TILE))
    shape_of = lambda array: jax.ShapeDtypeStruct(array.shape, array.dtype)
    params = pltpu.CompilerParams(vmem_limit_bytes=32 * 1024 * 1024)
    primal_side = [a.reshape(-1, TILE) for a in (primal, cost_vec, lower_bound, upper_bound, bound_kind)]
    dual_side = [by_block(a) for a in (right_side, row_kind)]
    own = [by_block(duals), in_hbm(tiles)]

    col_terms, slots, duals_kept, tiles_kept = pl.pallas_call(
        functools.partial(transpose_product_kernel, col_blocks),
        out_shape=(
            jax.ShapeDtypeStruct((n_row, SLOTS, TILE), i16),
            jax.ShapeDtypeStruct((k_tiles, TILE), i32),
            *[shape_of(a) for a in own],
        ),
        in_specs=[HBM] * 4,
        out_specs=(VMEM,) * 4,
        scratch_shapes=[
            pltpu.SMEM((k_tiles,), i32),
            pltpu.VMEM((1, k_tiles), i32),
            pltpu.VMEM((k_tiles, TILE), f32),
            pltpu.SemaphoreType.DMA((3,)),
            pltpu.SemaphoreType.DMA((k_tiles // CHUNK,)),
        ],
        compiler_params=params,
        name="transpose_product",
    )(in_hbm(rows), in_hbm(cols.reshape(1, k_tiles)), *own)
    primal_next, flag, wanted = pl.pallas_call(
        primal_kernel,
        out_shape=(
            jax.ShapeDtypeStruct((col_blocks, TILE), f32),
            jax.ShapeDtypeStruct((8, TILE), i32),
            jax.ShapeDtypeStruct((n_row, SLOTS, TILE), bf16),
        ),
        in_specs=[VMEM] * 6 + [SMEM],
        out_specs=(HBM, VMEM, VMEM),
        scratch_shapes=[
            pltpu.VMEM((col_blocks, TILE), f32),
            pltpu.VMEM((padded, TILE), f32),
            pltpu.SemaphoreType.DMA,
        ],
        compiler_params=params,
        name="primal_step",
    )(lax.all_to_all(col_terms, "row", 0, 0), *primal_side, step_sizes)
    row_terms, *dual_kept = pl.pallas_call(
        product_kernel,
        out_shape=(
            jax.ShapeDtypeStruct((k_tiles + HEAD, TILE), i16),
            *[shape_of(a) for a in dual_side],
        ),
        in_specs=[VMEM] * 5 + [HBM] * 2,
        out_specs=(VMEM,) * 3,
        scratch_shapes=[pltpu.SemaphoreType.DMA((2,))],
        compiler_params=params,
        name="product",
    )(rows.reshape(1, k_tiles), slots, tiles_kept, lax.all_to_all(wanted, "row", 0, 0), flag, *dual_side)
    _, *others = gathered_along(row_terms, "col")
    part = pl.pallas_call(
        own_dual_kernel,
        out_shape=jax.ShapeDtypeStruct((row_blocks, TILE), f32),
        in_specs=[VMEM] * 3 + [SMEM],
        out_specs=VMEM,
        compiler_params=params,
        cost_estimate=pl.CostEstimate(flops=4 * row_blocks * k_tiles * TILE, bytes_accessed=2**20, transcendentals=0),
        name="own_dual_step",
    )(row_terms, duals_kept, dual_kept[0], step_sizes)
    dual_next, too_many = pl.pallas_call(
        dual_kernel,
        out_shape=(jax.ShapeDtypeStruct((row_blocks, TILE), f32), jax.ShapeDtypeStruct((1,), i32)),
        in_specs=[VMEM] * (n_col + 2) + [SMEM],
        out_specs=(VMEM, SMEM),
        compiler_params=params,
        name="dual_step",
    )(*others, part, dual_kept[1], flag, step_sizes)
    vectors = (primal, duals, cost_vec, lower_bound, upper_bound, bound_kind, right_side, row_kind, step_sizes)
    return lax.cond(
        too_many[0] > 0,
        lambda done: full_step(tiles, rows, cols, *vectors),
        lambda done: done,
        (primal_next.reshape(-1), dual_next.reshape(-1)),
    )


def solution(mesh):
    return jax.shard_map(
        local,
        mesh=mesh,
        in_specs=(
            P("row", "col", None, None, None),
            P("row", "col", None),
            P("row", "col", None),
            P(("col", "row")),
            P("row"),
            P(("col", "row")),
            P(("col", "row")),
            P(("col", "row")),
            P(("col", "row")),
            P("row"),
            P("row"),
            P(),
        ),
        out_specs=(P(("col", "row")), P("row")),
        check_vma=False,
    )
```
